32 devices in a mesh: fsdp: 16 (over z, y, core), tp: 2 (over x).
Axes of the slice: x: 2, y: 2, z: 4, core: 2. Of those that a mesh axis runs over, the one named last changes fastest.
Arguments:
- hidden: bfloat16 [16384, 2048], P(('fsdp', 'tp')), may hold values from -6 to 6
- cotangent: bfloat16 [16384, 2048], P(('fsdp', 'tp')), may hold values from -6 to 6
- prefix: int32 [16], P('fsdp'), may hold values from 102 to 512, as said below
- input_norm_gain: bfloat16 [2048], P('fsdp'), may hold values from 0.5 to 1.5
- z_weight: bfloat16 [2048, 4096], P('fsdp', 'tp'), may hold values from -0.125 to 0.125
- x_weight: bfloat16 [2048, 4096], P('fsdp', 'tp'), may hold values from -0.125 to 0.125
- bc_weight: bfloat16 [2048, 256], P('fsdp'), may hold values from -0.125 to 0.125
- dt_weight: bfloat16 [2048, 64], P('fsdp', 'tp'), may hold values from -0.125 to 0.125
- x_conv: bfloat16 [64, 4, 64], P('tp', None, 'fsdp'), may hold values from -3 to 3
- bc_conv: bfloat16 [4, 256], P(None, 'fsdp'), may hold values from -3 to 3
- log_decay: float32 [64], P('tp'), may hold values from 0 to 2.77
- dt_bias: float32 [64], P('tp'), may hold values from -4 to -1
- skip_gain: float32 [64], P('tp'), may hold values from 0.5 to 1.5
- gate_gain: bfloat16 [64, 64], P('tp', 'fsdp'), may hold values from 0.5 to 1.5
- out_weight: bfloat16 [4096, 2048], P('tp', 'fsdp'), may hold values from -0.09375 to 0.09375
Outputs:
- mixed: float32 [16384, 2048], P(('fsdp', 'tp'))
- grad_hidden: float32 [16384, 2048], P(('fsdp', 'tp'))
- grad_input_norm_gain: float32 [2048], P('fsdp')
- grad_z_weight: float32 [2048, 4096], P('fsdp', 'tp')
- grad_x_weight: float32 [2048, 4096], P('fsdp', 'tp')
- grad_bc_weight: float32 [2048, 256], P('fsdp')
- grad_dt_weight: float32 [2048, 64], P('fsdp', 'tp')
- grad_x_conv: float32 [64, 4, 64], P('tp', None, 'fsdp')
- grad_bc_conv: float32 [4, 256], P(None, 'fsdp')
- grad_log_decay: float32 [64], P('tp')
- grad_dt_bias: float32 [64], P('tp')
- grad_skip_gain: float32 [64], P('tp')
- grad_gate_gain: float32 [64, 64], P('tp', 'fsdp')
- grad_out_weight: float32 [4096, 2048], P('tp', 'fsdp')
The draws below stay inside these ranges and needn't reach their ends.
Inputs may be any that keep to these rules, and one draw needn't show every extreme that they name: `prefix`: prefix length of each sequence; some sequence has the least and some the most.
All inputs are finite; a program needn't handle non-finite values.
Results may differ from the reference program's by a relative error of at most 0.0082.
Values may be sent and summed in bfloat16 or wider, within the bound.
No kernel may reach another device: no remote copies, remote signals or barrier semaphores. Data moves between devices by JAX's collectives and lax.ppermute only.
A program may use at most 384 MiB of HBM per device.

```python
import jax
import jax.numpy as jnp
from jax import lax

D = 2048
H = 64
P_SIZE = 64
N = 128
K = 4
Q = 256
LEN = 1024
SEQS = 16
TOKENS = 16384


def draw_prefix(key, part):
    key_values = jax.random.fold_in(key, 101)
    key_top = jax.random.fold_in(key, 202)
    key_low = jax.random.fold_in(key, 303)
    values = jax.random.randint(key_values, (SEQS,), LEN // 10, LEN // 2 + 1)
    top_slot = jax.random.randint(key_top, (), 0, SEQS)
    low_slot = (top_slot + 1 + jax.random.randint(key_low, (), 0, SEQS - 1)) % SEQS
    values = values.at[top_slot].set(LEN // 2).at[low_slot].set(LEN // 10)
    return values.astype(jnp.int32)


def levels(rng, extent, cuts, smallest, top_value):
    level = 1.0
    for position, parts in cuts:
        draws = jax.random.uniform(jax.random.fold_in(jax.random.fold_in(rng, 6), position), (parts,), jnp.float32, smallest / len(cuts), top_value / len(cuts))
        level = level * jnp.repeat(jnp.exp(draws), extent[position] // parts).reshape((-1,) + (1,) * (len(extent) - 1 - position))
    return level


def centred(rng, extent, width, most, cuts=(), held_as=jnp.bfloat16):
    level = levels(rng, extent, cuts, -0.22, 0.18) if cuts else 1.0
    values = jax.random.normal(rng, extent, jnp.float32) * width * level
    return jnp.minimum(jnp.maximum(values, -most), most).astype(held_as)


def setup_inputs(seed: int = 0) -> dict:
    arg_keys = jax.random.split(jax.random.key(seed), 16)
    hidden = centred(arg_keys[0], (TOKENS, D), 1.0, 6.0, ((0, 32),))
    cotangent = centred(arg_keys[1], (TOKENS, D), 1.0, 6.0, ((0, 32),))
    prefix = draw_prefix(jax.random.fold_in(arg_keys[15], 71), 0)
    input_norm_gain = jnp.clip(1.0 + 0.1 * jax.random.normal(arg_keys[3], (D,), jnp.float32), 0.5, 1.5).astype(jnp.bfloat16)
    z_weight = centred(arg_keys[4], (D, H * P_SIZE), D ** -0.5, 0.125, ((0, 16), (1, 2)))
    x_weight = centred(arg_keys[5], (D, H * P_SIZE), D ** -0.5, 0.125, ((0, 16), (1, 2)))
    bc_weight = centred(arg_keys[6], (D, 2 * N), D ** -0.5, 0.125, ((0, 16),))
    dt_weight = centred(arg_keys[7], (D, H), D ** -0.5, 0.125, ((0, 16), (1, 2)))
    x_conv = centred(arg_keys[8], (H, K, P_SIZE), K ** -0.5, 3.0, ((0, 2), (2, 16)))
    bc_conv = centred(arg_keys[9], (K, 2 * N), K ** -0.5, 3.0, ((1, 16),))
    log_decay = jnp.clip(2.77 * jax.random.uniform(arg_keys[10], (H,), jnp.float32) ** levels(arg_keys[10], (H,), ((0, 2),), -0.2, 0.2), 0.0, 2.77)
    dt_bias = jnp.clip(-4.0 + 3.0 * jax.random.uniform(arg_keys[11], (H,), jnp.float32) ** levels(arg_keys[11], (H,), ((0, 2),), -0.2, 0.2), -4.0, -1.0)
    skip_gain = jnp.clip(0.5 + 1.0 * jax.random.uniform(arg_keys[12], (H,), jnp.float32) ** levels(arg_keys[12], (H,), ((0, 2),), -0.2, 0.2), 0.5, 1.5)
    gate_gain = jnp.clip(1.0 + 0.1 * jax.random.normal(arg_keys[13], (H, P_SIZE), jnp.float32), 0.5, 1.5).astype(jnp.bfloat16)
    out_weight = centred(arg_keys[14], (H * P_SIZE, D), (H * P_SIZE) ** -0.5, 0.09375, ((0, 2), (1, 16)))
    return {"hidden": hidden, "cotangent": cotangent, "prefix": prefix, "input_norm_gain": input_norm_gain, "z_weight": z_weight, "x_weight": x_weight, "bc_weight": bc_weight, "dt_weight": dt_weight, "x_conv": x_conv, "bc_conv": bc_conv, "log_decay": log_decay, "dt_bias": dt_bias, "skip_gain": skip_gain, "gate_gain": gate_gain, "out_weight": out_weight}


EPSILON = 1e-05
HIGHEST = lax.Precision.HIGHEST

@jax.custom_vjp
def low(v):
    return lax.optimization_barrier(v.astype(jnp.bfloat16)).astype(jnp.float32)

@jax.custom_vjp
def low_back(v):
    return v

def low_keep(v):
    return (low(v), None)

def low_pass(kept, grad):
    return (grad,)

def back_keep(v):
    return (v, None)

def back_low(kept, grad):
    return (low(grad),)
low.defvjp(low_keep, low_pass)
low_back.defvjp(back_keep, back_low)

def causal_conv(values, kernel):
    kernel_len = kernel.shape[0]
    length = values.shape[1]
    padded = jnp.pad(values, ((0, 0), (kernel_len - 1, 0), (0, 0)))
    running = kernel[0] * padded[:, 0:length]
    for offset in range(1, kernel_len):
        running = running + kernel[offset] * padded[:, offset:offset + length]
    return running

def block_scan(inputs, steps_dt, rates, b_mat, c_mat, block_len):
    seq_count, length, head_count, head_width = inputs.shape
    block_count = length // block_len
    inputs = inputs.reshape(seq_count, block_count, block_len, head_count, head_width)
    steps_dt = steps_dt.reshape(seq_count, block_count, block_len, head_count)
    rates = rates.reshape(seq_count, block_count, block_len, head_count)
    b_mat = b_mat.reshape(seq_count, block_count, block_len, -1)
    c_mat = c_mat.reshape(seq_count, block_count, block_len, -1)
    cumulative = jnp.cumsum(rates, axis=2)
    products = jnp.einsum('scqn,sckn->scqk', c_mat, b_mat, precision=HIGHEST)
    exponent = cumulative[:, :, :, None, :] - cumulative[:, :, None, :, :]
    causal_mask = (jnp.arange(block_len)[:, None] >= jnp.arange(block_len)[None, :])[None, None, :, :, None]
    decays = jnp.where(causal_mask, jnp.exp(jnp.where(causal_mask, exponent, 0.0)), 0.0)
    mixing = products[..., None] * decays * steps_dt[:, :, None, :, :]
    local_out = jnp.einsum('sctkh,sckhp->scthp', mixing, inputs, precision=HIGHEST)
    last_cum = cumulative[:, :, -1:, :]
    to_last = jnp.exp(last_cum - cumulative) * steps_dt
    states = jnp.einsum('sckh,sckhp,sckn->schpn', to_last, inputs, b_mat, precision=HIGHEST)
    growth = jnp.exp(last_cum[:, :, 0, :])

    def advance(current, element):
        block_state, factor = element
        return (current * factor[:, :, None, None] + block_state, current)
    initial = jnp.zeros(states.shape[:1] + states.shape[2:], inputs.dtype)
    _, entering = lax.scan(advance, initial, (jnp.moveaxis(states, 1, 0), jnp.moveaxis(growth, 1, 0)))
    entering = jnp.moveaxis(entering, 0, 1)
    carried = jnp.einsum('sctn,schpn->scthp', c_mat, entering, precision=HIGHEST) * jnp.exp(cumulative)[..., None]
    return (local_out + carried).reshape(seq_count, length, head_count, head_width)

def mixer(x_pre, bc_pre, dt_pre, x_conv, bc_conv, log_decay, dt_bias, skip_gain, prefix, block_len):
    head_count, kernel_len, head_width = x_conv.shape
    seq_count, length = (x_pre.shape[0], x_pre.shape[1])
    x_kernel = jnp.transpose(x_conv, (1, 0, 2)).reshape(kernel_len, head_count * head_width)
    inputs = jax.nn.silu(causal_conv(x_pre, x_kernel)).reshape(seq_count, length, head_count, head_width)
    bc_act = jax.nn.silu(causal_conv(bc_pre, bc_conv))
    state_len = bc_pre.shape[-1] // 2
    b_mat = bc_act[..., :state_len]
    c_mat = bc_act[..., state_len:]
    steps_dt = jax.nn.softplus(dt_pre + dt_bias)
    rates = -jnp.exp(log_decay) * steps_dt
    prefix_mask = (jnp.arange(length)[None, :] < prefix[:, None]).astype(inputs.dtype)
    masked = inputs * prefix_mask[:, :, None, None]
    forward_out = block_scan(inputs, steps_dt, rates, b_mat, c_mat, block_len)
    flipped = block_scan(jnp.flip(masked, 1), jnp.flip(steps_dt, 1), jnp.flip(rates, 1), jnp.flip(b_mat, 1), jnp.flip(c_mat, 1), block_len)
    diagonal = lax.optimization_barrier(jnp.sum(b_mat * c_mat, axis=-1))[:, :, None, None] * steps_dt[..., None] * masked
    result = forward_out + jnp.flip(flipped, 1) - diagonal + skip_gain[:, None] * inputs
    return result.reshape(seq_count, length, head_count * head_width)

def forward(hidden, norm_gain, z_weight, x_weight, bc_weight, dt_weight, x_conv, bc_conv, log_decay, dt_bias, skip_gain, gate_gain, out_weight, prefix):
    inv_rms = lax.rsqrt(lax.optimization_barrier(jnp.mean(hidden * hidden, axis=-1, keepdims=True)) + EPSILON)
    normed = low(hidden * inv_rms * norm_gain)
    gate_pre = low_back(jnp.dot(normed, z_weight, precision=HIGHEST))
    x_pre = low_back(jnp.dot(normed, x_weight, precision=HIGHEST))
    bc_pre = low_back(jnp.dot(normed, bc_weight, precision=HIGHEST))
    dt_pre = low_back(jnp.dot(normed, dt_weight, precision=HIGHEST))
    seq_count = prefix.shape[0]
    length = hidden.shape[0] // seq_count

    def one_sequence(element):
        x_one, bc_one, dt_one, prefix_one = element
        return mixer(x_one[None], bc_one[None], dt_one[None], x_conv, bc_conv, log_decay, dt_bias, skip_gain, prefix_one[None], Q)[0]
    ssd_out = lax.map(jax.checkpoint(one_sequence), (x_pre.reshape(seq_count, length, -1), bc_pre.reshape(seq_count, length, -1), dt_pre.reshape(seq_count, length, -1), prefix))
    ssd_out = ssd_out.reshape(hidden.shape[0], -1)
    gated = ssd_out * jax.nn.silu(gate_pre)
    inv_gate = lax.rsqrt(lax.optimization_barrier(jnp.mean(gated * gated, axis=-1, keepdims=True)) + EPSILON)
    projected = low(gated * inv_gate * gate_gain.reshape(-1))
    return hidden + jnp.dot(projected, out_weight, precision=HIGHEST)

def reference(hidden, cotangent, prefix, input_norm_gain, z_weight, x_weight, bc_weight, dt_weight, x_conv, bc_conv, log_decay, dt_bias, skip_gain, gate_gain, out_weight):
    primals = [arg.astype(jnp.float32) for arg in (hidden, input_norm_gain, z_weight, x_weight, bc_weight, dt_weight, x_conv, bc_conv, log_decay, dt_bias, skip_gain, gate_gain, out_weight)]

    def closed(*values):
        return forward(*values, prefix)
    mixed, backward = jax.vjp(closed, *primals)
    grads = backward(cotangent.astype(jnp.float32))
    return (mixed, grads[0], grads[1], grads[2], grads[3], grads[4], grads[5], grads[6], grads[7], grads[8], grads[9], grads[10], grads[11], grads[12])
```

```python
import functools

import jax
import jax.numpy as jnp
from jax import lax
from jax.experimental import pallas as pl
from jax.experimental.pallas import tpu as pltpu
from jax.sharding import PartitionSpec as P

P_SIZE = 64
N = 128
Q = 128
HG = 8
CG = HG * P_SIZE
MAX_PREFIX = 512
EPSILON = 1e-05
F32 = jnp.float32
BF16 = jnp.bfloat16
HIGHEST = lax.Precision.HIGHEST
NEG = -1e30
NN = ((1,), (0,))
NT = ((1,), (1,))
TN = ((0,), (0,))
MIB = 1024 * 1024


def dot(a, b, dims=NN):
    return lax.dot_general(a, b, (dims, ((), ())), preferred_element_type=F32)


def exact_dot(a, b, dims=NN):
    return lax.dot_general(
        a, b, (dims, ((), ())), precision=HIGHEST, preferred_element_type=F32
    )


def low(v):
    return v.astype(BF16)


def split_dot(v, e):
    hi = low(v)
    rest = low(v - hi.astype(F32))
    return dot(hi, e) + dot(rest, e)


def iota(shape, dim):
    return lax.broadcasted_iota(jnp.int32, shape, dim)


def sig(v):
    return 0.5 + 0.5 * jnp.tanh(0.5 * v)


def rows_of(c):
    return pl.ds(pl.multiple_of(c * Q, Q), Q)


def shifted_rows(x_ref, c):
    cur = x_ref[rows_of(c), :].astype(F32)
    start = pl.multiple_of(jnp.maximum(c * Q - 16, 0), 16)
    before = x_ref[pl.ds(start, 16), :].astype(F32)[8:]
    before = jnp.where(c > 0, before, 0.0)
    both = jnp.concatenate([before, cur], axis=0)
    return [cur] + [pltpu.roll(both, j, 0)[8:] for j in (1, 2, 3)]


def conv_of(shifted, taps):
    total = taps[3:4] * shifted[0]
    for j in (1, 2, 3):
        total = total + taps[3 - j : 4 - j] * shifted[j]
    return total


def spread_matrix(heads, width):
    return jnp.where(
        iota((heads, width), 1) // P_SIZE == iota((heads, width), 0), 1.0, 0.0
    ).astype(BF16)


def gather_matrix(width, lane0=0):
    return jnp.where(
        iota((width, 128), 0) // P_SIZE + lane0 == iota((width, 128), 1), 1.0, 0.0
    ).astype(BF16)


def prep_kernel(bc_ref, dt_ref, taps_ref, decay_ref, bias_ref, act_ref, cols_ref, rows_ref):
    heads = dt_ref.shape[1]
    groups = cols_ref.shape[0]
    length = dt_ref.shape[0]
    taps = taps_ref[...]
    tri = jnp.where(iota((Q, Q), 0) >= iota((Q, Q), 1), 1.0, 0.0).astype(F32)
    place = [
        jnp.where(iota((heads, 128), 1) == iota((heads, 128), 0) + k * heads, 1.0, 0.0).astype(F32)
        for k in range(3)
    ]

    def body(c, _):
        conv = conv_of(shifted_rows(bc_ref, c), taps)
        act_ref[rows_of(c), :] = low(conv * sig(conv))
        raw = dt_ref[rows_of(c), :] + bias_ref[...]
        step = jnp.maximum(raw, 0.0) + jnp.log(1.0 + jnp.exp(-jnp.abs(raw)))
        rate = -jnp.exp(decay_ref[...]) * step
        cum = exact_dot(tri, rate)
        packed = (
            exact_dot(cum, place[0])
            + exact_dot(cum - rate, place[1])
            + exact_dot(step, place[2])
        )
        turned = packed.T
        for g in range(groups):
            pick = jnp.where(
                (iota((128, 128), 0) == (iota((128, 128), 1) // HG) * heads + g * HG + iota((128, 128), 1) % HG)
                & (iota((128, 128), 1) < 3 * HG),
                1.0,
                0.0,
            ).astype(F32)
            cols_ref[g, rows_of(c), :] = exact_dot(packed, pick)
            rows_ref[g, 0:HG, rows_of(c)] = turned[g * HG : g * HG + HG]
            rows_ref[g, HG : 2 * HG, rows_of(c)] = turned[heads + g * HG : heads + g * HG + HG]
        return 0

    lax.fori_loop(0, length // Q, body, 0)


def prep(bc_pre, dt_pre, bc_taps, log_decay, dt_bias):
    length, heads = dt_pre.shape
    groups = heads // HG
    return pl.pallas_call(
        prep_kernel,
        out_shape=(
            jax.ShapeDtypeStruct((length, 2 * N), BF16),
            jax.ShapeDtypeStruct((groups, length, 128), F32),
            jax.ShapeDtypeStruct((groups, 2 * HG, length), F32),
        ),
        compiler_params=pltpu.CompilerParams(vmem_limit_bytes=32 * MIB),
        name="prep",
    )(bc_pre, dt_pre, bc_taps, log_decay[None], dt_bias[None])


def chunk_scalars(cols_ref, c, spread):
    part = cols_ref[0, rows_of(c), :]
    cum = part[:, 0:HG]
    ecum = part[:, HG : 2 * HG]
    step = part[:, 2 * HG : 3 * HG]
    last = cum[Q - 1 : Q, :]
    return cum, ecum, step, last


def prefix_column(prefix, c):
    return jnp.where(iota((Q, 1), 0) + c * Q < prefix, 1.0, 0.0).astype(F32)


def forward_kernel(
    prefix_ref, x_ref, taps_ref, skip_ref, cols_ref, rows_ref, act_ref, out_ref, xd_ref, kept_ref, back_ref, state_ref
):
    length, width = x_ref.shape
    chunks = length // Q
    anti = min(MAX_PREFIX // Q, chunks)
    prefix = prefix_ref[0]
    taps = taps_ref[...].astype(F32)
    skip = skip_ref[...]
    spread = spread_matrix(HG, width)
    lane_low = iota((1, 128), 1) < P_SIZE

    def stage_a(c, _):
        conv = conv_of(shifted_rows(x_ref, c), taps)
        x = conv * sig(conv)
        _, _, step, _ = chunk_scalars(cols_ref, c, spread)
        xd_ref[rows_of(c), :] = low(x * split_dot(step, spread))
        kept_ref[rows_of(c), :] = x * skip
        return 0

    lax.fori_loop(0, chunks, stage_a, 0)

    state_ref[...] = jnp.zeros_like(state_ref)
    back_ref[anti - 1] = jnp.zeros_like(back_ref[anti - 1])
    for c in range(anti - 1, 0, -1):
        cum, ecum, _, last = chunk_scalars(cols_ref, c, spread)
        weight = split_dot(jnp.exp(ecum) * prefix_column(prefix, c), spread)
        grow = split_dot(jnp.exp(cum[Q - 8 :]), spread)[7:8]
        b_mat = act_ref[rows_of(c), 0:N]
        xw = low(xd_ref[rows_of(c), :].astype(F32) * weight)
        state_ref[...] = state_ref[...] * grow + dot(b_mat, xw, TN)
        back_ref[c - 1] = low(state_ref[...])

    state_ref[...] = jnp.zeros_like(state_ref)
    causal_bias = jnp.where(iota((Q, Q), 1) <= iota((Q, Q), 0), 0.0, NEG).astype(F32)

    def chunk_body(c, two_way):
        b_mat = act_ref[rows_of(c), 0:N]
        c_mat = act_ref[rows_of(c), N : 2 * N]
        products = dot(c_mat, b_mat, NT)
        cum, ecum, _, last = chunk_scalars(cols_ref, c, spread)
        entering = split_dot(jnp.exp(cum), spread)
        total = kept_ref[rows_of(c), :] + dot(c_mat, low(state_ref[...])) * entering
        if two_way:
            leaving = split_dot(jnp.exp(last - ecum), spread)
            total = total + dot(c_mat, back_ref[c]) * leaving
            anti_bias = jnp.where(
                (iota((Q, Q), 1) > iota((Q, Q), 0)) & (iota((Q, Q), 1) + c * Q < prefix), 0.0, NEG
            ).astype(F32)
        xd = xd_ref[rows_of(c), :]
        rows = rows_ref[0, :, rows_of(c)]
        parts = []
        for pair in range(HG // 2):
            mixes = []
            for h in (2 * pair, 2 * pair + 1):
                e = cum[:, h : h + 1] - rows[h : h + 1] + causal_bias
                if two_way:
                    back = rows[HG + h : HG + h + 1] - ecum[:, h : h + 1] + anti_bias
                    e = jnp.maximum(e, back)
                mixes.append(low(jnp.exp(e) * products))
            x_pair = xd[:, pair * 128 : pair * 128 + 128]
            zero = jnp.zeros_like(x_pair)
            blocks = jnp.concatenate(
                [jnp.where(lane_low, x_pair, zero), jnp.where(lane_low, zero, x_pair)], axis=0
            )
            parts.append(dot(jnp.concatenate(mixes, axis=1), blocks))
        out_ref[rows_of(c), :] = (total + jnp.concatenate(parts, axis=1)).astype(out_ref.dtype)
        weight = split_dot(jnp.exp(last - cum), spread)
        xw = low(xd.astype(F32) * weight)
        state_ref[...] = state_ref[...] * entering[Q - 1 : Q] + dot(b_mat, xw, TN)
        return 0

    lax.fori_loop(0, anti, lambda c, _: chunk_body(c, True), 0)
    if chunks > anti:
        lax.fori_loop(anti, chunks, lambda c, _: chunk_body(c, False), 0)


def scan_forward(prefix, x_pre, taps, skip, cols, rows, act, out_type=BF16):
    length, channels = x_pre.shape
    groups = channels // CG
    anti = min(MAX_PREFIX // Q, length // Q)
    return pl.pallas_call(
        forward_kernel,
        grid=(groups,),
        in_specs=[
            pl.BlockSpec(memory_space=pltpu.SMEM),
            pl.BlockSpec((length, CG), lambda g: (0, g)),
            pl.BlockSpec((4, CG), lambda g: (0, g)),
            pl.BlockSpec((1, CG), lambda g: (0, g)),
            pl.BlockSpec((1, length, 128), lambda g: (g, 0, 0)),
            pl.BlockSpec((1, 2 * HG, length), lambda g: (g, 0, 0)),
            pl.BlockSpec((length, 2 * N), lambda g: (0, 0)),
        ],
        out_specs=pl.BlockSpec((length, CG), lambda g: (0, g)),
        out_shape=jax.ShapeDtypeStruct((length, channels), out_type),
        scratch_shapes=[
            pltpu.VMEM((length, CG), BF16),
            pltpu.VMEM((length, CG), F32),
            pltpu.VMEM((anti, N, CG), BF16),
            pltpu.VMEM((N, CG), F32),
        ],
        compiler_params=pltpu.CompilerParams(vmem_limit_bytes=40 * MIB),
        cost_estimate=pl.CostEstimate(
            flops=length * channels * 1024, bytes_accessed=length * channels * 6, transcendentals=length * channels * 4
        ),
        name="scan_forward",
    )(prefix, x_pre, taps, skip, cols, rows, act)


def backward_kernel(
    prefix_ref,
    x_ref,
    gate_ref,
    ssd_ref,
    gp_ref,
    norm_ref,
    taps_ref,
    skip_ref,
    gain_ref,
    cols_ref,
    rows_ref,
    act_ref,
    ggate_ref,
    gx_ref,
    gact_ref,
    gcols_ref,
    grows_ref,
    gsum_ref,
    x_scr,
    slope_scr,
    dy_scr,
    states_scr,
    dback_scr,
    state_ref,
    dstate_ref,
    next_scr,
):
    length, width = x_ref.shape
    chunks = length // Q
    anti = min(MAX_PREFIX // Q, chunks)
    prefix = prefix_ref[0]
    taps = taps_ref[...].astype(F32)
    skip = skip_ref[...]
    gain = gain_ref[...]
    spread = spread_matrix(HG, width)
    collect = gather_matrix(width)
    lane_low = iota((1, 128), 1) < P_SIZE

    gsum_ref[...] = jnp.zeros_like(gsum_ref)
    state_ref[...] = jnp.zeros_like(state_ref)

    @pl.when(pl.program_id(0) == 0)
    def _():
        gact_ref[...] = jnp.zeros_like(gact_ref)

    def stage_a(c, two_way):
        conv = conv_of(shifted_rows(x_ref, c), taps)
        s = sig(conv)
        x = conv * s
        x_scr[rows_of(c), :] = low(x)
        slope_scr[rows_of(c), :] = s + x * (1.0 - s)
        norm = norm_ref[rows_of(c), :]
        inv, coef = norm[:, 0:1], norm[:, 1:2]
        z = gate_ref[rows_of(c), :].astype(F32)
        y = ssd_ref[rows_of(c), :].astype(F32)
        gp = gp_ref[rows_of(c), :].astype(F32)
        sg = sig(z)
        act = z * sg
        gated = y * act
        gsum_ref[5:6, :] += jnp.sum(gp * gated * inv, axis=0, keepdims=True)
        gg = inv * gain * gp - gated * coef
        dy = gg * act
        ggate_ref[rows_of(c), :] = low(gg * y * (sg + act * (1.0 - sg)))
        dy_scr[rows_of(c), :] = low(dy)
        gsum_ref[4:5, :] += jnp.sum(dy * x, axis=0, keepdims=True)
        cum, ecum, step, last = chunk_scalars(cols_ref, c, spread)
        states_scr[c] = low(state_ref[...])
        entering = split_dot(jnp.exp(cum[Q - 8 :]), spread)
        weight = split_dot(jnp.exp(last - cum) * step, spread)
        b_mat = act_ref[rows_of(c), 0:N]
        c_mat = act_ref[rows_of(c), N : 2 * N]
        state_ref[...] = state_ref[...] * entering[7:8] + dot(b_mat, low(x * weight), TN)
        if two_way:
            leaving = split_dot(jnp.exp(last - ecum), spread)
            dback_scr[c + 1] = low(
                dback_scr[c].astype(F32) * entering[7:8] + dot(c_mat, low(dy * leaving), TN)
            )
        return 0

    dback_scr[0] = jnp.zeros_like(dback_scr[0])
    lax.fori_loop(0, anti, lambda c, _: stage_a(c, True), 0)
    if chunks > anti:
        lax.fori_loop(anti, chunks, lambda c, _: stage_a(c, False), 0)

    state_ref[...] = jnp.zeros_like(state_ref)
    dstate_ref[...] = jnp.zeros_like(dstate_ref)
    next_scr[...] = jnp.zeros_like(next_scr)
    s_idx, t_idx = iota((Q, Q), 0), iota((Q, Q), 1)
    causal_bias = jnp.where(s_idx <= t_idx, 0.0, NEG).astype(F32)
    from_r = jnp.where(s_idx >= t_idx, 1.0, 0.0)
    upto_r = jnp.where(s_idx <= t_idx, 1.0, 0.0)
    zero_q = jnp.zeros((Q, Q), F32)

    def twice(m):
        return low(
            jnp.concatenate(
                [jnp.concatenate([m, zero_q], axis=1), jnp.concatenate([zero_q, m], axis=1)], axis=0
            )
        )

    from_pair, upto_pair = twice(from_r), twice(upto_r)
    pair_s, pair_r = iota((Q, 2 * Q), 0), iota((Q, 2 * Q), 1) % Q
    before_pair = pair_s < pair_r
    after_pair = pair_s > pair_r
    sum_from = jnp.where(t_idx >= s_idx, 1.0, 0.0)
    sum_before = jnp.where(t_idx < s_idx, 1.0, 0.0)
    sum_upto = jnp.where(t_idx <= s_idx, 1.0, 0.0)
    sum_after = jnp.where(t_idx > s_idx, 1.0, 0.0)

    def chunk_body(c, two_way):
        b_mat = act_ref[rows_of(c), 0:N]
        c_mat = act_ref[rows_of(c), N : 2 * N]
        products = dot(b_mat, c_mat, NT)
        cum, ecum, step, last = chunk_scalars(cols_ref, c, spread)
        rows = rows_ref[0, :, rows_of(c)]
        x = x_scr[rows_of(c), :].astype(F32)
        dy_low = dy_scr[rows_of(c), :]
        dy = dy_low.astype(F32)
        step_wide = split_dot(step, spread)
        xd = x * step_wide
        xd_low = low(xd)
        if two_way:
            anti_bias = jnp.where((s_idx > t_idx) & (s_idx + c * Q < prefix), 0.0, NEG).astype(F32)
        dprod = jnp.zeros((Q, Q), F32)
        parts, inner = [], []
        for pair in range(HG // 2):
            lanes = slice(pair * 128, pair * 128 + 128)
            dy_pair = dy_low[:, lanes]
            zero = jnp.zeros_like(dy_pair)
            blocks = jnp.concatenate(
                [jnp.where(lane_low, dy_pair, zero), jnp.where(lane_low, zero, dy_pair)], axis=0
            )
            dmix = dot(xd_low[:, lanes], blocks, NT)
            mixes, moved = [], []
            for k in (0, 1):
                h = 2 * pair + k
                e = rows[h : h + 1] - cum[:, h : h + 1] + causal_bias
                if two_way:
                    back = ecum[:, h : h + 1] - rows[HG + h : HG + h + 1] + anti_bias
                    e = jnp.maximum(e, back)
                decay = jnp.exp(e)
                slab = dmix[:, k * Q : k * Q + Q] * decay
                dprod = dprod + slab
                mixes.append(low(decay * products))
                moved.append(low(slab * products))
            parts.append(dot(jnp.concatenate(mixes, axis=1), blocks))
            both = jnp.concatenate(moved, axis=1)
            crossing = jnp.where(before_pair, dot(both, from_pair), 0.0)
            if two_way:
                crossing = jnp.where(after_pair, dot(both, upto_pair), crossing)
            inner.append(jnp.sum(crossing, axis=0, keepdims=True))
        for pair in range(HG // 2):
            for k in (0, 1):
                h = 2 * pair + k
                grows_ref[0, h : h + 1, rows_of(c)] = inner[pair][:, k * Q : k * Q + Q]

        entering = split_dot(jnp.exp(cum), spread)
        to_last = split_dot(jnp.exp(last - cum), spread)
        grow = entering[Q - 1 : Q]
        dstate_low = low(dstate_ref[...])
        state_in = states_scr[c]
        du_carry = dot(b_mat, dstate_low) * to_last
        du = jnp.concatenate(parts, axis=1) + du_carry
        y_in = dot(c_mat, state_in) * entering
        dy_in = low(dy * entering)
        x_out = low(xd * to_last)
        d_c = dot(low(dprod), b_mat, TN) + dot(dy_in, state_in, NT)
        d_b = dot(low(dprod), c_mat) + dot(x_out, dstate_low, NT)
        qk = exact_dot(sum_from, dot(low(dy * y_in), collect)) + exact_dot(
            sum_before, dot(low(xd * du_carry), collect)
        )
        across = jnp.sum(dstate_ref[...] * state_in.astype(F32), axis=0, keepdims=True) * grow
        if two_way:
            back_state = state_ref[...]
            back_low = low(back_state)
            dback_low = dback_scr[c]
            leaving = split_dot(jnp.exp(last - ecum), spread)
            from_first = split_dot(jnp.exp(ecum) * prefix_column(prefix, c), spread)
            du_back = dot(b_mat, dback_low) * from_first
            du = du + du_back
            y_back = dot(c_mat, back_low) * leaving
            x_back = low(xd * from_first)
            d_c = d_c + dot(low(dy * leaving), back_low, NT)
            d_b = d_b + dot(x_back, dback_low, NT)
            qk = (
                qk
                + exact_dot(sum_upto, dot(low(dy * y_back), collect))
                + exact_dot(sum_after, dot(low(xd * du_back), collect))
            )
            across = across + grow * jnp.sum(
                dback_low.astype(F32) * back_state, axis=0, keepdims=True
            )
            state_ref[...] = back_state * grow + dot(b_mat, x_back, TN)
        dstate_ref[...] = dstate_ref[...] * grow + dot(c_mat, dy_in, TN)
        gact_ref[rows_of(c), 0:N] += d_b
        gact_ref[rows_of(c), N : 2 * N] += d_c
        direct = dot(low(x * du), collect)
        across8 = split_dot(jnp.broadcast_to(across, (8, width)), collect)
        gcols_ref[0, rows_of(c), 0:128] = direct
        gcols_ref[0, rows_of(c), 128:256] = qk + across8[0:1]

        dconv = (du * step_wide + skip * dy) * slope_scr[rows_of(c), :]
        shifted = shifted_rows(x_ref, c)
        both = jnp.concatenate([dconv, next_scr[...]], axis=0)
        gx = taps[3:4] * dconv
        gsum_ref[3:4, :] += jnp.sum(dconv * shifted[0], axis=0, keepdims=True)
        for j in (1, 2, 3):
            gx = gx + taps[3 - j : 4 - j] * pltpu.roll(both, Q + 8 - j, 0)[:Q]
            gsum_ref[3 - j : 4 - j, :] += jnp.sum(dconv * shifted[j], axis=0, keepdims=True)
        gx_ref[rows_of(c), :] = low(gx)
        next_scr[...] = dconv[0:8]
        return 0

    if chunks > anti:
        lax.fori_loop(0, chunks - anti, lambda i, _: chunk_body(chunks - 1 - i, False), 0)
    lax.fori_loop(0, anti, lambda i, _: chunk_body(anti - 1 - i, True), 0)


def scan_backward(prefix, x_pre, gate_pre, ssd_out, grad_projected, norm, taps, skip, gain, cols, rows, act):
    length, channels = x_pre.shape
    groups = channels // CG
    chunks = length // Q
    anti = min(MAX_PREFIX // Q, chunks)
    wide = pl.BlockSpec((length, CG), lambda g: (0, g))
    return pl.pallas_call(
        backward_kernel,
        grid=(groups,),
        in_specs=[
            pl.BlockSpec(memory_space=pltpu.SMEM),
            wide,
            wide,
            wide,
            wide,
            pl.BlockSpec((length, 2), lambda g: (0, 0)),
            pl.BlockSpec((4, CG), lambda g: (0, g)),
            pl.BlockSpec((1, CG), lambda g: (0, g)),
            pl.BlockSpec((1, CG), lambda g: (0, g)),
            pl.BlockSpec((1, length, 128), lambda g: (g, 0, 0)),
            pl.BlockSpec((1, 2 * HG, length), lambda g: (g, 0, 0)),
            pl.BlockSpec((length, 2 * N), lambda g: (0, 0)),
        ],
        out_specs=[
            wide,
            wide,
            pl.BlockSpec((length, 2 * N), lambda g: (0, 0)),
            pl.BlockSpec((1, length, 256), lambda g: (g, 0, 0)),
            pl.BlockSpec((1, HG, length), lambda g: (g, 0, 0)),
            pl.BlockSpec((8, CG), lambda g: (0, g)),
        ],
        out_shape=(
            jax.ShapeDtypeStruct((length, channels), BF16),
            jax.ShapeDtypeStruct((length, channels), BF16),
            jax.ShapeDtypeStruct((length, 2 * N), F32),
            jax.ShapeDtypeStruct((groups, length, 256), F32),
            jax.ShapeDtypeStruct((groups, HG, length), F32),
            jax.ShapeDtypeStruct((8, channels), F32),
        ),
        scratch_shapes=[
            pltpu.VMEM((length, CG), BF16),
            pltpu.VMEM((length, CG), F32),
            pltpu.VMEM((length, CG), BF16),
            pltpu.VMEM((chunks, N, CG), BF16),
            pltpu.VMEM((anti + 1, N, CG), BF16),
            pltpu.VMEM((N, CG), F32),
            pltpu.VMEM((N, CG), F32),
            pltpu.VMEM((8, CG), F32),
        ],
        compiler_params=pltpu.CompilerParams(vmem_limit_bytes=48 * MIB),
        cost_estimate=pl.CostEstimate(
            flops=length * channels * 4096, bytes_accessed=length * channels * 14, transcendentals=length * channels * 8
        ),
        name="scan_backward",
    )(prefix, x_pre, gate_pre, ssd_out, grad_projected, norm, taps, skip, gain, cols, rows, act)


def post_kernel(
    bc_ref, dt_ref, taps_ref, decay_ref, bias_ref, gact_ref, gcols_ref, grows_ref, gbc_ref, gdt_ref, gtaps_ref, ghead_ref, next_scr
):
    length, heads = dt_ref.shape
    groups = gcols_ref.shape[0]
    chunks = length // Q
    taps = taps_ref[...]
    gtaps_ref[...] = jnp.zeros_like(gtaps_ref)
    ghead_ref[...] = jnp.zeros_like(ghead_ref)
    next_scr[...] = jnp.zeros_like(next_scr)
    growth = -jnp.exp(decay_ref[...])
    bias = bias_ref[...]

    def body(i, _):
        c = chunks - 1 - i
        shifted = shifted_rows(bc_ref, c)
        conv = conv_of(shifted, taps)
        s = sig(conv)
        dconv = gact_ref[rows_of(c), :] * (s + conv * s * (1.0 - s))
        both = jnp.concatenate([dconv, next_scr[...]], axis=0)
        g = taps[3:4] * dconv
        gtaps_ref[3:4, :] += jnp.sum(dconv * shifted[0], axis=0, keepdims=True)
        for j in (1, 2, 3):
            g = g + taps[3 - j : 4 - j] * pltpu.roll(both, Q + 8 - j, 0)[:Q]
            gtaps_ref[3 - j : 4 - j, :] += jnp.sum(dconv * shifted[j], axis=0, keepdims=True)
        gbc_ref[rows_of(c), :] = g
        next_scr[...] = dconv[0:8]

        direct = jnp.zeros((Q, heads), F32)
        moved = jnp.zeros((Q, heads), F32)
        for g in range(groups):
            lift = jnp.where(
                (iota((128, heads), 1) == iota((128, heads), 0) + g * HG) & (iota((128, heads), 0) < HG), 1.0, 0.0
            ).astype(F32)
            direct = direct + exact_dot(gcols_ref[g, rows_of(c), 0:128], lift)
            moved = moved + exact_dot(gcols_ref[g, rows_of(c), 128:256], lift)
            moved = moved + exact_dot(grows_ref[g, :, rows_of(c)], lift[0:HG], TN)
        raw = dt_ref[rows_of(c), :] + bias
        step = jnp.maximum(raw, 0.0) + jnp.log(1.0 + jnp.exp(-jnp.abs(raw)))
        gdt = (direct + moved * growth) * sig(raw)
        gdt_ref[rows_of(c), :] = low(gdt)
        ghead_ref[0:1, :] += jnp.sum(moved * growth * step, axis=0, keepdims=True)
        ghead_ref[1:2, :] += jnp.sum(gdt, axis=0, keepdims=True)
        return 0

    lax.fori_loop(0, chunks, body, 0)


def post(bc_pre, dt_pre, bc_taps, log_decay, dt_bias, grad_act, gcols, grows):
    length, heads = dt_pre.shape
    return pl.pallas_call(
        post_kernel,
        out_shape=(
            jax.ShapeDtypeStruct((length, 2 * N), F32),
            jax.ShapeDtypeStruct((length, heads), BF16),
            jax.ShapeDtypeStruct((8, 2 * N), F32),
            jax.ShapeDtypeStruct((8, heads), F32),
        ),
        scratch_shapes=[pltpu.VMEM((8, 2 * N), F32)],
        compiler_params=pltpu.CompilerParams(vmem_limit_bytes=40 * MIB),
        name="post",
    )(bc_pre, dt_pre, bc_taps, log_decay[None], dt_bias[None], grad_act, gcols, grows)


def on_device(
    hidden,
    cotangent,
    prefix,
    input_norm_gain,
    z_weight,
    x_weight,
    bc_weight,
    dt_weight,
    x_conv,
    bc_conv,
    log_decay,
    dt_bias,
    skip_gain,
    gate_gain,
    out_weight,
):
    fsdp = lax.axis_size("fsdp")
    tp = lax.axis_size("tp")
    own, width = hidden.shape
    heads = log_decay.shape[0]
    channels = heads * P_SIZE
    all_channels = channels * tp
    length = own * tp
    taps_own = x_conv.shape[2]

    def gather(v):
        return lax.all_gather(v, "fsdp", axis=0, tiled=True)

    small = jnp.concatenate(
        [input_norm_gain.reshape(-1), x_conv.reshape(-1), bc_conv.reshape(-1), gate_gain.reshape(-1)]
    )
    sizes = [input_norm_gain.size, x_conv.size, bc_conv.size, gate_gain.size]
    rows = width // fsdp
    small_columns = -(-small.size // rows)
    tail = jnp.pad(small, (0, small_columns * rows - small.size)).reshape(rows, small_columns)
    first = jnp.concatenate([bc_weight, dt_weight, tail], axis=1)
    hidden_all = lax.all_gather(hidden, "tp", axis=0, tiled=True)
    first_all = gather(first)
    x_all = gather(x_weight)
    z_all = gather(z_weight)
    cot_all = lax.all_gather(cotangent, "tp", axis=0, tiled=True)
    out_all = gather(out_weight.T)

    bc_all = first_all[:, : 2 * N]
    dt_all = first_all[:, 2 * N : 2 * N + heads]
    small_all = first_all[:, 2 * N + heads :].reshape(fsdp, -1)
    cuts = [0]
    for size in sizes:
        cuts.append(cuts[-1] + size)
    norm_gain = small_all[:, cuts[0] : cuts[1]].reshape(-1).astype(F32)
    x_taps = small_all[:, cuts[1] : cuts[2]].reshape(fsdp, heads, 4, taps_own)
    x_taps = jnp.transpose(x_taps, (2, 1, 0, 3)).reshape(4, channels).astype(F32)
    bc_taps = small_all[:, cuts[2] : cuts[3]].reshape(fsdp, 4, -1)
    bc_taps = jnp.transpose(bc_taps, (1, 0, 2)).reshape(4, 2 * N).astype(F32)
    gain = small_all[:, cuts[3] : cuts[4]].reshape(fsdp, heads, -1)
    gain = jnp.transpose(gain, (1, 0, 2)).reshape(1, channels).astype(F32)
    skip = jnp.repeat(skip_gain, P_SIZE)[None]

    wide_all = hidden_all.astype(F32)
    inv_rms_all = lax.rsqrt(jnp.mean(wide_all * wide_all, axis=-1, keepdims=True) + EPSILON)
    normed = low(wide_all * inv_rms_all * norm_gain)
    bc_pre = dot(normed, bc_all)
    dt_pre = dot(normed, dt_all)
    x_pre = low(dot(normed, x_all))
    act, cols, head_rows = prep(bc_pre, dt_pre, bc_taps, log_decay, dt_bias)
    ssd_out = scan_forward(prefix, x_pre, x_taps, skip, cols, head_rows, act)

    gate_pre = dot(normed, z_all)
    gated = ssd_out.astype(F32) * (gate_pre * sig(gate_pre))
    square_sum = lax.psum(jnp.sum(gated * gated, axis=-1), "tp")
    gate_low = low(gate_pre)
    inv_gate = lax.rsqrt(square_sum / all_channels + EPSILON)[:, None]
    projected = low(gated * inv_gate * gain)

    grad_projected = dot(cot_all, out_all)
    dot_sum = lax.psum(jnp.sum(grad_projected * gain * gated, axis=-1), "tp")
    coef = inv_gate * inv_gate * inv_gate * (dot_sum / all_channels)[:, None]
    norm = jnp.concatenate([inv_gate, coef], axis=1)
    grad_low = low(grad_projected)

    def scatter_tp(v):
        return lax.psum_scatter(low(v), "tp", scatter_dimension=0, tiled=True).astype(F32)

    def scatter(v):
        return lax.psum_scatter(low(v), "fsdp", scatter_dimension=0, tiled=True).astype(F32)

    wide = hidden.astype(F32)
    branch = scatter_tp(dot(projected, out_all, NT))
    mixed = wide + branch
    grad_out = scatter(dot(cot_all, projected, TN))

    ggate, gx, gact, gcols, grows, gsum = scan_backward(
        prefix, x_pre, gate_low, ssd_out, grad_low, norm, x_taps, skip, gain, cols, head_rows, act
    )
    gbc_part, gdt, gbc_taps, ghead = post(
        bc_pre, dt_pre, bc_taps, log_decay, dt_bias, gact, gcols, grows
    )
    grad_z = scatter(dot(normed, ggate, TN))
    grad_x = scatter(dot(normed, gx, TN))
    gbc = low(lax.psum_scatter(gbc_part, "tp", scatter_dimension=0, tiled=True))
    part = dot(ggate, z_all, NT) + dot(gx, x_all, NT) + dot(gdt, dt_all, NT)
    grad_normed = scatter_tp(part) + dot(gbc, bc_all, NT)
    inv_rms = lax.rsqrt(jnp.mean(wide * wide, axis=-1, keepdims=True) + EPSILON)
    normed_own = low(wide * inv_rms * norm_gain)
    grad_rest = scatter(
        jnp.concatenate([dot(normed_own, gbc, TN), dot(normed, gdt, TN)], axis=1)
    )
    grad_gain = jnp.sum(grad_normed * wide * inv_rms, axis=0)
    scaled = grad_normed * norm_gain
    grad_hidden = (
        inv_rms * scaled
        - wide * inv_rms * inv_rms * inv_rms * jnp.mean(scaled * wide, axis=-1, keepdims=True)
        + cotangent.astype(F32)
    )
    gx_taps = jnp.transpose(gsum[0:4].reshape(4, heads, fsdp, taps_own), (2, 1, 0, 3))
    g_taps = jnp.transpose(gbc_taps[0:4].reshape(4, fsdp, -1), (1, 0, 2))
    g_gain = jnp.transpose(gsum[5].reshape(heads, fsdp, -1), (1, 0, 2))
    g_skip = jnp.sum(gsum[4].reshape(heads, P_SIZE), axis=-1)
    slices = jnp.concatenate(
        [
            grad_gain.reshape(fsdp, -1),
            g_taps.reshape(fsdp, -1),
            gx_taps.reshape(fsdp, -1),
            g_gain.reshape(fsdp, -1),
        ],
        axis=1,
    )
    mine = lax.psum_scatter(slices, "fsdp", scatter_dimension=0, tiled=True)[0]
    per_head = lax.psum(jnp.concatenate([ghead[0], ghead[1], g_skip]), "fsdp")
    n_norm, n_taps = input_norm_gain.size, bc_conv.size
    shared = n_norm + n_taps
    together = lax.psum(
        jnp.concatenate([grad_rest[:, : 2 * N].reshape(-1), mine[:shared]]), "tp"
    )
    bc_size = rows * 2 * N
    return (
        mixed,
        grad_hidden,
        together[bc_size : bc_size + n_norm],
        grad_z,
        grad_x,
        together[:bc_size].reshape(rows, 2 * N),
        grad_rest[:, 2 * N :],
        mine[shared : shared + x_conv.size].reshape(x_conv.shape),
        together[bc_size + n_norm :].reshape(bc_conv.shape),
        per_head[:heads],
        per_head[heads : 2 * heads],
        per_head[2 * heads :],
        mine[shared + x_conv.size :].reshape(gate_gain.shape),
        grad_out.T,
    )


def solution(mesh):
    both = P(("fsdp", "tp"), None)
    split = P("fsdp", "tp")
    ins = (
        both, both, P("fsdp"), P("fsdp"), split, split, P("fsdp", None), split, P("tp", None, "fsdp"),
        P(None, "fsdp"), P("tp"), P("tp"), P("tp"), P("tp", "fsdp"), P("tp", "fsdp"),
    )
    outs = (
        both, both, P("fsdp"), split, split, P("fsdp", None), split, P("tp", None, "fsdp"),
        P(None, "fsdp"), P("tp"), P("tp"), P("tp"), P("tp", "fsdp"), P("tp", "fsdp"),
    )
    return jax.shard_map(on_device, mesh=mesh, in_specs=ins, out_specs=outs, check_vma=False)
```

```python
import functools

import jax
import jax.numpy as jnp
from jax import lax
from jax.experimental import pallas as pl
from jax.experimental.pallas import tpu as pltpu
from jax.sharding import PartitionSpec as P

P_SIZE = 64
N = 128
Q = 128
HG = 8
CG = HG * P_SIZE
MAX_PREFIX = 512
EPSILON = 1e-05
F32 = jnp.float32
BF16 = jnp.bfloat16
HIGHEST = lax.Precision.HIGHEST
NEG = -1e30
NN = ((1,), (0,))
NT = ((1,), (1,))
TN = ((0,), (0,))
MIB = 1024 * 1024
NO_COST = pl.CostEstimate(flops=0, bytes_accessed=0, transcendentals=0)


def dot(a, b, dims=NN):
    return lax.dot_general(a, b, (dims, ((), ())), preferred_element_type=F32)


def exact_dot(a, b, dims=NN):
    return lax.dot_general(
        a, b, (dims, ((), ())), precision=HIGHEST, preferred_element_type=F32
    )


def low(v):
    return v.astype(BF16)


def split_dot(v, e):
    hi = low(v)
    rest = low(v - hi.astype(F32))
    return dot(hi, e) + dot(rest, e)


def iota(shape, dim):
    return lax.broadcasted_iota(jnp.int32, shape, dim)


def sig(v):
    return 0.5 + 0.5 * jnp.tanh(0.5 * v)


def rows_of(c):
    return pl.ds(pl.multiple_of(c * Q, Q), Q)


def shifted_rows(x_ref, c):
    cur = x_ref[rows_of(c), :].astype(F32)
    start = pl.multiple_of(jnp.maximum(c * Q - 16, 0), 16)
    before = x_ref[pl.ds(start, 16), :].astype(F32)[8:]
    before = jnp.where(c > 0, before, 0.0)
    both = jnp.concatenate([before, cur], axis=0)
    return [cur] + [pltpu.roll(both, j, 0)[8:] for j in (1, 2, 3)]


def conv_of(shifted, taps):
    total = taps[3:4] * shifted[0]
    for j in (1, 2, 3):
        total = total + taps[3 - j : 4 - j] * shifted[j]
    return total


def spread_matrix(heads, width):
    return jnp.where(
        iota((heads, width), 1) // P_SIZE == iota((heads, width), 0), 1.0, 0.0
    ).astype(BF16)


def gather_matrix(width, lane0=0):
    return jnp.where(
        iota((width, 128), 0) // P_SIZE + lane0 == iota((width, 128), 1), 1.0, 0.0
    ).astype(BF16)


def prep_kernel(bc_ref, dt_ref, taps_ref, decay_ref, bias_ref, act_ref, cols_ref, rows_ref):
    heads = dt_ref.shape[1]
    groups = cols_ref.shape[0]
    length = dt_ref.shape[0]
    taps = taps_ref[...]
    tri = jnp.where(iota((Q, Q), 0) >= iota((Q, Q), 1), 1.0, 0.0).astype(F32)
    place = [
        jnp.where(iota((heads, 128), 1) == iota((heads, 128), 0) + k * heads, 1.0, 0.0).astype(F32)
        for k in range(3)
    ]

    def body(c, _):
        conv = conv_of(shifted_rows(bc_ref, c), taps)
        act_ref[rows_of(c), :] = low(conv * sig(conv))
        raw = dt_ref[rows_of(c), :] + bias_ref[...]
        step = jnp.maximum(raw, 0.0) + jnp.log(1.0 + jnp.exp(-jnp.abs(raw)))
        rate = -jnp.exp(decay_ref[...]) * step
        cum = exact_dot(tri, rate)
        packed = (
            exact_dot(cum, place[0])
            + exact_dot(cum - rate, place[1])
            + exact_dot(step, place[2])
        )
        turned = packed.T
        for g in range(groups):
            pick = jnp.where(
                (iota((128, 128), 0) == (iota((128, 128), 1) // HG) * heads + g * HG + iota((128, 128), 1) % HG)
                & (iota((128, 128), 1) < 3 * HG),
                1.0,
                0.0,
            ).astype(F32)
            cols_ref[g, rows_of(c), :] = exact_dot(packed, pick)
            rows_ref[g, 0:HG, rows_of(c)] = turned[g * HG : g * HG + HG]
            rows_ref[g, HG : 2 * HG, rows_of(c)] = turned[heads + g * HG : heads + g * HG + HG]
        return 0

    lax.fori_loop(0, length // Q, body, 0)


def prep(bc_pre, dt_pre, bc_taps, log_decay, dt_bias):
    length, heads = dt_pre.shape
    groups = heads // HG
    return pl.pallas_call(
        prep_kernel,
        out_shape=(
            jax.ShapeDtypeStruct((length, 2 * N), BF16),
            jax.ShapeDtypeStruct((groups, length, 128), F32),
            jax.ShapeDtypeStruct((groups, 2 * HG, length), F32),
        ),
        compiler_params=pltpu.CompilerParams(vmem_limit_bytes=32 * MIB),
        cost_estimate=NO_COST,
        name="prep",
    )(bc_pre, dt_pre, bc_taps, log_decay[None], dt_bias[None])


def chunk_scalars(cols_ref, c, spread):
    part = cols_ref[0, rows_of(c), :]
    cum = part[:, 0:HG]
    ecum = part[:, HG : 2 * HG]
    step = part[:, 2 * HG : 3 * HG]
    last = cum[Q - 1 : Q, :]
    return cum, ecum, step, last


def prefix_column(prefix, c):
    return jnp.where(iota((Q, 1), 0) + c * Q < prefix, 1.0, 0.0).astype(F32)


def forward_kernel(
    prefix_ref, x_ref, taps_ref, skip_ref, cols_ref, rows_ref, act_ref, *refs
):
    out_ref, xd_ref, kept_ref, back_ref, state_ref = refs[-5:]
    length, width = x_ref.shape
    chunks = length // Q
    anti = min(MAX_PREFIX // Q, chunks)
    prefix = prefix_ref[0]
    taps = taps_ref[...].astype(F32)
    skip = skip_ref[...]
    spread = spread_matrix(HG, width)
    lane_low = iota((1, 128), 1) < P_SIZE

    def stage_a(c, _):
        conv = conv_of(shifted_rows(x_ref, c), taps)
        x = conv * sig(conv)
        _, _, step, _ = chunk_scalars(cols_ref, c, spread)
        xd_ref[rows_of(c), :] = low(x * split_dot(step, spread))
        kept_ref[rows_of(c), :] = x * skip
        return 0

    lax.fori_loop(0, chunks, stage_a, 0)

    state_ref[...] = jnp.zeros_like(state_ref)
    back_ref[anti - 1] = jnp.zeros_like(back_ref[anti - 1])
    for c in range(anti - 1, 0, -1):
        cum, ecum, _, last = chunk_scalars(cols_ref, c, spread)
        weight = split_dot(jnp.exp(ecum) * prefix_column(prefix, c), spread)
        grow = split_dot(jnp.exp(cum[Q - 8 :]), spread)[7:8]
        b_mat = act_ref[rows_of(c), 0:N]
        xw = low(xd_ref[rows_of(c), :].astype(F32) * weight)
        state_ref[...] = state_ref[...] * grow + dot(b_mat, xw, TN)
        back_ref[c - 1] = low(state_ref[...])

    state_ref[...] = jnp.zeros_like(state_ref)
    causal_bias = jnp.where(iota((Q, Q), 1) <= iota((Q, Q), 0), 0.0, NEG).astype(F32)

    def chunk_body(c, two_way):
        b_mat = act_ref[rows_of(c), 0:N]
        c_mat = act_ref[rows_of(c), N : 2 * N]
        products = dot(c_mat, b_mat, NT)
        cum, ecum, _, last = chunk_scalars(cols_ref, c, spread)
        entering = split_dot(jnp.exp(cum), spread)
        total = kept_ref[rows_of(c), :] + dot(c_mat, low(state_ref[...])) * entering
        if two_way:
            leaving = split_dot(jnp.exp(last - ecum), spread)
            total = total + dot(c_mat, back_ref[c]) * leaving
            anti_bias = jnp.where(
                (iota((Q, Q), 1) > iota((Q, Q), 0)) & (iota((Q, Q), 1) + c * Q < prefix), 0.0, NEG
            ).astype(F32)
        xd = xd_ref[rows_of(c), :]
        rows = rows_ref[0, :, rows_of(c)]
        parts = []
        for pair in range(HG // 2):
            mixes = []
            for h in (2 * pair, 2 * pair + 1):
                e = cum[:, h : h + 1] - rows[h : h + 1] + causal_bias
                if two_way:
                    back = rows[HG + h : HG + h + 1] - ecum[:, h : h + 1] + anti_bias
                    e = jnp.maximum(e, back)
                mixes.append(low(jnp.exp(e) * products))
            x_pair = xd[:, pair * 128 : pair * 128 + 128]
            zero = jnp.zeros_like(x_pair)
            blocks = jnp.concatenate(
                [jnp.where(lane_low, x_pair, zero), jnp.where(lane_low, zero, x_pair)], axis=0
            )
            parts.append(dot(jnp.concatenate(mixes, axis=1), blocks))
        out_ref[rows_of(c), :] = (total + jnp.concatenate(parts, axis=1)).astype(out_ref.dtype)
        weight = split_dot(jnp.exp(last - cum), spread)
        xw = low(xd.astype(F32) * weight)
        state_ref[...] = state_ref[...] * entering[Q - 1 : Q] + dot(b_mat, xw, TN)
        return 0

    lax.fori_loop(0, anti, lambda c, _: chunk_body(c, True), 0)
    if chunks > anti:
        lax.fori_loop(anti, chunks, lambda c, _: chunk_body(c, False), 0)


def scan_forward(prefix, x_pre, taps, skip, cols, rows, act, start, stop, out):
    length, channels = x_pre.shape
    anti = min(MAX_PREFIX // Q, length // Q)
    given = [prefix, x_pre, taps, skip, cols, rows, act]
    in_specs = [
        pl.BlockSpec(memory_space=pltpu.SMEM),
        pl.BlockSpec((length, CG), lambda g: (0, start + g)),
        pl.BlockSpec((4, CG), lambda g: (0, start + g)),
        pl.BlockSpec((1, CG), lambda g: (0, start + g)),
        pl.BlockSpec((1, length, 128), lambda g: (start + g, 0, 0)),
        pl.BlockSpec((1, 2 * HG, length), lambda g: (start + g, 0, 0)),
        pl.BlockSpec((length, 2 * N), lambda g: (0, 0)),
    ]
    aliases = {}
    if out is not None:
        aliases = {len(given): 0}
        given.append(out)
        in_specs.append(pl.BlockSpec(memory_space=pl.ANY))
    return pl.pallas_call(
        forward_kernel,
        grid=(stop - start,),
        in_specs=in_specs,
        out_specs=pl.BlockSpec((length, CG), lambda g: (0, start + g)),
        out_shape=jax.ShapeDtypeStruct((length, channels), BF16),
        input_output_aliases=aliases,
        scratch_shapes=[
            pltpu.VMEM((length, CG), BF16),
            pltpu.VMEM((length, CG), F32),
            pltpu.VMEM((anti, N, CG), BF16),
            pltpu.VMEM((N, CG), F32),
        ],
        compiler_params=pltpu.CompilerParams(vmem_limit_bytes=40 * MIB),
        cost_estimate=NO_COST,
        name="scan_forward",
    )(*given)


def backward_kernel(
    prefix_ref,
    x_ref,
    dy_scr,
    taps_ref,
    skip_ref,
    cols_ref,
    rows_ref,
    act_ref,
    *refs,
):
    (
        gx_ref,
        gact_ref,
        gcols_ref,
        grows_ref,
        gsum_ref,
        x_scr,
        slope_scr,
        states_scr,
        dback_scr,
        state_ref,
        dstate_ref,
        next_scr,
    ) = refs[-12:]
    length, width = x_ref.shape
    chunks = length // Q
    anti = min(MAX_PREFIX // Q, chunks)
    prefix = prefix_ref[0]
    taps = taps_ref[...].astype(F32)
    skip = skip_ref[...]
    spread = spread_matrix(HG, width)
    collect = gather_matrix(width)
    lane_low = iota((1, 128), 1) < P_SIZE

    gsum_ref[...] = jnp.zeros_like(gsum_ref)
    state_ref[...] = jnp.zeros_like(state_ref)

    @pl.when(pl.program_id(0) == 0)
    def _():
        gact_ref[...] = jnp.zeros_like(gact_ref)

    def stage_a(c, two_way):
        conv = conv_of(shifted_rows(x_ref, c), taps)
        s = sig(conv)
        x = conv * s
        x_scr[rows_of(c), :] = x
        slope_scr[rows_of(c), :] = s + x * (1.0 - s)
        dy = dy_scr[rows_of(c), :].astype(F32)
        gsum_ref[4:5, :] += jnp.sum(dy * x, axis=0, keepdims=True)
        cum, ecum, step, last = chunk_scalars(cols_ref, c, spread)
        states_scr[c] = low(state_ref[...])
        entering = split_dot(jnp.exp(cum[Q - 8 :]), spread)
        weight = split_dot(jnp.exp(last - cum) * step, spread)
        b_mat = act_ref[rows_of(c), 0:N]
        c_mat = act_ref[rows_of(c), N : 2 * N]
        state_ref[...] = state_ref[...] * entering[7:8] + dot(b_mat, low(x * weight), TN)
        if two_way:
            leaving = split_dot(jnp.exp(last - ecum), spread)
            dback_scr[c + 1] = low(
                dback_scr[c].astype(F32) * entering[7:8] + dot(c_mat, low(dy * leaving), TN)
            )
        return 0

    dback_scr[0] = jnp.zeros_like(dback_scr[0])
    lax.fori_loop(0, anti, lambda c, _: stage_a(c, True), 0)
    if chunks > anti:
        lax.fori_loop(anti, chunks, lambda c, _: stage_a(c, False), 0)

    state_ref[...] = jnp.zeros_like(state_ref)
    dstate_ref[...] = jnp.zeros_like(dstate_ref)
    next_scr[...] = jnp.zeros_like(next_scr)
    s_idx, t_idx = iota((Q, Q), 0), iota((Q, Q), 1)
    causal_bias = jnp.where(s_idx <= t_idx, 0.0, NEG).astype(F32)
    from_r = jnp.where(s_idx >= t_idx, 1.0, 0.0)
    upto_r = jnp.where(s_idx <= t_idx, 1.0, 0.0)
    zero_q = jnp.zeros((Q, Q), F32)

    def twice(m):
        return low(
            jnp.concatenate(
                [jnp.concatenate([m, zero_q], axis=1), jnp.concatenate([zero_q, m], axis=1)], axis=0
            )
        )

    from_pair, upto_pair = twice(from_r), twice(upto_r)
    pair_s, pair_r = iota((Q, 2 * Q), 0), iota((Q, 2 * Q), 1) % Q
    before_pair = pair_s < pair_r
    after_pair = pair_s > pair_r
    sum_from = jnp.where(t_idx >= s_idx, 1.0, 0.0)
    sum_before = jnp.where(t_idx < s_idx, 1.0, 0.0)
    sum_upto = jnp.where(t_idx <= s_idx, 1.0, 0.0)
    sum_after = jnp.where(t_idx > s_idx, 1.0, 0.0)

    def chunk_body(c, two_way):
        b_mat = act_ref[rows_of(c), 0:N]
        c_mat = act_ref[rows_of(c), N : 2 * N]
        products = dot(b_mat, c_mat, NT)
        cum, ecum, step, last = chunk_scalars(cols_ref, c, spread)
        rows = rows_ref[0, :, rows_of(c)]
        x = x_scr[rows_of(c), :]
        dy_low = dy_scr[rows_of(c), :]
        dy = dy_low.astype(F32)
        step_wide = split_dot(step, spread)
        xd = x * step_wide
        xd_low = low(xd)
        if two_way:
            anti_bias = jnp.where((s_idx > t_idx) & (s_idx + c * Q < prefix), 0.0, NEG).astype(F32)
        dprod = jnp.zeros((Q, Q), F32)
        parts, inner = [], []
        for pair in range(HG // 2):
            lanes = slice(pair * 128, pair * 128 + 128)
            dy_pair = dy_low[:, lanes]
            zero = jnp.zeros_like(dy_pair)
            blocks = jnp.concatenate(
                [jnp.where(lane_low, dy_pair, zero), jnp.where(lane_low, zero, dy_pair)], axis=0
            )
            dmix = dot(xd_low[:, lanes], blocks, NT)
            mixes, moved = [], []
            for k in (0, 1):
                h = 2 * pair + k
                e = rows[h : h + 1] - cum[:, h : h + 1] + causal_bias
                if two_way:
                    back = ecum[:, h : h + 1] - rows[HG + h : HG + h + 1] + anti_bias
                    e = jnp.maximum(e, back)
                decay = jnp.exp(e)
                slab = dmix[:, k * Q : k * Q + Q] * decay
                dprod = dprod + slab
                mixes.append(low(decay * products))
                moved.append(low(slab * products))
            parts.append(dot(jnp.concatenate(mixes, axis=1), blocks))
            both = jnp.concatenate(moved, axis=1)
            crossing = jnp.where(before_pair, dot(both, from_pair), 0.0)
            if two_way:
                crossing = jnp.where(after_pair, dot(both, upto_pair), crossing)
            inner.append(jnp.sum(crossing, axis=0, keepdims=True))
        for pair in range(HG // 2):
            for k in (0, 1):
                h = 2 * pair + k
                grows_ref[0, h : h + 1, rows_of(c)] = inner[pair][:, k * Q : k * Q + Q]

        entering = split_dot(jnp.exp(cum), spread)
        to_last = split_dot(jnp.exp(last - cum), spread)
        grow = entering[Q - 1 : Q]
        dstate_low = low(dstate_ref[...])
        state_in = states_scr[c]
        du_carry = dot(b_mat, dstate_low) * to_last
        du = jnp.concatenate(parts, axis=1) + du_carry
        y_in = dot(c_mat, state_in) * entering
        dy_in = low(dy * entering)
        x_out = low(xd * to_last)
        d_c = dot(low(dprod), b_mat, TN) + dot(dy_in, state_in, NT)
        d_b = dot(low(dprod), c_mat) + dot(x_out, dstate_low, NT)
        qk = exact_dot(sum_from, dot(low(dy * y_in), collect)) + exact_dot(
            sum_before, dot(low(xd * du_carry), collect)
        )
        across = jnp.sum(dstate_ref[...] * state_in.astype(F32), axis=0, keepdims=True) * grow
        if two_way:
            back_state = state_ref[...]
            back_low = low(back_state)
            dback_low = dback_scr[c]
            leaving = split_dot(jnp.exp(last - ecum), spread)
            from_first = split_dot(jnp.exp(ecum) * prefix_column(prefix, c), spread)
            du_back = dot(b_mat, dback_low) * from_first
            du = du + du_back
            y_back = dot(c_mat, back_low) * leaving
            x_back = low(xd * from_first)
            d_c = d_c + dot(low(dy * leaving), back_low, NT)
            d_b = d_b + dot(x_back, dback_low, NT)
            qk = (
                qk
                + exact_dot(sum_upto, dot(low(dy * y_back), collect))
                + exact_dot(sum_after, dot(low(xd * du_back), collect))
            )
            across = across + grow * jnp.sum(
                dback_low.astype(F32) * back_state, axis=0, keepdims=True
            )
            state_ref[...] = back_state * grow + dot(b_mat, x_back, TN)
        dstate_ref[...] = dstate_ref[...] * grow + dot(c_mat, dy_in, TN)
        gact_ref[rows_of(c), 0:N] += d_b
        gact_ref[rows_of(c), N : 2 * N] += d_c
        direct = dot(low(x * du), collect)
        across8 = split_dot(jnp.broadcast_to(across, (8, width)), collect)
        gcols_ref[0, rows_of(c), 0:128] = direct
        gcols_ref[0, rows_of(c), 128:256] = qk + across8[0:1]

        dconv = (du * step_wide + skip * dy) * slope_scr[rows_of(c), :]
        shifted = shifted_rows(x_ref, c)
        both = jnp.concatenate([dconv, next_scr[...]], axis=0)
        gx = taps[3:4] * dconv
        gsum_ref[3:4, :] += jnp.sum(dconv * shifted[0], axis=0, keepdims=True)
        for j in (1, 2, 3):
            gx = gx + taps[3 - j : 4 - j] * pltpu.roll(both, Q + 8 - j, 0)[:Q]
            gsum_ref[3 - j : 4 - j, :] += jnp.sum(dconv * shifted[j], axis=0, keepdims=True)
        gx_ref[rows_of(c), :] = low(gx)
        next_scr[...] = dconv[0:8]
        return 0

    if chunks > anti:
        lax.fori_loop(0, chunks - anti, lambda i, _: chunk_body(chunks - 1 - i, False), 0)
    lax.fori_loop(0, anti, lambda i, _: chunk_body(anti - 1 - i, True), 0)


def scan_backward(prefix, x_pre, grad_ssd, taps, skip, cols, rows, act, group, place, places, gx):
    length, channels = x_pre.shape
    chunks = length // Q
    anti = min(MAX_PREFIX // Q, chunks)
    wide = pl.BlockSpec((length, CG), lambda i: (0, group))
    given = [prefix, x_pre, grad_ssd, taps, skip, cols, rows, act]
    in_specs = [
        pl.BlockSpec(memory_space=pltpu.SMEM),
        wide,
        wide,
        pl.BlockSpec((4, CG), lambda i: (0, group)),
        pl.BlockSpec((1, CG), lambda i: (0, group)),
        pl.BlockSpec((1, length, 128), lambda i: (group, 0, 0)),
        pl.BlockSpec((1, 2 * HG, length), lambda i: (group, 0, 0)),
        pl.BlockSpec((length, 2 * N), lambda i: (0, 0)),
    ]
    aliases = {}
    if gx is not None:
        aliases = {len(given): 0}
        given.append(gx)
        in_specs.append(pl.BlockSpec(memory_space=pl.ANY))
    return pl.pallas_call(
        backward_kernel,
        grid=(1,),
        in_specs=in_specs,
        out_specs=[
            pl.BlockSpec((length, CG), lambda i: (0, place)),
            pl.BlockSpec((length, 2 * N), lambda i: (0, 0)),
            pl.BlockSpec((1, length, 256), lambda i: (0, 0, 0)),
            pl.BlockSpec((1, HG, length), lambda i: (0, 0, 0)),
            pl.BlockSpec((8, CG), lambda i: (0, 0)),
        ],
        out_shape=(
            jax.ShapeDtypeStruct((length, places * CG), BF16),
            jax.ShapeDtypeStruct((length, 2 * N), F32),
            jax.ShapeDtypeStruct((1, length, 256), F32),
            jax.ShapeDtypeStruct((1, HG, length), F32),
            jax.ShapeDtypeStruct((8, CG), F32),
        ),
        input_output_aliases=aliases,
        scratch_shapes=[
            pltpu.VMEM((length, CG), F32),
            pltpu.VMEM((length, CG), F32),
            pltpu.VMEM((chunks, N, CG), BF16),
            pltpu.VMEM((anti + 1, N, CG), BF16),
            pltpu.VMEM((N, CG), F32),
            pltpu.VMEM((N, CG), F32),
            pltpu.VMEM((8, CG), F32),
        ],
        compiler_params=pltpu.CompilerParams(vmem_limit_bytes=40 * MIB),
        cost_estimate=NO_COST,
        name="scan_backward",
    )(*given)


def gating_kernel(gate_ref, ssd_ref, gp_ref, norm_ref, gain_ref, ggate_ref, dy_ref, ggain_ref):
    gain = gain_ref[...]
    ggain_ref[...] = jnp.zeros_like(ggain_ref)

    def body(c, _):
        norm = norm_ref[rows_of(c), :]
        inv, coef = norm[:, 0:1], norm[:, 1:2]
        z = gate_ref[rows_of(c), :].astype(F32)
        y = ssd_ref[rows_of(c), :].astype(F32)
        gp = gp_ref[rows_of(c), :].astype(F32)
        sg = sig(z)
        act = z * sg
        gated = y * act
        scaled = inv * gp
        ggain_ref[0:1, :] += jnp.sum(scaled * gated, axis=0, keepdims=True)
        gg = gain * scaled - gated * coef
        ggate_ref[rows_of(c), :] = low(gg * y * (sg + act * (1.0 - sg)))
        dy_ref[rows_of(c), :] = low(gg * act)
        return 0

    lax.fori_loop(0, gate_ref.shape[0] // Q, body, 0)


def gating(gate_pre, ssd_out, grad_projected, norm, gain):
    length, channels = gate_pre.shape
    wide = pl.BlockSpec((length, CG), lambda g: (0, g))
    return pl.pallas_call(
        gating_kernel,
        grid=(channels // CG,),
        in_specs=[wide, wide, wide, pl.BlockSpec((length, 2), lambda g: (0, 0)), pl.BlockSpec((1, CG), lambda g: (0, g))],
        out_specs=[wide, wide, pl.BlockSpec((8, CG), lambda g: (0, g))],
        out_shape=(
            jax.ShapeDtypeStruct((length, channels), BF16),
            jax.ShapeDtypeStruct((length, channels), BF16),
            jax.ShapeDtypeStruct((8, channels), F32),
        ),
        compiler_params=pltpu.CompilerParams(vmem_limit_bytes=40 * MIB),
        cost_estimate=NO_COST,
        name="gating",
    )(gate_pre, ssd_out, grad_projected, norm, gain)


TILE = 128


def block_of(lanes_ref, j):
    return pl.ds(pl.multiple_of(lanes_ref[j] * 128, 128), 128)


def place_kernel(normalize, count, tiles, lanes_ref, slots_ref, *refs):
    sources, gain_ref, out_ref = refs[:count], refs[count], refs[count + 1]
    width = out_ref.shape[1]
    for k in range(count):

        @pl.when(pl.program_id(0) // tiles == k)
        def _(ref=sources[k]):
            if normalize:
                wide = ref[...].astype(F32)
                inv = lax.rsqrt(jnp.sum(wide * wide, axis=-1, keepdims=True) / width + EPSILON)
            for j in range(width // 128):
                here = slice(j * 128, j * 128 + 128)
                v = ref[:, block_of(lanes_ref, j)]
                if normalize:
                    v = low(v.astype(F32) * inv * gain_ref[:, here])
                out_ref[:, here] = v


def place_tokens(lanes, slots, sources, gain, normalize):
    tokens, width = sources[0].shape
    count, tiles = len(sources), tokens // TILE

    def source(k):
        return pl.BlockSpec((TILE, width), lambda i, a, s: (jnp.clip(i - k * tiles, 0, tiles - 1), 0))

    return pl.pallas_call(
        functools.partial(place_kernel, normalize, count, tiles),
        grid_spec=pltpu.PrefetchScalarGridSpec(
            num_scalar_prefetch=2,
            grid=(count * tiles,),
            in_specs=[source(k) for k in range(count)] + [pl.BlockSpec((1, width), lambda i, a, s: (0, 0))],
            out_specs=pl.BlockSpec((TILE, width), lambda i, a, s: (s[i // tiles] * tiles + i % tiles, 0)),
        ),
        out_shape=jax.ShapeDtypeStruct((tokens * count, width), BF16),
        compiler_params=pltpu.CompilerParams(vmem_limit_bytes=32 * MIB),
        cost_estimate=NO_COST,
        name="place_tokens",
    )(lanes, slots, *sources, gain)


def half_sum(refs, j, per_half):
    here = slice((j % per_half) * 128, (j % per_half) * 128 + 128)
    side = refs[: len(refs) // 2] if j < per_half else refs[len(refs) // 2 :]
    total = side[0][:, here].astype(F32)
    for ref in side[1:]:
        total = total + ref[:, here].astype(F32)
    return total


def mixed_kernel(lanes_ref, slots_ref, hidden_ref, *refs):
    out_ref = refs[-1]
    blocks = hidden_ref.shape[1] // 128
    for j in range(blocks):
        there = block_of(lanes_ref, j)
        out_ref[:, there] = hidden_ref[:, there].astype(F32) + half_sum(refs[:-1], j, blocks // 2)


def finish_kernel(lanes_ref, slots_ref, hidden_ref, cot_ref, gain_ref, *refs):
    out_ref = refs[-1]
    width = hidden_ref.shape[1]
    blocks = width // 128
    wide = hidden_ref[...].astype(F32)
    inv = lax.rsqrt(jnp.sum(wide * wide, axis=-1, keepdims=True) / width + EPSILON)
    total = jnp.zeros((TILE, 128), F32)
    for j in range(blocks):
        there = block_of(lanes_ref, j)
        scaled = half_sum(refs[:-1], j, blocks // 2) * gain_ref[:, j * 128 : j * 128 + 128]
        total = total + scaled * hidden_ref[:, there].astype(F32)
        out_ref[:, there] = scaled
    coef = inv * inv * inv * (jnp.sum(total, axis=-1, keepdims=True) / width)
    out_ref[...] = inv * out_ref[...] - wide * coef + cot_ref[...].astype(F32)


def own_rows(kernel, name, lanes, slots, hidden, more, gain, halves):
    tokens, width = hidden.shape
    tiles = tokens // TILE
    tile = pl.BlockSpec((TILE, width), lambda i, a, s: (i, 0))
    given, specs = [hidden, *more], [tile] * (1 + len(more))
    if gain is not None:
        given.append(gain)
        specs.append(pl.BlockSpec((1, width), lambda i, a, s: (0, 0)))
    for half in halves:
        for array, whole in half:
            given.append(array)
            if whole:
                specs.append(pl.BlockSpec((TILE, width // 2), lambda i, a, s: (s[0] * tiles + i, 0)))
            else:
                specs.append(pl.BlockSpec((TILE, width // 2), lambda i, a, s: (i, 0)))
    return pl.pallas_call(
        kernel,
        grid_spec=pltpu.PrefetchScalarGridSpec(
            num_scalar_prefetch=2, grid=(tiles,), in_specs=specs, out_specs=tile
        ),
        out_shape=jax.ShapeDtypeStruct((tokens, width), F32),
        compiler_params=pltpu.CompilerParams(vmem_limit_bytes=40 * MIB),
        cost_estimate=NO_COST,
        name=name,
    )(lanes, slots, *given)


def post_kernel(bc_ref, dt_ref, taps_ref, decay_ref, bias_ref, *refs):
    gbc_ref, gtaps_ref, ghead_ref, next_scr = refs[-4:]
    groups = (len(refs) - 4) // 3
    gacts, gcols, grows = refs[:groups], refs[groups : 2 * groups], refs[2 * groups : 3 * groups]
    length, heads = dt_ref.shape
    chunks = length // Q
    taps = taps_ref[...]
    gtaps_ref[...] = jnp.zeros_like(gtaps_ref)
    ghead_ref[...] = jnp.zeros_like(ghead_ref)
    next_scr[...] = jnp.zeros_like(next_scr)
    growth = -jnp.exp(decay_ref[...])
    bias = bias_ref[...]

    def body(i, _):
        c = chunks - 1 - i
        shifted = shifted_rows(bc_ref, c)
        conv = conv_of(shifted, taps)
        s = sig(conv)
        grad_act = sum(ref[rows_of(c), :] for ref in gacts[1:]) + gacts[0][rows_of(c), :]
        dconv = grad_act * (s + conv * s * (1.0 - s))
        both = jnp.concatenate([dconv, next_scr[...]], axis=0)
        g = taps[3:4] * dconv
        gtaps_ref[3:4, :] += jnp.sum(dconv * shifted[0], axis=0, keepdims=True)
        for j in (1, 2, 3):
            g = g + taps[3 - j : 4 - j] * pltpu.roll(both, Q + 8 - j, 0)[:Q]
            gtaps_ref[3 - j : 4 - j, :] += jnp.sum(dconv * shifted[j], axis=0, keepdims=True)
        gbc_ref[rows_of(c), 0 : 2 * N] = low(g)
        next_scr[...] = dconv[0:8]

        direct = jnp.zeros((Q, heads), F32)
        moved = jnp.zeros((Q, heads), F32)
        for g in range(groups):
            lift = jnp.where(
                (iota((128, heads), 1) == iota((128, heads), 0) + g * HG) & (iota((128, heads), 0) < HG), 1.0, 0.0
            ).astype(F32)
            direct = direct + exact_dot(gcols[g][0, rows_of(c), 0:128], lift)
            moved = moved + exact_dot(gcols[g][0, rows_of(c), 128:256], lift)
            moved = moved + exact_dot(grows[g][0, :, rows_of(c)], lift[0:HG], TN)
        raw = dt_ref[rows_of(c), :] + bias
        step = jnp.maximum(raw, 0.0) + jnp.log(1.0 + jnp.exp(-jnp.abs(raw)))
        gdt = (direct + moved * growth) * sig(raw)
        gbc_ref[rows_of(c), 2 * N :] = low(gdt)
        ghead_ref[0:1, :] += jnp.sum(moved * growth * step, axis=0, keepdims=True)
        ghead_ref[1:2, :] += jnp.sum(gdt, axis=0, keepdims=True)
        return 0

    lax.fori_loop(0, chunks, body, 0)


def post(bc_pre, dt_pre, bc_taps, log_decay, dt_bias, grad_act, gcols, grows):
    length, heads = dt_pre.shape
    return pl.pallas_call(
        post_kernel,
        out_shape=(
            jax.ShapeDtypeStruct((length, 2 * N + heads), BF16),
            jax.ShapeDtypeStruct((8, 2 * N), F32),
            jax.ShapeDtypeStruct((8, heads), F32),
        ),
        scratch_shapes=[pltpu.VMEM((8, 2 * N), F32)],
        compiler_params=pltpu.CompilerParams(vmem_limit_bytes=40 * MIB),
        cost_estimate=NO_COST,
        name="post",
    )(bc_pre, dt_pre, bc_taps, log_decay[None], dt_bias[None], *grad_act, *gcols, *grows)


def snake(devices):
    half = devices // 4
    return [z * 2 for z in range(half)] + [z * 2 + 1 for z in reversed(range(half))]


def chip_groups(devices):
    return [[chip * 2 + core for chip in snake(devices)] for core in (0, 1)]


def other_core(v, devices):
    return lax.ppermute(v, "fsdp", [(i, i ^ 1) for i in range(devices)])


def other_half(v):
    return lax.ppermute(v, "tp", [(0, 1), (1, 0)])


def tie(first, second):
    return lax.optimization_barrier((first, second))


def gather(v, devices):
    return lax.all_gather(v, "fsdp", axis=0, tiled=True, axis_index_groups=chip_groups(devices))


def scatter(v, devices):
    return lax.psum_scatter(
        v, "fsdp", scatter_dimension=0, tiled=True, axis_index_groups=chip_groups(devices)
    )


def add_low(own, came):
    return low(own.astype(F32) + came.astype(F32))


def spans(groups):
    half = groups // 2
    return [(0, half), (half, groups)] if half else [(0, groups)]


def on_device(
    hidden,
    cotangent,
    prefix,
    input_norm_gain,
    z_weight,
    x_weight,
    bc_weight,
    dt_weight,
    x_conv,
    bc_conv,
    log_decay,
    dt_bias,
    skip_gain,
    gate_gain,
    out_weight,
):
    fsdp = lax.axis_size("fsdp")
    tp = lax.axis_size("tp")
    own_tokens, width = hidden.shape
    heads = log_decay.shape[0]
    channels = heads * P_SIZE
    all_channels = channels * tp
    groups = channels // CG
    taps_own = x_conv.shape[2]
    rows = width // fsdp
    ring = fsdp // 2
    half_width = width // 2

    order = snake(fsdp)
    core = lax.axis_index("fsdp") % 2
    line = jnp.array(order, jnp.int32)
    blocks = jnp.concatenate([line * 2 + core, line * 2 + 1 - core])
    direct = rows % 128 == 0
    per = max(rows // 128, 1)
    if direct:
        lanes = (blocks[:, None] * per + jnp.arange(per)[None]).reshape(-1)
    else:
        lanes = jnp.arange(width // 128)
    lanes = lanes.astype(jnp.int32)

    def by_core(own, other):
        zero, one = jnp.where(core == 0, own, other), jnp.where(core == 0, other, own)
        return jnp.stack([m[order.index(chip)] for chip in range(ring) for m in (zero, one)])

    def to_cores(v):
        zero = jnp.stack([v[2 * chip] for chip in order])
        one = jnp.stack([v[2 * chip + 1] for chip in order])
        return jnp.where(core == 0, zero, one), jnp.where(core == 0, one, zero)

    def to_ring(v):
        return v if direct else v.reshape(-1, fsdp, rows)[:, blocks].reshape(v.shape)

    def from_ring(v):
        if direct:
            return v
        return v.reshape(-1, fsdp, rows)[:, jnp.argsort(blocks)].reshape(v.shape)

    small = jnp.concatenate(
        [input_norm_gain.reshape(-1), x_conv.reshape(-1), bc_conv.reshape(-1), gate_gain.reshape(-1)]
    )
    sizes = [input_norm_gain.size, x_conv.size, bc_conv.size, gate_gain.size]
    cuts = [0]
    for size in sizes:
        cuts.append(cuts[-1] + size)
    wide = channels + 2 * N + heads
    small_columns = -(-small.size // rows)
    columns = -(-(wide + small_columns) // 128) * 128
    tail = jnp.pad(small, (0, (columns - wide) * rows - small.size)).reshape(rows, columns - wide)
    payload = jnp.concatenate([x_weight, bc_weight, dt_weight, tail], axis=1)

    if tp == 2:
        mine = lax.axis_index("tp").astype(jnp.int32)
        slots = jnp.stack([mine, 1 - mine])
        hidden_other = other_half(hidden)
        cot_given, hidden_other = tie(cotangent, hidden_other)
        hidden_parts = [hidden, hidden_other]
        cot_parts = [cotangent, other_half(cot_given)]
    else:
        slots = jnp.zeros((2,), jnp.int32)
        hidden_parts = [lax.all_gather(hidden, "tp", axis=0, tiled=True)]
        cot_parts = [lax.all_gather(cotangent, "tp", axis=0, tiled=True)]
    hidden_parts = [to_ring(v) for v in hidden_parts]
    cot_parts = [to_ring(v) for v in cot_parts]

    x_own = gather(payload, fsdp)
    z_own = gather(z_weight, fsdp)
    out_own = gather(out_weight.T, fsdp)
    x_own, hidden_parts[-1] = tie(x_own, hidden_parts[-1])
    x_other = other_core(x_own, fsdp)

    tail_own = x_own[:, wide:].reshape(ring, -1)
    tail_other = x_other[:, wide:].reshape(ring, -1)
    norm_gain = jnp.concatenate([tail_own[:, : cuts[1]].reshape(1, -1), tail_other[:, : cuts[1]].reshape(1, -1)], axis=1)
    norm_gain = norm_gain.astype(F32)
    placed = by_core(tail_own, tail_other)
    x_taps = placed[:, cuts[1] : cuts[2]].reshape(fsdp, heads, 4, taps_own)
    x_taps = jnp.transpose(x_taps, (2, 1, 0, 3)).reshape(4, channels).astype(F32)
    bc_taps = placed[:, cuts[2] : cuts[3]].reshape(fsdp, 4, -1)
    bc_taps = jnp.transpose(bc_taps, (1, 0, 2)).reshape(4, 2 * N).astype(F32)
    gain = placed[:, cuts[3] : cuts[4]].reshape(fsdp, heads, -1)
    gain = jnp.transpose(gain, (1, 0, 2)).reshape(1, channels).astype(F32)
    skip = jnp.repeat(skip_gain, P_SIZE)[None]

    normed = place_tokens(lanes, slots, hidden_parts, norm_gain, True)
    na, nb = normed[:, :half_width], normed[:, half_width:]
    rest_own, rest_other = x_own[:, channels:wide], x_other[:, channels:wide]
    rest_pre = dot(na, rest_own) + dot(nb, rest_other)
    bc_pre, dt_pre = rest_pre[:, : 2 * N], rest_pre[:, 2 * N :]
    act, cols, head_rows = prep(bc_pre, dt_pre, bc_taps, log_decay, dt_bias)
    x_pre = low(dot(na, x_own[:, :channels]) + dot(nb, x_other[:, :channels]))
    ssd_out = None
    for start, stop in spans(groups):
        ssd_out = scan_forward(
            prefix, x_pre, x_taps, skip, cols, head_rows, act, start, stop, ssd_out
        )
        if start == 0:
            (z_own, cot_parts[-1]), ssd_out = tie((z_own, cot_parts[-1]), ssd_out)
            z_other = other_core(z_own, fsdp)

    gate_pre = dot(na, z_own) + dot(nb, z_other)
    gated = ssd_out.astype(F32) * (gate_pre * sig(gate_pre))
    square_sum = lax.psum(jnp.sum(gated * gated, axis=-1), "tp")
    gate_low = low(gate_pre)
    inv_gate = lax.rsqrt(square_sum / all_channels + EPSILON)[:, None]
    projected = low(gated * inv_gate * gain)

    out_own, projected = tie(out_own, projected)
    out_other = other_core(out_own, fsdp)
    cot_rel = place_tokens(lanes, slots, cot_parts, norm_gain, False)
    ca, cb = cot_rel[:, :half_width], cot_rel[:, half_width:]
    gout_other = low(dot(cb, projected, TN))
    gout_came = other_core(gout_other, fsdp)
    gout_own = low(dot(ca, projected, TN))

    (out_own, out_other), gout_own = tie((out_own, out_other), gout_own)
    grad_projected = dot(ca, out_own) + dot(cb, out_other)
    dot_sum = lax.psum(jnp.sum(grad_projected * gain * gated, axis=-1), "tp")
    coef = inv_gate * inv_gate * inv_gate * (dot_sum / all_channels)[:, None]
    norm = jnp.concatenate([inv_gate, coef], axis=1)
    gout_sum = add_low(gout_own, gout_came)
    norm, gout_sum = tie(norm, gout_sum)
    grad_out = scatter(gout_sum, fsdp)

    def to_own_tokens(v):
        if tp == 2:
            leaving = lax.dynamic_slice_in_dim(v, (1 - mine) * own_tokens, own_tokens, 0)
            return [(v, True), (other_half(leaving), False)]
        return [(lax.psum_scatter(v, "tp", scatter_dimension=0, tiled=True), False)]

    ggate, dy, ggain = gating(gate_low, ssd_out, low(grad_projected), norm, gain)
    gz_other = low(dot(nb, ggate, TN))
    gz_came = other_core(gz_other, fsdp)
    gz_own = low(dot(na, ggate, TN))
    projected, gz_own = tie(projected, gz_own)
    branch = [low(dot(projected, out_own, NT)), low(dot(projected, out_other, NT))]
    branch_parts = [to_own_tokens(v) for v in branch]
    kinds = [[whole for _, whole in half] for half in branch_parts]
    branch_parts = [[v for v, _ in half] for half in branch_parts]
    gz_sum = add_low(gz_own, gz_came)
    dy, gz_sum = tie(dy, gz_sum)
    grad_z = scatter(gz_sum, fsdp)

    gacts, gcols, grows, gsums = [], [], [], []
    first = groups // 2

    def back_through(start, stop, dy):
        gx = None
        for g in range(start, stop):
            gx, gact, gcol, grow, gsum = scan_backward(
                prefix, x_pre, dy, x_taps, skip, cols, head_rows, act, g, g - start, stop - start, gx
            )
            gacts.append(gact)
            gcols.append(gcol)
            grows.append(grow)
            gsums.append(gsum)
        return gx

    x_parts, sums = [], []
    if first:
        gx = back_through(0, first, dy)
        other = low(dot(nb, gx, TN))
        came = other_core(other, fsdp)
        own = low(dot(na, gx, TN))
        dy, (own, grad_out, branch_parts) = tie(dy, (own, grad_out, branch_parts))
        x_parts.append((0, first * CG, gx))
        sums.append((own, came))
    gx = back_through(first, groups, dy)
    gx, grad_z = tie(gx, grad_z)
    x_parts.append((first * CG, channels, gx))
    grad_x = []
    if first:
        total = add_low(*sums[0])
        gx, total = tie(gx, total)
        x_parts[-1] = (first * CG, channels, gx)
        grad_x.append(scatter(total, fsdp))
    gsum = jnp.concatenate(gsums, axis=1)
    grest, gbc_taps, ghead = post(bc_pre, dt_pre, bc_taps, log_decay, dt_bias, gacts, gcols, grows)

    def part_of(z_half, x_half):
        v = dot(ggate, z_half, NT)
        for lo, hi, gx in x_parts:
            v = v + dot(gx, x_half[:, lo:hi], NT)
        return v

    part = low(part_of(z_own, x_own) + dot(grest, rest_own, NT))
    part_sums = [to_own_tokens(part)]
    lo, hi, gx = x_parts[-1]
    gx, part = tie(gx, part)
    other = low(dot(nb, gx, TN))
    came = other_core(other, fsdp)
    own = low(dot(na, gx, TN))
    late = part_of(z_other, x_other)
    kinds_part = [whole for _, whole in part_sums[0]]
    (grest, own), arrived = tie((grest, own), [v for v, _ in part_sums[0]])
    part_sums = [list(zip(arrived, kinds_part))]
    parts = [part, low(late + dot(grest, rest_other, NT))]
    part_sums.append(to_own_tokens(parts[1]))
    grad_x.append(scatter(add_low(own, came), fsdp))
    grad_x = jnp.concatenate(grad_x, axis=1).astype(F32)

    mixed = from_ring(
        own_rows(
            mixed_kernel, "add_branch", lanes, slots, to_ring(hidden), [], None,
            [list(zip(half, kind)) for half, kind in zip(branch_parts, kinds)],
        )
    )
    grad_hidden = from_ring(
        own_rows(finish_kernel, "finish", lanes, slots, to_ring(hidden), [to_ring(cotangent)], norm_gain, part_sums)
    )

    grad_gain = jnp.concatenate(
        [
            jnp.sum(parts[0].astype(F32) * na.astype(F32), axis=0),
            jnp.sum(parts[1].astype(F32) * nb.astype(F32), axis=0),
        ]
    ) / norm_gain[0]
    grad_gain = grad_gain.reshape(2, ring, -1)
    gx_taps = jnp.transpose(gsum[0:4].reshape(4, heads, fsdp, taps_own), (2, 1, 0, 3))
    g_taps = jnp.transpose(gbc_taps[0:4].reshape(4, fsdp, -1), (1, 0, 2))
    g_gain = jnp.transpose(ggain[0].reshape(heads, fsdp, -1), (1, 0, 2))
    g_skip = jnp.sum(gsum[4].reshape(heads, P_SIZE), axis=-1)
    per_head = jnp.concatenate([ghead[0], ghead[1], g_skip])
    slices = jnp.concatenate(
        [
            g_taps.reshape(fsdp, -1),
            gx_taps.reshape(fsdp, -1),
            g_gain.reshape(fsdp, -1),
            jnp.broadcast_to(per_head[None], (fsdp, per_head.size)),
        ],
        axis=1,
    )
    size = grad_gain.shape[2] + slices.shape[1]
    lone = -(-size // rows)
    sides = []
    for side, n_half, slice_half in zip((0, 1), (na, nb), to_cores(slices)):
        lines = jnp.concatenate([grad_gain[side], slice_half], axis=1)
        lines = jnp.pad(lines, ((0, 0), (0, lone * rows - size))).reshape(half_width, lone)
        sides.append(jnp.concatenate([dot(n_half, grest, TN), lines], axis=1))
    mine_rest = scatter(sides[0] + other_core(sides[1], fsdp), fsdp)
    lines = mine_rest[:, 2 * N + heads :].reshape(-1)
    n_norm, n_taps = input_norm_gain.size, bc_conv.size
    shared = n_norm + n_taps
    together = jnp.concatenate([mine_rest[:, : 2 * N].reshape(-1), lines[:shared]])
    together = together + other_half(together) if tp == 2 else lax.psum(together, "tp")
    bc_size = rows * 2 * N
    at = [shared]
    for size in (x_conv.size, gate_gain.size, heads, heads, heads):
        at.append(at[-1] + size)
    return (
        mixed,
        grad_hidden,
        together[bc_size : bc_size + n_norm],
        grad_z.astype(F32),
        grad_x,
        together[:bc_size].reshape(rows, 2 * N),
        mine_rest[:, 2 * N : 2 * N + heads],
        lines[at[0] : at[1]].reshape(x_conv.shape),
        together[bc_size + n_norm :].reshape(bc_conv.shape),
        lines[at[2] : at[3]],
        lines[at[3] : at[4]],
        lines[at[4] : at[5]],
        lines[at[1] : at[2]].reshape(gate_gain.shape),
        grad_out.astype(F32).T,
    )


def solution(mesh):
    both = P(("fsdp", "tp"), None)
    split = P("fsdp", "tp")
    ins = (
        both, both, P("fsdp"), P("fsdp"), split, split, P("fsdp", None), split, P("tp", None, "fsdp"),
        P(None, "fsdp"), P("tp"), P("tp"), P("tp"), P("tp", "fsdp"), P("tp", "fsdp"),
    )
    outs = (
        both, both, P("fsdp"), split, split, P("fsdp", None), split, P("tp", None, "fsdp"),
        P(None, "fsdp"), P("tp"), P("tp"), P("tp"), P("tp", "fsdp"), P("tp", "fsdp"),
    )
    return jax.shard_map(on_device, mesh=mesh, in_specs=ins, out_specs=outs, check_vma=False)
```

```python
import functools

import jax
import jax.numpy as jnp
from jax import lax
from jax.experimental import pallas as pl
from jax.experimental.pallas import tpu as pltpu
from jax.sharding import PartitionSpec as P

P_SIZE = 64
N = 128
Q = 128
HG = 8
CG = HG * P_SIZE
MAX_PREFIX = 512
EPSILON = 1e-05
F32 = jnp.float32
BF16 = jnp.bfloat16
NEG = -1e30
NN = ((1,), (0,))
NT = ((1,), (1,))
TN = ((0,), (0,))
MIB = 1024 * 1024
NO_COST = pl.CostEstimate(flops=0, bytes_accessed=0, transcendentals=0)


def dot(a, b, dims=NN):
    return lax.dot_general(a, b, (dims, ((), ())), preferred_element_type=F32)


def low(v):
    return v.astype(BF16)


def split_dot(v, e):
    hi = low(v)
    rest = low(v - hi.astype(F32))
    return dot(jnp.concatenate([hi, rest], axis=1), e)


def low_pair_dot(v, e):
    hi = low(v)
    return dot(hi, e) + dot(low(v - hi.astype(F32)), e)


def three_dot(e, v):
    hi = low(v)
    rest = v - hi.astype(F32)
    mid = low(rest)
    return dot(e, hi) + (dot(e, mid) + dot(e, low(rest - mid.astype(F32))))


def iota(shape, dim):
    return lax.broadcasted_iota(jnp.int32, shape, dim)


def sig(v):
    return 0.5 + 0.5 * jnp.tanh(0.5 * v)


def rows_of(c):
    return pl.ds(pl.multiple_of(c * Q, Q), Q)


def shifted_rows(x_ref, c, width=None):
    lanes = slice(0, width)
    cur = x_ref[rows_of(c), lanes].astype(F32)
    start = pl.multiple_of(jnp.maximum(c * Q - 16, 0), 16)
    before = x_ref[pl.ds(start, 16), lanes].astype(F32)[8:]
    before = jnp.where(c > 0, before, 0.0)
    both = jnp.concatenate([before, cur], axis=0)
    return [cur] + [pltpu.roll(both, j, 0)[8:] for j in (1, 2, 3)]


def conv_of(shifted, taps):
    total = taps[3:4] * shifted[0]
    for j in (1, 2, 3):
        total = total + taps[3 - j : 4 - j] * shifted[j]
    return total


def spread_matrix(start, width):
    return jnp.where(
        iota((256, width), 1) // P_SIZE + start == iota((256, width), 0) % 128, 1.0, 0.0
    ).astype(BF16)


def gather_matrix(start, width):
    return jnp.where(
        iota((width, 128), 0) // P_SIZE + start == iota((width, 128), 1), 1.0, 0.0
    ).astype(BF16)


def prep_kernel(rest_ref, taps_ref, decay_ref, bias_ref, act_ref, cols_ref, rows_ref):
    heads = decay_ref.shape[1]
    length = rest_ref.shape[0]
    taps = taps_ref[...]
    tri = jnp.where(iota((Q, Q), 0) >= iota((Q, Q), 1), 1.0, 0.0).astype(BF16)
    lane = iota((1, 128), 1)
    filler = jnp.zeros((1, 128 - 3 * heads), F32)
    decay = jnp.concatenate([decay_ref[...]] * 3 + [filler], axis=1)
    bias = jnp.concatenate([bias_ref[...]] * 3 + [filler], axis=1)
    growth = -jnp.exp(decay)

    def body(c, _):
        conv = conv_of(shifted_rows(rest_ref, c, 2 * N), taps)
        act_ref[rows_of(c), :] = low(conv * sig(conv))
        raw = rest_ref[rows_of(c), 2 * N :] + bias
        raw = jnp.where(lane < 3 * heads, raw, 0.0)
        step = jnp.maximum(raw, 0.0) + jnp.log(1.0 + jnp.exp(-jnp.abs(raw)))
        rate = growth * step
        cum = three_dot(tri, rate)
        packed = jnp.where(lane < heads, cum, jnp.where(lane < 2 * heads, cum - rate, step))
        packed = jnp.where(lane < 3 * heads, packed, 0.0)
        cols_ref[rows_of(c), :] = packed
        rows_ref[:, rows_of(c)] = packed.T
        return 0

    lax.fori_loop(0, length // Q, body, 0, unroll=4)


def prep(rest_pre, bc_taps, log_decay, dt_bias):
    length = rest_pre.shape[0]
    return pl.pallas_call(
        prep_kernel,
        out_shape=(
            jax.ShapeDtypeStruct((length, 2 * N), BF16),
            jax.ShapeDtypeStruct((length, 128), F32),
            jax.ShapeDtypeStruct((128, length), F32),
        ),
        compiler_params=pltpu.CompilerParams(vmem_limit_bytes=32 * MIB),
        cost_estimate=NO_COST,
        name="prep",
    )(rest_pre, bc_taps, log_decay[None], dt_bias[None])


def prefix_column(prefix, c):
    return jnp.where(iota((Q, 1), 0) + c * Q < prefix, 1.0, 0.0).astype(F32)


def growths(part, heads):
    lane = iota((1, 128), 1)
    used = lane < 2 * heads
    tail = part[Q - 8 :]
    last = jnp.where(lane < heads, tail, pltpu.roll(tail, heads, 1))[7:8]
    within = jnp.where(used, jnp.exp(jnp.where(used, part, 0.0)), 0.0)
    beyond = jnp.where(used, jnp.exp(jnp.where(used, last - part, 0.0)), 0.0)
    return within, beyond


def forward_kernel(
    heads, first, prefix_ref, x_ref, taps_ref, skip_ref, cols_ref, rows_ref, act_ref, *refs
):
    out_ref, xd_ref, kept_ref, back_ref, state_ref = refs[-5:]
    length, width = x_ref.shape
    chunks = length // Q
    anti = min(MAX_PREFIX // Q, chunks)
    prefix = prefix_ref[0]
    taps = taps_ref[...].astype(F32)
    skip = skip_ref[...]
    by_cum = spread_matrix(first, width)
    by_ecum = spread_matrix(heads + first, width)
    by_step = spread_matrix(2 * heads + first, width)
    lane_low = iota((1, 128), 1) < P_SIZE

    def stage_a(c, _):
        conv = conv_of(shifted_rows(x_ref, c), taps)
        x = conv * sig(conv)
        xd_ref[rows_of(c), :] = low(x * split_dot(cols_ref[rows_of(c), :], by_step))
        kept_ref[rows_of(c), :] = x * skip
        return 0

    lax.fori_loop(0, chunks, stage_a, 0, unroll=4)

    state_ref[...] = jnp.zeros_like(state_ref)
    back_ref[anti - 1] = jnp.zeros_like(back_ref[anti - 1])
    for c in range(anti - 1, 0, -1):
        within, _ = growths(cols_ref[rows_of(c), :], heads)
        weight = split_dot(within * prefix_column(prefix, c), by_ecum)
        grow = split_dot(within[Q - 8 :], by_cum)[7:8]
        b_mat = act_ref[rows_of(c), 0:N]
        xw = low(xd_ref[rows_of(c), :].astype(F32) * weight)
        state_ref[...] = state_ref[...] * grow + dot(b_mat, xw, TN)
        back_ref[c - 1] = low(state_ref[...])

    state_ref[...] = jnp.zeros_like(state_ref)
    causal_bias = jnp.where(iota((Q, Q), 1) <= iota((Q, Q), 0), 0.0, NEG).astype(F32)

    def chunk_body(c, two_way):
        b_mat = act_ref[rows_of(c), 0:N]
        c_mat = act_ref[rows_of(c), N : 2 * N]
        products = dot(c_mat, b_mat, NT)
        part = cols_ref[rows_of(c), :]
        within, beyond = growths(part, heads)
        entering = split_dot(within, by_cum)
        total = kept_ref[rows_of(c), :] + dot(c_mat, low(state_ref[...])) * entering
        if two_way:
            leaving = split_dot(beyond, by_ecum)
            total = total + dot(c_mat, back_ref[c]) * leaving
            anti_bias = jnp.where(
                (iota((Q, Q), 1) > iota((Q, Q), 0)) & (iota((Q, Q), 1) + c * Q < prefix), 0.0, NEG
            ).astype(F32)
        xd = xd_ref[rows_of(c), :]
        rows = rows_ref[first : first + HG, rows_of(c)]
        erows = rows_ref[heads + first : heads + first + HG, rows_of(c)]
        parts = []
        for pair in range(HG // 2):
            mixes = []
            for h in (2 * pair, 2 * pair + 1):
                e = part[:, first + h : first + h + 1] - rows[h : h + 1] + causal_bias
                if two_way:
                    at = heads + first + h
                    back = erows[h : h + 1] - part[:, at : at + 1] + anti_bias
                    e = jnp.maximum(e, back)
                mixes.append(low(jnp.exp(e) * products))
            x_pair = xd[:, pair * 128 : pair * 128 + 128]
            zero = jnp.zeros_like(x_pair)
            blocks = jnp.concatenate(
                [jnp.where(lane_low, x_pair, zero), jnp.where(lane_low, zero, x_pair)], axis=0
            )
            parts.append(dot(jnp.concatenate(mixes, axis=1), blocks))
        out_ref[rows_of(c), :] = (total + jnp.concatenate(parts, axis=1)).astype(out_ref.dtype)
        weight = split_dot(beyond, by_cum)
        xw = low(xd.astype(F32) * weight)
        state_ref[...] = state_ref[...] * entering[Q - 1 : Q] + dot(b_mat, xw, TN)
        return 0

    lax.fori_loop(0, anti, lambda c, _: chunk_body(c, True), 0, unroll=4)
    if chunks > anti:
        lax.fori_loop(anti, chunks, lambda c, _: chunk_body(c, False), 0, unroll=4)


def scan_forward(prefix, x_pre, taps, skip, cols, rows, act, group, out):
    length, channels = x_pre.shape
    anti = min(MAX_PREFIX // Q, length // Q)
    given = [prefix, x_pre, taps, skip, cols, rows, act]
    in_specs = [
        pl.BlockSpec(memory_space=pltpu.SMEM),
        pl.BlockSpec((length, CG), lambda g: (0, group)),
        pl.BlockSpec((4, CG), lambda g: (0, group)),
        pl.BlockSpec((1, CG), lambda g: (0, group)),
        pl.BlockSpec((length, 128), lambda g: (0, 0)),
        pl.BlockSpec((128, length), lambda g: (0, 0)),
        pl.BlockSpec((length, 2 * N), lambda g: (0, 0)),
    ]
    aliases = {}
    if out is not None:
        aliases = {len(given): 0}
        given.append(out)
        in_specs.append(pl.BlockSpec(memory_space=pl.ANY))
    return pl.pallas_call(
        functools.partial(forward_kernel, channels // P_SIZE, group * HG),
        grid=(1,),
        in_specs=in_specs,
        out_specs=pl.BlockSpec((length, CG), lambda g: (0, group)),
        out_shape=jax.ShapeDtypeStruct((length, channels), BF16),
        input_output_aliases=aliases,
        scratch_shapes=[
            pltpu.VMEM((length, CG), BF16),
            pltpu.VMEM((length, CG), F32),
            pltpu.VMEM((anti, N, CG), BF16),
            pltpu.VMEM((N, CG), F32),
        ],
        compiler_params=pltpu.CompilerParams(vmem_limit_bytes=40 * MIB),
        cost_estimate=NO_COST,
        name="scan_forward",
    )(*given)


def backward_kernel(
    heads,
    first,
    more,
    prefix_ref,
    x_ref,
    dy_scr,
    taps_ref,
    skip_ref,
    cols_ref,
    rows_ref,
    act_ref,
    *refs,
):
    (
        gx_ref,
        gact_ref,
        gcols_ref,
        grows_ref,
        gsum_ref,
        x_scr,
        slope_scr,
        states_scr,
        dback_scr,
        state_ref,
        dstate_ref,
        next_scr,
    ) = refs[-12:]
    length, width = x_ref.shape
    chunks = length // Q
    anti = min(MAX_PREFIX // Q, chunks)
    prefix = prefix_ref[0]
    taps = taps_ref[...].astype(F32)
    skip = skip_ref[...]
    by_cum = spread_matrix(first, width)
    by_ecum = spread_matrix(heads + first, width)
    by_step = spread_matrix(2 * heads + first, width)
    collect = gather_matrix(first, width)
    lane_low = iota((1, 128), 1) < P_SIZE

    gsum_ref[...] = jnp.zeros_like(gsum_ref)
    state_ref[...] = jnp.zeros_like(state_ref)

    def stage_a(c, two_way):
        conv = conv_of(shifted_rows(x_ref, c), taps)
        s = sig(conv)
        x = conv * s
        x_scr[rows_of(c), :] = x
        slope_scr[rows_of(c), :] = s + x * (1.0 - s)
        dy = dy_scr[rows_of(c), :].astype(F32)
        gsum_ref[4:5, :] += jnp.sum(dy * x, axis=0, keepdims=True)
        part = cols_ref[rows_of(c), :]
        within, beyond = growths(part, heads)
        states_scr[c] = low(state_ref[...])
        entering = split_dot(within[Q - 8 :], by_cum)
        x_low = low(x * split_dot(part, by_step) * split_dot(beyond, by_cum))
        b_mat = act_ref[rows_of(c), 0:N]
        c_mat = act_ref[rows_of(c), N : 2 * N]
        state_ref[...] = state_ref[...] * entering[7:8] + dot(b_mat, x_low, TN)
        if two_way:
            leaving = split_dot(beyond, by_ecum)
            dback_scr[c + 1] = low(
                dback_scr[c].astype(F32) * entering[7:8] + dot(c_mat, low(dy * leaving), TN)
            )
        return 0

    dback_scr[0] = jnp.zeros_like(dback_scr[0])
    lax.fori_loop(0, anti, lambda c, _: stage_a(c, True), 0, unroll=4)
    if chunks > anti:
        lax.fori_loop(anti, chunks, lambda c, _: stage_a(c, False), 0, unroll=4)

    state_ref[...] = jnp.zeros_like(state_ref)
    dstate_ref[...] = jnp.zeros_like(dstate_ref)
    next_scr[...] = jnp.zeros_like(next_scr)
    s_idx, t_idx = iota((Q, Q), 0), iota((Q, Q), 1)
    causal_bias = jnp.where(s_idx <= t_idx, 0.0, NEG).astype(F32)
    from_r = jnp.where(s_idx >= t_idx, 1.0, 0.0)
    upto_r = jnp.where(s_idx <= t_idx, 1.0, 0.0)
    zero_q = jnp.zeros((Q, Q), F32)

    def twice(m):
        return low(
            jnp.concatenate(
                [jnp.concatenate([m, zero_q], axis=1), jnp.concatenate([zero_q, m], axis=1)], axis=0
            )
        )

    from_pair, upto_pair = twice(from_r), twice(upto_r)
    pair_s, pair_r = iota((Q, 2 * Q), 0), iota((Q, 2 * Q), 1) % Q
    before_pair = pair_s < pair_r
    after_pair = pair_s > pair_r
    sum_from = jnp.where(t_idx >= s_idx, 1.0, 0.0).astype(BF16)
    sum_before = jnp.where(t_idx < s_idx, 1.0, 0.0).astype(BF16)
    sum_upto = jnp.where(t_idx <= s_idx, 1.0, 0.0).astype(BF16)
    sum_after = jnp.where(t_idx > s_idx, 1.0, 0.0).astype(BF16)
    sum_all = jnp.concatenate([sum_from, sum_before, sum_upto, sum_after], axis=1)

    def chunk_body(c, two_way):
        b_mat = act_ref[rows_of(c), 0:N]
        c_mat = act_ref[rows_of(c), N : 2 * N]
        products = dot(b_mat, c_mat, NT)
        part = cols_ref[rows_of(c), :]
        within, beyond = growths(part, heads)
        rows = rows_ref[first : first + HG, rows_of(c)]
        erows = rows_ref[heads + first : heads + first + HG, rows_of(c)]
        x = x_scr[rows_of(c), :]
        dy_low = dy_scr[rows_of(c), :]
        dy = dy_low.astype(F32)
        step_wide = split_dot(part, by_step)
        xd = x * step_wide
        xd_low = low(xd)
        if two_way:
            anti_bias = jnp.where((s_idx > t_idx) & (s_idx + c * Q < prefix), 0.0, NEG).astype(F32)
        dprod = jnp.zeros((Q, Q), F32)
        parts, inner = [], []
        for pair in range(HG // 2):
            lanes = slice(pair * 128, pair * 128 + 128)
            dy_pair = dy_low[:, lanes]
            zero = jnp.zeros_like(dy_pair)
            blocks = jnp.concatenate(
                [jnp.where(lane_low, dy_pair, zero), jnp.where(lane_low, zero, dy_pair)], axis=0
            )
            dmix = dot(xd_low[:, lanes], blocks, NT)
            mixes, moved = [], []
            for k in (0, 1):
                h = 2 * pair + k
                e = rows[h : h + 1] - part[:, first + h : first + h + 1] + causal_bias
                if two_way:
                    at = heads + first + h
                    back = part[:, at : at + 1] - erows[h : h + 1] + anti_bias
                    e = jnp.maximum(e, back)
                decay = jnp.exp(e)
                slab = dmix[:, k * Q : k * Q + Q] * decay
                dprod = dprod + slab
                mixes.append(low(decay * products))
                moved.append(low(slab * products))
            parts.append(dot(jnp.concatenate(mixes, axis=1), blocks))
            both = jnp.concatenate(moved, axis=1)
            crossing = jnp.where(before_pair, dot(both, from_pair), 0.0)
            if two_way:
                crossing = jnp.where(after_pair, dot(both, upto_pair), crossing)
            inner.append(jnp.sum(crossing, axis=0, keepdims=True))
        for pair in range(HG // 2):
            for k in (0, 1):
                h = 2 * pair + k
                grows_ref[0, h : h + 1, rows_of(c)] = inner[pair][:, k * Q : k * Q + Q]

        entering = split_dot(within, by_cum)
        to_last = split_dot(beyond, by_cum)
        grow = entering[Q - 1 : Q]
        dstate_low = low(dstate_ref[...])
        state_in = states_scr[c]
        du_carry = dot(b_mat, dstate_low) * to_last
        du = jnp.concatenate(parts, axis=1) + du_carry
        y_in = dot(c_mat, state_in) * entering
        dy_in = low(dy * entering)
        x_out = low(xd * to_last)
        d_c = dot(low(dprod), b_mat, TN) + dot(dy_in, state_in, NT)
        d_b = dot(low(dprod), c_mat) + dot(x_out, dstate_low, NT)
        moved_by = [low(dy * y_in), low(xd * du_carry)]
        across = jnp.sum(dstate_ref[...] * state_in.astype(F32), axis=0, keepdims=True) * grow
        if two_way:
            back_state = state_ref[...]
            back_low = low(back_state)
            dback_low = dback_scr[c]
            leaving = split_dot(beyond, by_ecum)
            from_first = split_dot(within * prefix_column(prefix, c), by_ecum)
            du_back = dot(b_mat, dback_low) * from_first
            du = du + du_back
            y_back = dot(c_mat, back_low) * leaving
            x_back = low(xd * from_first)
            d_c = d_c + dot(low(dy * leaving), back_low, NT)
            d_b = d_b + dot(x_back, dback_low, NT)
            moved_by = moved_by + [low(dy * y_back), low(xd * du_back)]
            across = across + grow * jnp.sum(
                dback_low.astype(F32) * back_state, axis=0, keepdims=True
            )
            state_ref[...] = back_state * grow + dot(b_mat, x_back, TN)
        dstate_ref[...] = dstate_ref[...] * grow + dot(c_mat, dy_in, TN)
        d_bc = jnp.concatenate([d_b, d_c], axis=1)
        summed = dot(sum_all if two_way else sum_all[:, : 2 * Q], jnp.concatenate(moved_by, axis=0))
        qk = dot(low(summed), collect)
        direct = dot(low(x * du), collect)
        across8 = low_pair_dot(jnp.broadcast_to(across, (8, width)), collect)
        d_cols = jnp.concatenate([direct, qk + across8[0:1]], axis=1)
        if more:
            d_bc = d_bc + refs[0][rows_of(c), :]
            d_cols = d_cols + refs[1][rows_of(c), :]
        gact_ref[rows_of(c), :] = d_bc
        gcols_ref[rows_of(c), :] = d_cols

        dconv = (du * step_wide + skip * dy) * slope_scr[rows_of(c), :]
        shifted = shifted_rows(x_ref, c)
        both = jnp.concatenate([dconv, next_scr[...]], axis=0)
        gx = taps[3:4] * dconv
        gsum_ref[3:4, :] += jnp.sum(dconv * shifted[0], axis=0, keepdims=True)
        for j in (1, 2, 3):
            gx = gx + taps[3 - j : 4 - j] * pltpu.roll(both, Q + 8 - j, 0)[:Q]
            gsum_ref[3 - j : 4 - j, :] += jnp.sum(dconv * shifted[j], axis=0, keepdims=True)
        gx_ref[rows_of(c), :] = low(gx)
        next_scr[...] = dconv[0:8]
        return 0

    if chunks > anti:
        lax.fori_loop(0, chunks - anti, lambda i, _: chunk_body(chunks - 1 - i, False), 0, unroll=4)
    lax.fori_loop(0, anti, lambda i, _: chunk_body(anti - 1 - i, True), 0, unroll=4)


def scan_backward(prefix, x_pre, grad_ssd, taps, skip, cols, rows, act, group, place, places, gx, before):
    length, channels = x_pre.shape
    chunks = length // Q
    anti = min(MAX_PREFIX // Q, chunks)
    wide = pl.BlockSpec((length, CG), lambda i: (0, group))
    given = [prefix, x_pre, grad_ssd, taps, skip, cols, rows, act]
    in_specs = [
        pl.BlockSpec(memory_space=pltpu.SMEM),
        wide,
        wide,
        pl.BlockSpec((4, CG), lambda i: (0, group)),
        pl.BlockSpec((1, CG), lambda i: (0, group)),
        pl.BlockSpec((length, 128), lambda i: (0, 0)),
        pl.BlockSpec((128, length), lambda i: (0, 0)),
        pl.BlockSpec((length, 2 * N), lambda i: (0, 0)),
    ]
    aliases = {}
    if before is not None:
        given += list(before)
        in_specs += [
            pl.BlockSpec((length, 2 * N), lambda i: (0, 0)),
            pl.BlockSpec((length, 256), lambda i: (0, 0)),
        ]
        aliases = {len(given) - 2: 1, len(given) - 1: 2}
    if gx is not None:
        aliases[len(given)] = 0
        given.append(gx)
        in_specs.append(pl.BlockSpec(memory_space=pl.ANY))
    return pl.pallas_call(
        functools.partial(backward_kernel, channels // P_SIZE, group * HG, before is not None),
        grid=(1,),
        in_specs=in_specs,
        out_specs=[
            pl.BlockSpec((length, CG), lambda i: (0, place)),
            pl.BlockSpec((length, 2 * N), lambda i: (0, 0)),
            pl.BlockSpec((length, 256), lambda i: (0, 0)),
            pl.BlockSpec((1, HG, length), lambda i: (0, 0, 0)),
            pl.BlockSpec((8, CG), lambda i: (0, 0)),
        ],
        out_shape=(
            jax.ShapeDtypeStruct((length, places * CG), BF16),
            jax.ShapeDtypeStruct((length, 2 * N), F32),
            jax.ShapeDtypeStruct((length, 256), F32),
            jax.ShapeDtypeStruct((1, HG, length), F32),
            jax.ShapeDtypeStruct((8, CG), F32),
        ),
        input_output_aliases=aliases,
        scratch_shapes=[
            pltpu.VMEM((length, CG), F32),
            pltpu.VMEM((length, CG), F32),
            pltpu.VMEM((chunks, N, CG), BF16),
            pltpu.VMEM((anti + 1, N, CG), BF16),
            pltpu.VMEM((N, CG), F32),
            pltpu.VMEM((N, CG), F32),
            pltpu.VMEM((8, CG), F32),
        ],
        compiler_params=pltpu.CompilerParams(vmem_limit_bytes=40 * MIB),
        cost_estimate=NO_COST,
        name="scan_backward",
    )(*given)


TILE = 128


def block_of(lanes_ref, j):
    return pl.ds(pl.multiple_of(lanes_ref[j] * 128, 128), 128)


def place_kernel(normalize, count, tiles, lanes_ref, slots_ref, *refs):
    sources, by_ref, out_ref = refs[:count], refs[count], refs[count + 1]
    width = out_ref.shape[1]
    for k in range(count):

        @pl.when(pl.program_id(0) // tiles == k)
        def _(ref=sources[k]):
            if normalize:
                wide = ref[...].astype(F32)
                inv = lax.rsqrt(jnp.sum(wide * wide, axis=-1, keepdims=True) / width + EPSILON)
            else:
                inv = by_ref[...]
            for j in range(width // 128):
                there = block_of(lanes_ref, j)
                v = ref[:, there].astype(F32) * inv
                if normalize:
                    v = v * by_ref[:, there]
                out_ref[:, j * 128 : j * 128 + 128] = low(v)


def place_tokens(lanes, slots, sources, by, normalize):
    tokens, width = sources[0].shape
    count, tiles = len(sources), tokens // TILE

    def source(k):
        return pl.BlockSpec((TILE, width), lambda i, a, s: (jnp.clip(i - k * tiles, 0, tiles - 1), 0))

    def placed(i, a, s):
        return (s[i // tiles] * tiles + i % tiles, 0)

    by_spec = pl.BlockSpec((1, width), lambda i, a, s: (0, 0)) if normalize else pl.BlockSpec((TILE, 1), placed)
    return pl.pallas_call(
        functools.partial(place_kernel, normalize, count, tiles),
        grid_spec=pltpu.PrefetchScalarGridSpec(
            num_scalar_prefetch=2,
            grid=(count * tiles,),
            in_specs=[source(k) for k in range(count)] + [by_spec],
            out_specs=pl.BlockSpec((TILE, width), placed),
        ),
        out_shape=jax.ShapeDtypeStruct((tokens * count, width), BF16),
        compiler_params=pltpu.CompilerParams(vmem_limit_bytes=32 * MIB),
        cost_estimate=NO_COST,
        name="place_tokens",
    )(lanes, slots, *sources, by)


def half_sum(refs, j, per_half):
    here = slice((j % per_half) * 128, (j % per_half) * 128 + 128)
    side = refs[: len(refs) // 2] if j < per_half else refs[len(refs) // 2 :]
    total = side[0][:, here].astype(F32)
    for ref in side[1:]:
        total = total + ref[:, here].astype(F32)
    return total


def mixed_kernel(lanes_ref, slots_ref, hidden_ref, *refs):
    out_ref = refs[-1]
    blocks = hidden_ref.shape[1] // 128
    for j in range(blocks):
        there = block_of(lanes_ref, j)
        out_ref[:, there] = hidden_ref[:, there].astype(F32) + half_sum(refs[:-1], j, blocks // 2)


def finish_kernel(lanes_ref, slots_ref, hidden_ref, cot_ref, gain_ref, *refs):
    out_ref = refs[-1]
    width = hidden_ref.shape[1]
    blocks = width // 128
    wide = hidden_ref[...].astype(F32)
    inv = lax.rsqrt(jnp.sum(wide * wide, axis=-1, keepdims=True) / width + EPSILON)
    total = jnp.zeros((TILE, 128), F32)
    for j in range(blocks):
        there = block_of(lanes_ref, j)
        scaled = half_sum(refs[:-1], j, blocks // 2) * gain_ref[:, there]
        total = total + scaled * hidden_ref[:, there].astype(F32)
        out_ref[:, there] = scaled
    coef = inv * inv * inv * (jnp.sum(total, axis=-1, keepdims=True) / width)
    out_ref[...] = inv * out_ref[...] - wide * coef + cot_ref[...].astype(F32)


def own_rows(kernel, name, lanes, slots, hidden, more, gain, halves):
    tokens, width = hidden.shape
    tiles = tokens // TILE
    tile = pl.BlockSpec((TILE, width), lambda i, a, s: (i, 0))
    given, specs = [hidden, *more], [tile] * (1 + len(more))
    if gain is not None:
        given.append(gain)
        specs.append(pl.BlockSpec((1, width), lambda i, a, s: (0, 0)))
    for half in halves:
        for array, whole in half:
            given.append(array)
            if whole:
                specs.append(pl.BlockSpec((TILE, width // 2), lambda i, a, s: (s[0] * tiles + i, 0)))
            else:
                specs.append(pl.BlockSpec((TILE, width // 2), lambda i, a, s: (i, 0)))
    return pl.pallas_call(
        kernel,
        grid_spec=pltpu.PrefetchScalarGridSpec(
            num_scalar_prefetch=2, grid=(tiles,), in_specs=specs, out_specs=tile
        ),
        out_shape=jax.ShapeDtypeStruct((tokens, width), F32),
        compiler_params=pltpu.CompilerParams(vmem_limit_bytes=40 * MIB),
        cost_estimate=NO_COST,
        name=name,
    )(lanes, slots, *given)


def post_kernel(rest_ref, taps_ref, decay_ref, bias_ref, *refs):
    gbc_ref, gtaps_ref, ghead_ref, next_scr = refs[-4:]
    gact_ref, gcols_ref, grows = refs[0], refs[1], refs[2:-4]
    length, heads = rest_ref.shape[0], decay_ref.shape[1]
    chunks = length // Q
    taps = taps_ref[...]
    gtaps_ref[...] = jnp.zeros_like(gtaps_ref)
    ghead_ref[...] = jnp.zeros_like(ghead_ref)
    next_scr[...] = jnp.zeros_like(next_scr)
    filler = jnp.zeros((1, 128 - heads), F32)
    growth = -jnp.exp(jnp.concatenate([decay_ref[...], filler], axis=1))
    bias = jnp.concatenate([bias_ref[...], filler], axis=1)

    def body(i, _):
        c = chunks - 1 - i
        shifted = shifted_rows(rest_ref, c, 2 * N)
        conv = conv_of(shifted, taps)
        s = sig(conv)
        dconv = gact_ref[rows_of(c), :] * (s + conv * s * (1.0 - s))
        both = jnp.concatenate([dconv, next_scr[...]], axis=0)
        g = taps[3:4] * dconv
        gtaps_ref[3:4, :] += jnp.sum(dconv * shifted[0], axis=0, keepdims=True)
        for j in (1, 2, 3):
            g = g + taps[3 - j : 4 - j] * pltpu.roll(both, Q + 8 - j, 0)[:Q]
            gtaps_ref[3 - j : 4 - j, :] += jnp.sum(dconv * shifted[j], axis=0, keepdims=True)
        gbc_ref[rows_of(c), 0 : 2 * N] = low(g)
        next_scr[...] = dconv[0:8]

        direct, moved = gcols_ref[rows_of(c), 0:128], gcols_ref[rows_of(c), 128:256]
        inner = [ref[0, :, rows_of(c)] for ref in grows]
        inner.append(jnp.zeros((128 - heads, Q), F32))
        moved = moved + jnp.concatenate(inner, axis=0).T
        raw = rest_ref[rows_of(c), 2 * N :] + bias
        step = jnp.maximum(raw, 0.0) + jnp.log(1.0 + jnp.exp(-jnp.abs(raw)))
        gdt = (direct + moved * growth) * sig(raw)
        gbc_ref[rows_of(c), 2 * N :] = low(gdt[:, 0:heads])
        ghead_ref[0:1, :] += jnp.sum(moved * growth * step, axis=0, keepdims=True)
        ghead_ref[1:2, :] += jnp.sum(gdt, axis=0, keepdims=True)
        return 0

    lax.fori_loop(0, chunks, body, 0, unroll=4)


def post(rest_pre, bc_taps, log_decay, dt_bias, grad_act, gcols, grows):
    length, heads = rest_pre.shape[0], log_decay.shape[0]
    return pl.pallas_call(
        post_kernel,
        out_shape=(
            jax.ShapeDtypeStruct((length, 2 * N + heads), BF16),
            jax.ShapeDtypeStruct((8, 2 * N), F32),
            jax.ShapeDtypeStruct((8, 128), F32),
        ),
        scratch_shapes=[pltpu.VMEM((8, 2 * N), F32)],
        compiler_params=pltpu.CompilerParams(vmem_limit_bytes=40 * MIB),
        cost_estimate=NO_COST,
        name="post",
    )(rest_pre, bc_taps, log_decay[None], dt_bias[None], grad_act, gcols, *grows)


def snake(devices):
    half = devices // 4
    return [z * 2 for z in range(half)] + [z * 2 + 1 for z in reversed(range(half))]


def chip_groups(devices):
    return [[chip * 2 + core for chip in snake(devices)] for core in (0, 1)]


def other_core(v, devices):
    return lax.ppermute(v, "fsdp", [(i, i ^ 1) for i in range(devices)])


def other_half(v):
    return lax.ppermute(v, "tp", [(0, 1), (1, 0)])


def tie(first, second):
    return lax.optimization_barrier((first, second))


def gather(v, devices):
    return lax.all_gather(v, "fsdp", axis=0, tiled=True, axis_index_groups=chip_groups(devices))


def doubling_gather(v, devices):
    me = lax.axis_index("fsdp")
    bit = 1
    while bit < devices:
        came = lax.ppermute(v, "fsdp", [(i, i ^ bit) for i in range(devices)])
        mine_first = me & bit == 0
        v = jnp.concatenate([jnp.where(mine_first, v, came), jnp.where(mine_first, came, v)], axis=0)
        bit *= 2
    return v


def scatter(v, devices):
    return lax.psum_scatter(
        v, "fsdp", scatter_dimension=0, tiled=True, axis_index_groups=chip_groups(devices)
    )


def on_device(
    hidden,
    cotangent,
    prefix,
    input_norm_gain,
    z_weight,
    x_weight,
    bc_weight,
    dt_weight,
    x_conv,
    bc_conv,
    log_decay,
    dt_bias,
    skip_gain,
    gate_gain,
    out_weight,
):
    fsdp = lax.axis_size("fsdp")
    tp = lax.axis_size("tp")
    own_tokens, width = hidden.shape
    heads = log_decay.shape[0]
    channels = heads * P_SIZE
    all_channels = channels * tp
    groups = channels // CG
    taps_own = x_conv.shape[2]
    rows = width // fsdp
    ring = fsdp // 2
    half_width = width // 2

    order = snake(fsdp)
    core = lax.axis_index("fsdp") % 2
    line = jnp.array(order, jnp.int32)
    blocks = jnp.concatenate([line * 2 + core, line * 2 + 1 - core])
    direct = rows % 128 == 0
    per = max(rows // 128, 1)
    if direct:
        lanes = (blocks[:, None] * per + jnp.arange(per)[None]).reshape(-1)
    else:
        lanes = jnp.arange(width // 128)
    lanes = lanes.astype(jnp.int32)

    def to_cores(v):
        zero = jnp.stack([v[2 * chip] for chip in order])
        one = jnp.stack([v[2 * chip + 1] for chip in order])
        return jnp.where(core == 0, zero, one), jnp.where(core == 0, one, zero)

    def to_ring(v):
        return v if direct else v.reshape(-1, fsdp, rows)[:, blocks].reshape(v.shape)

    def from_ring(v):
        if direct:
            return v
        return v.reshape(-1, fsdp, rows)[:, jnp.argsort(blocks)].reshape(v.shape)

    small = jnp.concatenate(
        [input_norm_gain.reshape(-1), x_conv.reshape(-1), bc_conv.reshape(-1), gate_gain.reshape(-1)]
    )
    sizes = [input_norm_gain.size, x_conv.size, bc_conv.size, gate_gain.size]
    cuts = [0]
    for size in sizes:
        cuts.append(cuts[-1] + size)
    small_all = doubling_gather(jnp.pad(small, (0, -small.size % 128))[None], fsdp)
    payload = jnp.concatenate([x_weight, bc_weight, dt_weight, dt_weight, dt_weight], axis=1)
    payload = jnp.pad(payload, ((0, 0), (0, 128 - 3 * heads)))

    if tp == 2:
        mine = lax.axis_index("tp").astype(jnp.int32)
        slots = jnp.stack([mine, 1 - mine])
        hidden_other = other_half(hidden)
        cot_given, hidden_other = tie(cotangent, hidden_other)
        hidden_parts = [hidden, hidden_other]
        cot_parts = [cotangent, other_half(cot_given)]
    else:
        slots = jnp.zeros((2,), jnp.int32)
        hidden_parts = [lax.all_gather(hidden, "tp", axis=0, tiled=True)]
        cot_parts = [lax.all_gather(cotangent, "tp", axis=0, tiled=True)]
    hidden_parts = [to_ring(v) for v in hidden_parts]
    cot_parts = [to_ring(v) for v in cot_parts]

    norm_gain = small_all[:, cuts[0] : cuts[1]].reshape(1, -1).astype(F32)
    x_taps = small_all[:, cuts[1] : cuts[2]].reshape(fsdp, heads, 4, taps_own)
    x_taps = jnp.transpose(x_taps, (2, 1, 0, 3)).reshape(4, channels).astype(F32)
    bc_taps = small_all[:, cuts[2] : cuts[3]].reshape(fsdp, 4, -1)
    bc_taps = jnp.transpose(bc_taps, (1, 0, 2)).reshape(4, 2 * N).astype(F32)
    gain = small_all[:, cuts[3] : cuts[4]].reshape(fsdp, heads, -1)
    gain = jnp.transpose(gain, (1, 0, 2)).reshape(1, channels).astype(F32)
    skip = jnp.repeat(skip_gain, P_SIZE)[None]
    hidden_parts[-1], (norm_gain, x_taps, bc_taps, gain, skip) = tie(
        hidden_parts[-1], (norm_gain, x_taps, bc_taps, gain, skip)
    )

    x_own = gather(payload, fsdp)
    z_own = gather(z_weight, fsdp)
    out_own = gather(out_weight.T, fsdp)
    x_own, hidden_parts[-1] = tie(x_own, hidden_parts[-1])
    x_other = other_core(x_own, fsdp)

    norm_gain = to_ring(norm_gain)
    normed = place_tokens(lanes, slots, hidden_parts, norm_gain, True)
    na, nb = normed[:, :half_width], normed[:, half_width:]
    few = slice(channels, channels + 2 * N + 128)
    rest_pre = dot(na, x_own[:, few]) + dot(nb, x_other[:, few])
    rest = slice(channels, channels + 2 * N + heads)
    rest_own, rest_other = x_own[:, rest], x_other[:, rest]
    act, cols, head_rows = prep(rest_pre, bc_taps, log_decay, dt_bias)
    x_pre = low(dot(na, x_own[:, :channels]) + dot(nb, x_other[:, :channels]))
    ssd_out = None
    for g in range(groups):
        ssd_out = scan_forward(prefix, x_pre, x_taps, skip, cols, head_rows, act, g, ssd_out)
    (z_own, cot_parts[-1]), ssd_out = tie((z_own, cot_parts[-1]), ssd_out)
    z_other = other_core(z_own, fsdp)

    gate_pre = dot(na, z_own) + dot(nb, z_other)
    gated = ssd_out.astype(F32) * (gate_pre * sig(gate_pre))
    square_sum = lax.psum(jnp.sum(gated * gated, axis=-1), "tp")
    gate_low = low(gate_pre)
    scaled_out = low(gated * gain)
    out_own, scaled_out = tie(out_own, scaled_out)
    out_other = other_core(out_own, fsdp)

    inv_gate = lax.rsqrt(square_sum / all_channels + EPSILON)[:, None]
    cot_rel = place_tokens(lanes, slots, cot_parts, inv_gate, False)
    ca, cb = cot_rel[:, :half_width], cot_rel[:, half_width:]
    gout_came = other_core(low(dot(cb, scaled_out, TN)), fsdp)

    branch, along = [], 0.0
    for cot_half, out_half in ((ca, out_own), (cb, out_other)):
        v = dot(scaled_out, out_half, NT)
        along = along + jnp.sum(v * cot_half.astype(F32), axis=-1)
        branch.append(low(v * inv_gate))
    along = lax.psum(along, "tp")
    coef = inv_gate * inv_gate * (along / all_channels)[:, None]
    scaled_out, coef = tie(scaled_out, coef)
    gout_sum = low(dot(ca, scaled_out, TN) + gout_came.astype(F32))
    (coef, branch), gout_sum = tie((coef, branch), gout_sum)
    grad_out = scatter(gout_sum, fsdp)

    def to_own_tokens(v):
        if tp == 2:
            leaving = lax.dynamic_slice_in_dim(v, (1 - mine) * own_tokens, own_tokens, 0)
            return [(v, True), (other_half(leaving), False)]
        return [(lax.psum_scatter(v, "tp", scatter_dimension=0, tiled=True), False)]

    branch_parts = [to_own_tokens(v) for v in branch]
    kinds = [[whole for _, whole in half] for half in branch_parts]
    branch_parts = [[v for v, _ in half] for half in branch_parts]

    scaled = dot(ca, out_own) + dot(cb, out_other)
    z = gate_low.astype(F32)
    s = sig(z)
    gate_act = z * s
    y = ssd_out.astype(F32)
    gated = y * gate_act
    ggain = jnp.sum(scaled * gated, axis=0)
    grad_gated = gain * scaled - gated * coef
    ggate = low(grad_gated * y * (s + gate_act * (1.0 - s)))
    dy = low(grad_gated * gate_act)
    gz_came = other_core(low(dot(nb, ggate, TN)), fsdp)
    z_parts = [dot(ggate, z_own, NT), dot(ggate, z_other, NT)]
    na, z_parts = tie(na, z_parts)
    gz_sum = low(dot(na, ggate, TN) + gz_came.astype(F32))
    dy, gz_sum = tie(dy, gz_sum)
    grad_z = scatter(gz_sum, fsdp)

    grows, gsums = [], []
    first = groups // 2
    before = None

    def back_through(start, stop, dy, before):
        gx = None
        for g in range(start, stop):
            if g == 1:
                dy, branch_parts[0] = tie(dy, branch_parts[0])
            gx, gact, gcol, grow, gsum = scan_backward(
                prefix, x_pre, dy, x_taps, skip, cols, head_rows, act, g, g - start, stop - start, gx, before
            )
            before = (gact, gcol)
            grows.append(grow)
            gsums.append(gsum)
        return gx, before

    grad_x = []
    if first:
        gx, before = back_through(0, first, dy, before)
        gx, branch_parts[1] = tie(gx, branch_parts[1])
        came = other_core(low(dot(nb, gx, TN)), fsdp)
        z_parts = [
            v + dot(gx, half[:, : first * CG], NT) for v, half in zip(z_parts, (x_own, x_other))
        ]
        na, z_parts = tie(na, z_parts)
        total = low(dot(na, gx, TN) + came.astype(F32))
        dy, (total, grad_out) = tie(dy, (total, grad_out))
        grad_x.append(scatter(total, fsdp))
    gx, before = back_through(first, groups, dy, before)
    gx, (grad_z, *grad_x) = tie(gx, (grad_z, *grad_x))
    gx_other = low(dot(nb, gx, TN))
    came = other_core(gx_other, fsdp)
    before, gx_other = tie(before, gx_other)
    grest, gbc_taps, ghead = post(rest_pre, bc_taps, log_decay, dt_bias, before[0], before[1], grows)
    na, grest = tie(na, grest)
    gx_sum = low(dot(na, gx, TN) + came.astype(F32))
    (gx, grest, ghead), gx_sum = tie((gx, grest, ghead), gx_sum)
    grad_x = list(grad_x)
    grad_x.append(scatter(gx_sum, fsdp))

    gsum = jnp.concatenate(gsums, axis=1)
    gx_taps = jnp.transpose(gsum[0:4].reshape(4, heads, fsdp, taps_own), (2, 1, 0, 3))
    g_taps = jnp.transpose(gbc_taps[0:4].reshape(4, fsdp, -1), (1, 0, 2))
    g_gain = jnp.transpose(ggain.reshape(heads, fsdp, -1), (1, 0, 2))
    g_skip = jnp.sum(gsum[4].reshape(heads, P_SIZE), axis=-1)
    per_head = jnp.concatenate([ghead[0, :heads], ghead[1, :heads], g_skip])
    slices = jnp.concatenate(
        [
            g_taps.reshape(fsdp, -1),
            gx_taps.reshape(fsdp, -1),
            g_gain.reshape(fsdp, -1),
            jnp.broadcast_to(per_head[None], (fsdp, per_head.size)),
        ],
        axis=1,
    )
    size = slices.shape[1]
    lone = -(-size // rows)
    lines_own, lines_other = [
        jnp.pad(v, ((0, 0), (0, lone * rows - size))).reshape(half_width, lone) for v in to_cores(slices)
    ]
    rest_came = other_core(jnp.concatenate([dot(nb, grest, TN), lines_other], axis=1), fsdp)

    def part_of(v, x_half, r_half):
        return low(v + dot(gx, x_half[:, first * CG : channels], NT) + dot(grest, r_half, NT))

    part_sums = [to_own_tokens(part_of(z_parts[0], x_own, rest_own))]
    kinds_part = [whole for _, whole in part_sums[0]]
    gx, first_part = tie(gx, part_sums[0][0][0])
    arrived = [first_part] + [v for v, _ in part_sums[0][1:]]
    second = part_of(z_parts[1], x_other, rest_other)
    part_sums.append(to_own_tokens(second))
    rest_sum = jnp.concatenate([dot(na, grest, TN), lines_own], axis=1) + rest_came
    rest_sum, arrived, second, grad_x[-1] = lax.optimization_barrier(
        (rest_sum, arrived, second, grad_x[-1])
    )
    part_sums[0] = list(zip(arrived, kinds_part))
    mine_rest = scatter(rest_sum, fsdp)

    mixed = from_ring(
        own_rows(
            mixed_kernel, "add_branch", lanes, slots, to_ring(hidden), [], None,
            [list(zip(half, kind)) for half, kind in zip(branch_parts, kinds)],
        )
    )
    grad_hidden = from_ring(
        own_rows(finish_kernel, "finish", lanes, slots, to_ring(hidden), [to_ring(cotangent)], norm_gain, part_sums)
    )

    grad_z, grad_out = grad_z.astype(F32), grad_out.astype(F32).T
    grad_x = jnp.concatenate(grad_x, axis=1).astype(F32)
    grad_bc, grad_dt = mine_rest[:, : 2 * N], mine_rest[:, 2 * N : 2 * N + heads]
    lines = mine_rest[:, 2 * N + heads :].reshape(-1)
    grad_gain = sum(
        jnp.sum(w.astype(F32) * g, axis=1)
        for w, g in ((z_weight, grad_z), (x_weight, grad_x), (bc_weight, grad_bc), (dt_weight, grad_dt))
    ) / input_norm_gain.astype(F32)
    n_taps = bc_conv.size
    together = jnp.concatenate([grad_bc.reshape(-1), grad_gain, lines[:n_taps]])
    together = together + other_half(together) if tp == 2 else lax.psum(together, "tp")
    bc_size = rows * 2 * N
    at = [n_taps]
    for size in (x_conv.size, gate_gain.size, heads, heads, heads):
        at.append(at[-1] + size)
    return (
        mixed,
        grad_hidden,
        together[bc_size : bc_size + rows],
        grad_z,
        grad_x,
        together[:bc_size].reshape(rows, 2 * N),
        grad_dt,
        lines[at[0] : at[1]].reshape(x_conv.shape),
        together[bc_size + rows :].reshape(bc_conv.shape),
        lines[at[2] : at[3]],
        lines[at[3] : at[4]],
        lines[at[4] : at[5]],
        lines[at[1] : at[2]].reshape(gate_gain.shape),
        grad_out,
    )


def solution(mesh):
    both = P(("fsdp", "tp"), None)
    split = P("fsdp", "tp")
    ins = (
        both, both, P("fsdp"), P("fsdp"), split, split, P("fsdp", None), split, P("tp", None, "fsdp"),
        P(None, "fsdp"), P("tp"), P("tp"), P("tp"), P("tp", "fsdp"), P("tp", "fsdp"),
    )
    outs = (
        both, both, P("fsdp"), split, split, P("fsdp", None), split, P("tp", None, "fsdp"),
        P(None, "fsdp"), P("tp"), P("tp"), P("tp"), P("tp", "fsdp"), P("tp", "fsdp"),
    )
    return jax.shard_map(on_device, mesh=mesh, in_specs=ins, out_specs=outs, check_vma=False)
```

```python
import functools

import jax
import jax.numpy as jnp
from jax import lax
from jax.experimental import pallas as pl
from jax.experimental.pallas import tpu as pltpu
from jax.sharding import PartitionSpec as P

P_SIZE = 64
N = 128
Q = 128
HG = 8
CG = HG * P_SIZE
MAX_PREFIX = 512
EPSILON = 1e-05
F32 = jnp.float32
BF16 = jnp.bfloat16
NEG = -1e30
NN = ((1,), (0,))
NT = ((1,), (1,))
TN = ((0,), (0,))
MIB = 1024 * 1024
NO_COST = pl.CostEstimate(flops=0, bytes_accessed=0, transcendentals=0)


def dot(a, b, dims=NN):
    return lax.dot_general(a, b, (dims, ((), ())), preferred_element_type=F32)


def low(v):
    return v.astype(BF16)


def split_dot(v, e):
    hi = low(v)
    rest = low(v - hi.astype(F32))
    return dot(jnp.concatenate([hi, rest], axis=1), e)


def low_pair_dot(v, e):
    hi = low(v)
    return dot(hi, e) + dot(low(v - hi.astype(F32)), e)


def three_dot(e, v):
    hi = low(v)
    rest = v - hi.astype(F32)
    mid = low(rest)
    return dot(e, hi) + (dot(e, mid) + dot(e, low(rest - mid.astype(F32))))


def iota(shape, dim):
    return lax.broadcasted_iota(jnp.int32, shape, dim)


def sig(v):
    return 0.5 + 0.5 * jnp.tanh(0.5 * v)


def rows_of(c):
    return pl.ds(pl.multiple_of(c * Q, Q), Q)


def shifted_rows(x_ref, c, width=None):
    lanes = slice(0, width)
    cur = x_ref[rows_of(c), lanes].astype(F32)
    start = pl.multiple_of(jnp.maximum(c * Q - 16, 0), 16)
    before = x_ref[pl.ds(start, 16), lanes].astype(F32)[8:]
    before = jnp.where(c > 0, before, 0.0)
    both = jnp.concatenate([before, cur], axis=0)
    return [cur] + [pltpu.roll(both, j, 0)[8:] for j in (1, 2, 3)]


def conv_of(shifted, taps):
    total = taps[3:4] * shifted[0]
    for j in (1, 2, 3):
        total = total + taps[3 - j : 4 - j] * shifted[j]
    return total


def spread_matrix(start, width):
    return jnp.where(
        iota((256, width), 1) // P_SIZE + start == iota((256, width), 0) % 128, 1.0, 0.0
    ).astype(BF16)


def gather_matrix(start, width):
    return jnp.where(
        iota((width, 128), 0) // P_SIZE + start == iota((width, 128), 1), 1.0, 0.0
    ).astype(BF16)


def prep_kernel(rest_ref, taps_ref, decay_ref, bias_ref, act_ref, cols_ref, rows_ref):
    heads = decay_ref.shape[1]
    length = rest_ref.shape[0]
    taps = taps_ref[...]
    tri = jnp.where(iota((Q, Q), 0) >= iota((Q, Q), 1), 1.0, 0.0).astype(BF16)
    lane = iota((1, 128), 1)
    filler = jnp.zeros((1, 128 - 3 * heads), F32)
    decay = jnp.concatenate([decay_ref[...]] * 3 + [filler], axis=1)
    bias = jnp.concatenate([bias_ref[...]] * 3 + [filler], axis=1)
    growth = -jnp.exp(decay)

    def body(c, _):
        conv = conv_of(shifted_rows(rest_ref, c, 2 * N), taps)
        act_ref[rows_of(c), :] = low(conv * sig(conv))
        raw = rest_ref[rows_of(c), 2 * N :] + bias
        raw = jnp.where(lane < 3 * heads, raw, 0.0)
        step = jnp.maximum(raw, 0.0) + jnp.log(1.0 + jnp.exp(-jnp.abs(raw)))
        rate = growth * step
        cum = three_dot(tri, rate)
        packed = jnp.where(lane < heads, cum, jnp.where(lane < 2 * heads, cum - rate, step))
        packed = jnp.where(lane < 3 * heads, packed, 0.0)
        cols_ref[rows_of(c), :] = packed
        rows_ref[:, rows_of(c)] = packed.T
        return 0

    lax.fori_loop(0, length // Q, body, 0, unroll=4)


def prep(rest_pre, bc_taps, log_decay, dt_bias):
    length = rest_pre.shape[0]
    return pl.pallas_call(
        prep_kernel,
        out_shape=(
            jax.ShapeDtypeStruct((length, 2 * N), BF16),
            jax.ShapeDtypeStruct((length, 128), F32),
            jax.ShapeDtypeStruct((128, length), F32),
        ),
        compiler_params=pltpu.CompilerParams(vmem_limit_bytes=32 * MIB),
        cost_estimate=NO_COST,
        name="prep",
    )(rest_pre, bc_taps, log_decay[None], dt_bias[None])


def prefix_column(prefix, c):
    return jnp.where(iota((Q, 1), 0) + c * Q < prefix, 1.0, 0.0).astype(F32)


def growths(part, heads):
    lane = iota((1, 128), 1)
    used = lane < 2 * heads
    tail = part[Q - 8 :]
    last = jnp.where(lane < heads, tail, pltpu.roll(tail, heads, 1))[7:8]
    within = jnp.where(used, jnp.exp(jnp.where(used, part, 0.0)), 0.0)
    beyond = jnp.where(used, jnp.exp(jnp.where(used, last - part, 0.0)), 0.0)
    return within, beyond


def forward_kernel(
    heads, first, prefix_ref, x_ref, taps_ref, skip_ref, cols_ref, rows_ref, act_ref, *refs
):
    out_ref, xd_ref, kept_ref, back_ref, state_ref = refs[-5:]
    length, width = x_ref.shape
    chunks = length // Q
    anti = min(MAX_PREFIX // Q, chunks)
    prefix = prefix_ref[0]
    taps = taps_ref[...].astype(F32)
    skip = skip_ref[...]
    by_cum = spread_matrix(first, width)
    by_ecum = spread_matrix(heads + first, width)
    by_step = spread_matrix(2 * heads + first, width)
    lane_low = iota((1, 128), 1) < P_SIZE

    def stage_a(c, _):
        conv = conv_of(shifted_rows(x_ref, c), taps)
        x = conv * sig(conv)
        xd_ref[rows_of(c), :] = low(x * split_dot(cols_ref[rows_of(c), :], by_step))
        kept_ref[rows_of(c), :] = x * skip
        return 0

    lax.fori_loop(0, chunks, stage_a, 0, unroll=4)

    state_ref[...] = jnp.zeros_like(state_ref)
    back_ref[anti - 1] = jnp.zeros_like(back_ref[anti - 1])
    for c in range(anti - 1, 0, -1):
        within, _ = growths(cols_ref[rows_of(c), :], heads)
        weight = split_dot(within * prefix_column(prefix, c), by_ecum)
        grow = split_dot(within[Q - 8 :], by_cum)[7:8]
        b_mat = act_ref[rows_of(c), 0:N]
        xw = low(xd_ref[rows_of(c), :].astype(F32) * weight)
        state_ref[...] = state_ref[...] * grow + dot(b_mat, xw, TN)
        back_ref[c - 1] = low(state_ref[...])

    state_ref[...] = jnp.zeros_like(state_ref)
    causal_bias = jnp.where(iota((Q, Q), 1) <= iota((Q, Q), 0), 0.0, NEG).astype(F32)

    def chunk_body(c, two_way):
        b_mat = act_ref[rows_of(c), 0:N]
        c_mat = act_ref[rows_of(c), N : 2 * N]
        products = dot(c_mat, b_mat, NT)
        part = cols_ref[rows_of(c), :]
        within, beyond = growths(part, heads)
        entering = split_dot(within, by_cum)
        total = kept_ref[rows_of(c), :] + dot(c_mat, low(state_ref[...])) * entering
        if two_way:
            leaving = split_dot(beyond, by_ecum)
            total = total + dot(c_mat, back_ref[c]) * leaving
            anti_bias = jnp.where(
                (iota((Q, Q), 1) > iota((Q, Q), 0)) & (iota((Q, Q), 1) + c * Q < prefix), 0.0, NEG
            ).astype(F32)
        xd = xd_ref[rows_of(c), :]
        rows = rows_ref[first : first + HG, rows_of(c)]
        erows = rows_ref[heads + first : heads + first + HG, rows_of(c)]
        parts = []
        for pair in range(HG // 2):
            mixes = []
            for h in (2 * pair, 2 * pair + 1):
                e = part[:, first + h : first + h + 1] - rows[h : h + 1] + causal_bias
                if two_way:
                    at = heads + first + h
                    back = erows[h : h + 1] - part[:, at : at + 1] + anti_bias
                    e = jnp.maximum(e, back)
                mixes.append(low(jnp.exp(e) * products))
            x_pair = xd[:, pair * 128 : pair * 128 + 128]
            zero = jnp.zeros_like(x_pair)
            blocks = jnp.concatenate(
                [jnp.where(lane_low, x_pair, zero), jnp.where(lane_low, zero, x_pair)], axis=0
            )
            parts.append(dot(jnp.concatenate(mixes, axis=1), blocks))
        out_ref[rows_of(c), :] = (total + jnp.concatenate(parts, axis=1)).astype(out_ref.dtype)
        weight = split_dot(beyond, by_cum)
        xw = low(xd.astype(F32) * weight)
        state_ref[...] = state_ref[...] * entering[Q - 1 : Q] + dot(b_mat, xw, TN)
        return 0

    lax.fori_loop(0, anti, lambda c, _: chunk_body(c, True), 0, unroll=4)
    if chunks > anti:
        lax.fori_loop(anti, chunks, lambda c, _: chunk_body(c, False), 0, unroll=4)


def scan_forward(prefix, x_pre, taps, skip, cols, rows, act, group, out):
    length, channels = x_pre.shape
    anti = min(MAX_PREFIX // Q, length // Q)
    given = [prefix, x_pre, taps, skip, cols, rows, act]
    in_specs = [
        pl.BlockSpec(memory_space=pltpu.SMEM),
        pl.BlockSpec((length, CG), lambda g: (0, group)),
        pl.BlockSpec((4, CG), lambda g: (0, group)),
        pl.BlockSpec((1, CG), lambda g: (0, group)),
        pl.BlockSpec((length, 128), lambda g: (0, 0)),
        pl.BlockSpec((128, length), lambda g: (0, 0)),
        pl.BlockSpec((length, 2 * N), lambda g: (0, 0)),
    ]
    aliases = {}
    if out is not None:
        aliases = {len(given): 0}
        given.append(out)
        in_specs.append(pl.BlockSpec(memory_space=pl.ANY))
    return pl.pallas_call(
        functools.partial(forward_kernel, channels // P_SIZE, group * HG),
        grid=(1,),
        in_specs=in_specs,
        out_specs=pl.BlockSpec((length, CG), lambda g: (0, group)),
        out_shape=jax.ShapeDtypeStruct((length, channels), BF16),
        input_output_aliases=aliases,
        scratch_shapes=[
            pltpu.VMEM((length, CG), BF16),
            pltpu.VMEM((length, CG), F32),
            pltpu.VMEM((anti, N, CG), BF16),
            pltpu.VMEM((N, CG), F32),
        ],
        compiler_params=pltpu.CompilerParams(vmem_limit_bytes=40 * MIB),
        cost_estimate=NO_COST,
        name="scan_forward",
    )(*given)


def backward_kernel(
    heads,
    first,
    more,
    prefix_ref,
    x_ref,
    dy_scr,
    taps_ref,
    skip_ref,
    cols_ref,
    rows_ref,
    act_ref,
    *refs,
):
    (
        gx_ref,
        gact_ref,
        gcols_ref,
        grows_ref,
        gsum_ref,
        x_scr,
        slope_scr,
        states_scr,
        dback_scr,
        state_ref,
        dstate_ref,
        next_scr,
    ) = refs[-12:]
    length, width = x_ref.shape
    chunks = length // Q
    anti = min(MAX_PREFIX // Q, chunks)
    prefix = prefix_ref[0]
    taps = taps_ref[...].astype(F32)
    skip = skip_ref[...]
    by_cum = spread_matrix(first, width)
    by_ecum = spread_matrix(heads + first, width)
    by_step = spread_matrix(2 * heads + first, width)
    collect = gather_matrix(first, width)
    lane_low = iota((1, 128), 1) < P_SIZE

    gsum_ref[...] = jnp.zeros_like(gsum_ref)
    state_ref[...] = jnp.zeros_like(state_ref)

    def stage_a(c, two_way):
        conv = conv_of(shifted_rows(x_ref, c), taps)
        s = sig(conv)
        x = conv * s
        x_scr[rows_of(c), :] = x
        slope_scr[rows_of(c), :] = s + x * (1.0 - s)
        dy = dy_scr[rows_of(c), :].astype(F32)
        gsum_ref[4:5, :] += jnp.sum(dy * x, axis=0, keepdims=True)
        part = cols_ref[rows_of(c), :]
        within, beyond = growths(part, heads)
        states_scr[c] = low(state_ref[...])
        entering = split_dot(within[Q - 8 :], by_cum)
        x_low = low(x * split_dot(part, by_step) * split_dot(beyond, by_cum))
        b_mat = act_ref[rows_of(c), 0:N]
        c_mat = act_ref[rows_of(c), N : 2 * N]
        state_ref[...] = state_ref[...] * entering[7:8] + dot(b_mat, x_low, TN)
        if two_way:
            leaving = split_dot(beyond, by_ecum)
            dback_scr[c + 1] = low(
                dback_scr[c].astype(F32) * entering[7:8] + dot(c_mat, low(dy * leaving), TN)
            )
        return 0

    dback_scr[0] = jnp.zeros_like(dback_scr[0])
    lax.fori_loop(0, anti, lambda c, _: stage_a(c, True), 0, unroll=4)
    if chunks > anti:
        lax.fori_loop(anti, chunks, lambda c, _: stage_a(c, False), 0, unroll=4)

    state_ref[...] = jnp.zeros_like(state_ref)
    dstate_ref[...] = jnp.zeros_like(dstate_ref)
    next_scr[...] = jnp.zeros_like(next_scr)
    s_idx, t_idx = iota((Q, Q), 0), iota((Q, Q), 1)
    causal_bias = jnp.where(s_idx <= t_idx, 0.0, NEG).astype(F32)
    from_r = jnp.where(s_idx >= t_idx, 1.0, 0.0)
    upto_r = jnp.where(s_idx <= t_idx, 1.0, 0.0)
    zero_q = jnp.zeros((Q, Q), F32)

    def twice(m):
        return low(
            jnp.concatenate(
                [jnp.concatenate([m, zero_q], axis=1), jnp.concatenate([zero_q, m], axis=1)], axis=0
            )
        )

    from_pair, upto_pair = twice(from_r), twice(upto_r)
    pair_s, pair_r = iota((Q, 2 * Q), 0), iota((Q, 2 * Q), 1) % Q
    before_pair = pair_s < pair_r
    after_pair = pair_s > pair_r
    sum_from = jnp.where(t_idx >= s_idx, 1.0, 0.0).astype(BF16)
    sum_before = jnp.where(t_idx < s_idx, 1.0, 0.0).astype(BF16)
    sum_upto = jnp.where(t_idx <= s_idx, 1.0, 0.0).astype(BF16)
    sum_after = jnp.where(t_idx > s_idx, 1.0, 0.0).astype(BF16)
    sum_all = jnp.concatenate([sum_from, sum_before, sum_upto, sum_after], axis=1)

    def chunk_body(c, two_way):
        b_mat = act_ref[rows_of(c), 0:N]
        c_mat = act_ref[rows_of(c), N : 2 * N]
        products = dot(b_mat, c_mat, NT)
        part = cols_ref[rows_of(c), :]
        within, beyond = growths(part, heads)
        rows = rows_ref[first : first + HG, rows_of(c)]
        erows = rows_ref[heads + first : heads + first + HG, rows_of(c)]
        x = x_scr[rows_of(c), :]
        dy_low = dy_scr[rows_of(c), :]
        dy = dy_low.astype(F32)
        step_wide = split_dot(part, by_step)
        xd = x * step_wide
        xd_low = low(xd)
        if two_way:
            anti_bias = jnp.where((s_idx > t_idx) & (s_idx + c * Q < prefix), 0.0, NEG).astype(F32)
        dprod = jnp.zeros((Q, Q), F32)
        parts, inner = [], []
        for pair in range(HG // 2):
            lanes = slice(pair * 128, pair * 128 + 128)
            dy_pair = dy_low[:, lanes]
            zero = jnp.zeros_like(dy_pair)
            blocks = jnp.concatenate(
                [jnp.where(lane_low, dy_pair, zero), jnp.where(lane_low, zero, dy_pair)], axis=0
            )
            dmix = dot(xd_low[:, lanes], blocks, NT)
            mixes, moved = [], []
            for k in (0, 1):
                h = 2 * pair + k
                e = rows[h : h + 1] - part[:, first + h : first + h + 1] + causal_bias
                if two_way:
                    at = heads + first + h
                    back = part[:, at : at + 1] - erows[h : h + 1] + anti_bias
                    e = jnp.maximum(e, back)
                decay = jnp.exp(e)
                slab = dmix[:, k * Q : k * Q + Q] * decay
                dprod = dprod + slab
                mixes.append(low(decay * products))
                moved.append(low(slab * products))
            parts.append(dot(jnp.concatenate(mixes, axis=1), blocks))
            both = jnp.concatenate(moved, axis=1)
            crossing = jnp.where(before_pair, dot(both, from_pair), 0.0)
            if two_way:
                crossing = jnp.where(after_pair, dot(both, upto_pair), crossing)
            inner.append(jnp.sum(crossing, axis=0, keepdims=True))
        for pair in range(HG // 2):
            for k in (0, 1):
                h = 2 * pair + k
                grows_ref[0, h : h + 1, rows_of(c)] = inner[pair][:, k * Q : k * Q + Q]

        entering = split_dot(within, by_cum)
        to_last = split_dot(beyond, by_cum)
        grow = entering[Q - 1 : Q]
        dstate_low = low(dstate_ref[...])
        state_in = states_scr[c]
        du_carry = dot(b_mat, dstate_low) * to_last
        du = jnp.concatenate(parts, axis=1) + du_carry
        y_in = dot(c_mat, state_in) * entering
        dy_in = low(dy * entering)
        x_out = low(xd * to_last)
        d_c = dot(low(dprod), b_mat, TN) + dot(dy_in, state_in, NT)
        d_b = dot(low(dprod), c_mat) + dot(x_out, dstate_low, NT)
        moved_by = [low(dy * y_in), low(xd * du_carry)]
        across = jnp.sum(dstate_ref[...] * state_in.astype(F32), axis=0, keepdims=True) * grow
        if two_way:
            back_state = state_ref[...]
            back_low = low(back_state)
            dback_low = dback_scr[c]
            leaving = split_dot(beyond, by_ecum)
            from_first = split_dot(within * prefix_column(prefix, c), by_ecum)
            du_back = dot(b_mat, dback_low) * from_first
            du = du + du_back
            y_back = dot(c_mat, back_low) * leaving
            x_back = low(xd * from_first)
            d_c = d_c + dot(low(dy * leaving), back_low, NT)
            d_b = d_b + dot(x_back, dback_low, NT)
            moved_by = moved_by + [low(dy * y_back), low(xd * du_back)]
            across = across + grow * jnp.sum(
                dback_low.astype(F32) * back_state, axis=0, keepdims=True
            )
            state_ref[...] = back_state * grow + dot(b_mat, x_back, TN)
        dstate_ref[...] = dstate_ref[...] * grow + dot(c_mat, dy_in, TN)
        d_bc = jnp.concatenate([d_b, d_c], axis=1)
        summed = dot(sum_all if two_way else sum_all[:, : 2 * Q], jnp.concatenate(moved_by, axis=0))
        qk = dot(low(summed), collect)
        direct = dot(low(x * du), collect)
        across8 = low_pair_dot(jnp.broadcast_to(across, (8, width)), collect)
        d_cols = jnp.concatenate([direct, qk + across8[0:1]], axis=1)
        if more:
            d_bc = d_bc + refs[0][rows_of(c), :]
            d_cols = d_cols + refs[1][rows_of(c), :]
        gact_ref[rows_of(c), :] = d_bc
        gcols_ref[rows_of(c), :] = d_cols

        dconv = (du * step_wide + skip * dy) * slope_scr[rows_of(c), :]
        shifted = shifted_rows(x_ref, c)
        both = jnp.concatenate([dconv, next_scr[...]], axis=0)
        gx = taps[3:4] * dconv
        gsum_ref[3:4, :] += jnp.sum(dconv * shifted[0], axis=0, keepdims=True)
        for j in (1, 2, 3):
            gx = gx + taps[3 - j : 4 - j] * pltpu.roll(both, Q + 8 - j, 0)[:Q]
            gsum_ref[3 - j : 4 - j, :] += jnp.sum(dconv * shifted[j], axis=0, keepdims=True)
        gx_ref[rows_of(c), :] = low(gx)
        next_scr[...] = dconv[0:8]
        return 0

    if chunks > anti:
        lax.fori_loop(0, chunks - anti, lambda i, _: chunk_body(chunks - 1 - i, False), 0, unroll=4)
    lax.fori_loop(0, anti, lambda i, _: chunk_body(anti - 1 - i, True), 0, unroll=4)


def scan_backward(prefix, x_pre, grad_ssd, taps, skip, cols, rows, act, group, place, places, gx, before):
    length, channels = x_pre.shape
    chunks = length // Q
    anti = min(MAX_PREFIX // Q, chunks)
    wide = pl.BlockSpec((length, CG), lambda i: (0, group))
    given = [prefix, x_pre, grad_ssd, taps, skip, cols, rows, act]
    in_specs = [
        pl.BlockSpec(memory_space=pltpu.SMEM),
        wide,
        wide,
        pl.BlockSpec((4, CG), lambda i: (0, group)),
        pl.BlockSpec((1, CG), lambda i: (0, group)),
        pl.BlockSpec((length, 128), lambda i: (0, 0)),
        pl.BlockSpec((128, length), lambda i: (0, 0)),
        pl.BlockSpec((length, 2 * N), lambda i: (0, 0)),
    ]
    aliases = {}
    if before is not None:
        given += list(before)
        in_specs += [
            pl.BlockSpec((length, 2 * N), lambda i: (0, 0)),
            pl.BlockSpec((length, 256), lambda i: (0, 0)),
        ]
        aliases = {len(given) - 2: 1, len(given) - 1: 2}
    if gx is not None:
        aliases[len(given)] = 0
        given.append(gx)
        in_specs.append(pl.BlockSpec(memory_space=pl.ANY))
    return pl.pallas_call(
        functools.partial(backward_kernel, channels // P_SIZE, group * HG, before is not None),
        grid=(1,),
        in_specs=in_specs,
        out_specs=[
            pl.BlockSpec((length, CG), lambda i: (0, place)),
            pl.BlockSpec((length, 2 * N), lambda i: (0, 0)),
            pl.BlockSpec((length, 256), lambda i: (0, 0)),
            pl.BlockSpec((1, HG, length), lambda i: (0, 0, 0)),
            pl.BlockSpec((8, CG), lambda i: (0, 0)),
        ],
        out_shape=(
            jax.ShapeDtypeStruct((length, places * CG), BF16),
            jax.ShapeDtypeStruct((length, 2 * N), F32),
            jax.ShapeDtypeStruct((length, 256), F32),
            jax.ShapeDtypeStruct((1, HG, length), F32),
            jax.ShapeDtypeStruct((8, CG), F32),
        ),
        input_output_aliases=aliases,
        scratch_shapes=[
            pltpu.VMEM((length, CG), F32),
            pltpu.VMEM((length, CG), F32),
            pltpu.VMEM((chunks, N, CG), BF16),
            pltpu.VMEM((anti + 1, N, CG), BF16),
            pltpu.VMEM((N, CG), F32),
            pltpu.VMEM((N, CG), F32),
            pltpu.VMEM((8, CG), F32),
        ],
        compiler_params=pltpu.CompilerParams(vmem_limit_bytes=40 * MIB),
        cost_estimate=NO_COST,
        name="scan_backward",
    )(*given)


TILE = 128


def block_of(lanes_ref, j):
    return pl.ds(pl.multiple_of(lanes_ref[j] * 128, 128), 128)


def place_kernel(normalize, count, tiles, lanes_ref, slots_ref, *refs):
    sources, by_ref, out_ref = refs[:count], refs[count], refs[count + 1]
    width = out_ref.shape[1]
    for k in range(count):

        @pl.when(pl.program_id(0) // tiles == k)
        def _(ref=sources[k]):
            if normalize:
                wide = ref[...].astype(F32)
                inv = lax.rsqrt(jnp.sum(wide * wide, axis=-1, keepdims=True) / width + EPSILON)
            else:
                inv = by_ref[...]
            for j in range(width // 128):
                there = block_of(lanes_ref, j)
                v = ref[:, there].astype(F32) * inv
                if normalize:
                    v = v * by_ref[:, there]
                out_ref[:, j * 128 : j * 128 + 128] = low(v)


def place_tokens(lanes, slots, sources, by, normalize):
    tokens, width = sources[0].shape
    count, tiles = len(sources), tokens // TILE

    def source(k):
        return pl.BlockSpec((TILE, width), lambda i, a, s: (jnp.clip(i - k * tiles, 0, tiles - 1), 0))

    def placed(i, a, s):
        return (s[i // tiles] * tiles + i % tiles, 0)

    by_spec = pl.BlockSpec((1, width), lambda i, a, s: (0, 0)) if normalize else pl.BlockSpec((TILE, 1), placed)
    return pl.pallas_call(
        functools.partial(place_kernel, normalize, count, tiles),
        grid_spec=pltpu.PrefetchScalarGridSpec(
            num_scalar_prefetch=2,
            grid=(count * tiles,),
            in_specs=[source(k) for k in range(count)] + [by_spec],
            out_specs=pl.BlockSpec((TILE, width), placed),
        ),
        out_shape=jax.ShapeDtypeStruct((tokens * count, width), BF16),
        compiler_params=pltpu.CompilerParams(vmem_limit_bytes=32 * MIB),
        cost_estimate=NO_COST,
        name="place_tokens",
    )(lanes, slots, *sources, by)


def half_sum(refs, j, per_half):
    here = slice((j % per_half) * 128, (j % per_half) * 128 + 128)
    side = refs[: len(refs) // 2] if j < per_half else refs[len(refs) // 2 :]
    total = side[0][:, here].astype(F32)
    for ref in side[1:]:
        total = total + ref[:, here].astype(F32)
    return total


def mixed_kernel(lanes_ref, slots_ref, hidden_ref, *refs):
    out_ref = refs[-1]
    blocks = hidden_ref.shape[1] // 128
    for j in range(blocks):
        there = block_of(lanes_ref, j)
        out_ref[:, there] = hidden_ref[:, there].astype(F32) + half_sum(refs[:-1], j, blocks // 2)


def finish_kernel(lanes_ref, slots_ref, hidden_ref, cot_ref, gain_ref, *refs):
    out_ref = refs[-1]
    width = hidden_ref.shape[1]
    blocks = width // 128
    wide = hidden_ref[...].astype(F32)
    inv = lax.rsqrt(jnp.sum(wide * wide, axis=-1, keepdims=True) / width + EPSILON)
    total = jnp.zeros((TILE, 128), F32)
    for j in range(blocks):
        there = block_of(lanes_ref, j)
        scaled = half_sum(refs[:-1], j, blocks // 2) * gain_ref[:, there]
        total = total + scaled * hidden_ref[:, there].astype(F32)
        out_ref[:, there] = scaled
    coef = inv * inv * inv * (jnp.sum(total, axis=-1, keepdims=True) / width)
    out_ref[...] = inv * out_ref[...] - wide * coef + cot_ref[...].astype(F32)


def own_rows(kernel, name, lanes, slots, hidden, more, gain, halves):
    tokens, width = hidden.shape
    tiles = tokens // TILE
    tile = pl.BlockSpec((TILE, width), lambda i, a, s: (i, 0))
    given, specs = [hidden, *more], [tile] * (1 + len(more))
    if gain is not None:
        given.append(gain)
        specs.append(pl.BlockSpec((1, width), lambda i, a, s: (0, 0)))
    for half in halves:
        for array, whole in half:
            given.append(array)
            if whole:
                specs.append(pl.BlockSpec((TILE, width // 2), lambda i, a, s: (s[0] * tiles + i, 0)))
            else:
                specs.append(pl.BlockSpec((TILE, width // 2), lambda i, a, s: (i, 0)))
    return pl.pallas_call(
        kernel,
        grid_spec=pltpu.PrefetchScalarGridSpec(
            num_scalar_prefetch=2, grid=(tiles,), in_specs=specs, out_specs=tile
        ),
        out_shape=jax.ShapeDtypeStruct((tokens, width), F32),
        compiler_params=pltpu.CompilerParams(vmem_limit_bytes=60 * MIB),
        cost_estimate=NO_COST,
        name=name,
    )(lanes, slots, *given)


def post_kernel(rest_ref, taps_ref, decay_ref, bias_ref, *refs):
    gbc_ref, gtaps_ref, ghead_ref, next_scr = refs[-4:]
    gact_ref, gcols_ref, grows = refs[0], refs[1], refs[2:-4]
    length, heads = rest_ref.shape[0], decay_ref.shape[1]
    chunks = length // Q
    taps = taps_ref[...]
    gtaps_ref[...] = jnp.zeros_like(gtaps_ref)
    ghead_ref[...] = jnp.zeros_like(ghead_ref)
    next_scr[...] = jnp.zeros_like(next_scr)
    filler = jnp.zeros((1, 128 - heads), F32)
    growth = -jnp.exp(jnp.concatenate([decay_ref[...], filler], axis=1))
    bias = jnp.concatenate([bias_ref[...], filler], axis=1)

    def body(i, _):
        c = chunks - 1 - i
        shifted = shifted_rows(rest_ref, c, 2 * N)
        conv = conv_of(shifted, taps)
        s = sig(conv)
        dconv = gact_ref[rows_of(c), :] * (s + conv * s * (1.0 - s))
        both = jnp.concatenate([dconv, next_scr[...]], axis=0)
        g = taps[3:4] * dconv
        gtaps_ref[3:4, :] += jnp.sum(dconv * shifted[0], axis=0, keepdims=True)
        for j in (1, 2, 3):
            g = g + taps[3 - j : 4 - j] * pltpu.roll(both, Q + 8 - j, 0)[:Q]
            gtaps_ref[3 - j : 4 - j, :] += jnp.sum(dconv * shifted[j], axis=0, keepdims=True)
        gbc_ref[rows_of(c), 0 : 2 * N] = low(g)
        next_scr[...] = dconv[0:8]

        direct, moved = gcols_ref[rows_of(c), 0:128], gcols_ref[rows_of(c), 128:256]
        inner = [ref[0, :, rows_of(c)] for ref in grows]
        inner.append(jnp.zeros((128 - heads, Q), F32))
        moved = moved + jnp.concatenate(inner, axis=0).T
        raw = rest_ref[rows_of(c), 2 * N :] + bias
        step = jnp.maximum(raw, 0.0) + jnp.log(1.0 + jnp.exp(-jnp.abs(raw)))
        gdt = (direct + moved * growth) * sig(raw)
        gbc_ref[rows_of(c), 2 * N :] = low(gdt[:, 0:heads])
        ghead_ref[0:1, :] += jnp.sum(moved * growth * step, axis=0, keepdims=True)
        ghead_ref[1:2, :] += jnp.sum(gdt, axis=0, keepdims=True)
        return 0

    lax.fori_loop(0, chunks, body, 0, unroll=4)


def post(rest_pre, bc_taps, log_decay, dt_bias, grad_act, gcols, grows):
    length, heads = rest_pre.shape[0], log_decay.shape[0]
    return pl.pallas_call(
        post_kernel,
        out_shape=(
            jax.ShapeDtypeStruct((length, 2 * N + heads), BF16),
            jax.ShapeDtypeStruct((8, 2 * N), F32),
            jax.ShapeDtypeStruct((8, 128), F32),
        ),
        scratch_shapes=[pltpu.VMEM((8, 2 * N), F32)],
        compiler_params=pltpu.CompilerParams(vmem_limit_bytes=40 * MIB),
        cost_estimate=NO_COST,
        name="post",
    )(rest_pre, bc_taps, log_decay[None], dt_bias[None], grad_act, gcols, *grows)


def gate_kernel(a_ref, own_ref, other_ref, ssd_ref, gain_ref, gate_ref, out_ref, square_ref):
    depth = own_ref.shape[0]
    gain = gain_ref[...]

    @pl.when(pl.program_id(0) == 0)
    def _():
        square_ref[...] = jnp.zeros_like(square_ref)

    for m in range(0, a_ref.shape[0], 256):
        here = slice(m, m + 256)
        z = dot(a_ref[here, :depth], own_ref[...]) + dot(a_ref[here, depth:], other_ref[...])
        gated = ssd_ref[here, :].astype(F32) * (z * sig(z))
        gate_ref[here, :] = low(z)
        out_ref[here, :] = low(gated * gain)
        square = gated * gated
        square_ref[here, :] += sum(square[:, k : k + 128] for k in range(0, CG, 128))


def gate_product(normed, own, other, ssd_out, gain):
    tokens, width = normed.shape
    channels = ssd_out.shape[1]
    tall = pl.BlockSpec((tokens, CG), lambda j: (0, j))
    deep = pl.BlockSpec((width // 2, CG), lambda j: (0, j))
    return pl.pallas_call(
        gate_kernel,
        grid=(channels // CG,),
        in_specs=[
            pl.BlockSpec((tokens, width), lambda j: (0, 0)), deep, deep, tall, pl.BlockSpec((1, CG), lambda j: (0, j)),
        ],
        out_specs=[tall, tall, pl.BlockSpec((tokens, 128), lambda j: (0, 0))],
        out_shape=(
            jax.ShapeDtypeStruct((tokens, channels), BF16),
            jax.ShapeDtypeStruct((tokens, channels), BF16),
            jax.ShapeDtypeStruct((tokens, 128), F32),
        ),
        compiler_params=pltpu.CompilerParams(vmem_limit_bytes=40 * MIB),
        cost_estimate=NO_COST,
        name="gate_product",
    )(normed, own, other, ssd_out, gain)


def gating_kernel(a_ref, own_ref, other_ref, gate_ref, ssd_ref, coef_ref, gain_ref, ggate_ref, dy_ref):
    depth = own_ref.shape[0]
    gain = gain_ref[...]
    for m in range(0, a_ref.shape[0], 256):
        here = slice(m, m + 256)
        scaled = dot(a_ref[here, :depth], own_ref[...]) + dot(a_ref[here, depth:], other_ref[...])
        z = gate_ref[here, :].astype(F32)
        y = ssd_ref[here, :].astype(F32)
        s = sig(z)
        act = z * s
        grad = gain * scaled - y * act * coef_ref[here, :]
        ggate_ref[here, :] = low(grad * y * (s + act * (1.0 - s)))
        dy_ref[here, :] = low(grad * act)


def gating_product(cot, own, other, gate, ssd_out, coef, gain):
    tokens, width = cot.shape
    channels = ssd_out.shape[1]
    tall = pl.BlockSpec((tokens, CG), lambda j: (0, j))
    deep = pl.BlockSpec((width // 2, CG), lambda j: (0, j))
    return pl.pallas_call(
        gating_kernel,
        grid=(channels // CG,),
        in_specs=[
            pl.BlockSpec((tokens, width), lambda j: (0, 0)), deep, deep, tall, tall,
            pl.BlockSpec((tokens, 1), lambda j: (0, 0)), pl.BlockSpec((1, CG), lambda j: (0, j)),
        ],
        out_specs=[tall, tall],
        out_shape=(
            jax.ShapeDtypeStruct((tokens, channels), BF16),
            jax.ShapeDtypeStruct((tokens, channels), BF16),
        ),
        compiler_params=pltpu.CompilerParams(vmem_limit_bytes=40 * MIB),
        cost_estimate=NO_COST,
        name="gating_product",
    )(cot, own, other, gate, ssd_out, coef, gain)


def snake(devices):
    half = devices // 4
    return [z * 2 for z in range(half)] + [z * 2 + 1 for z in reversed(range(half))]


def chip_groups(devices):
    return [[chip * 2 + core for chip in snake(devices)] for core in (0, 1)]


def other_core(v, devices):
    return lax.ppermute(v, "fsdp", [(i, i ^ 1) for i in range(devices)])


def other_half(v):
    return lax.ppermute(v, "tp", [(0, 1), (1, 0)])


def tie(first, second):
    return lax.optimization_barrier((first, second))


def gather(v, devices):
    return lax.all_gather(v, "fsdp", axis=0, tiled=True, axis_index_groups=chip_groups(devices))


def doubling_gather(v, devices):
    me = lax.axis_index("fsdp")
    bit = 1
    while bit < devices:
        came = lax.ppermute(v, "fsdp", [(i, i ^ bit) for i in range(devices)])
        mine_first = me & bit == 0
        v = jnp.concatenate([jnp.where(mine_first, v, came), jnp.where(mine_first, came, v)], axis=0)
        bit *= 2
    return v


def scatter(v, devices):
    return lax.psum_scatter(
        v, "fsdp", scatter_dimension=0, tiled=True, axis_index_groups=chip_groups(devices)
    )


def on_device(
    hidden,
    cotangent,
    prefix,
    input_norm_gain,
    z_weight,
    x_weight,
    bc_weight,
    dt_weight,
    x_conv,
    bc_conv,
    log_decay,
    dt_bias,
    skip_gain,
    gate_gain,
    out_weight,
):
    fsdp = lax.axis_size("fsdp")
    tp = lax.axis_size("tp")
    own_tokens, width = hidden.shape
    heads = log_decay.shape[0]
    channels = heads * P_SIZE
    all_channels = channels * tp
    groups = channels // CG
    taps_own = x_conv.shape[2]
    rows = width // fsdp
    ring = fsdp // 2
    half_width = width // 2

    order = snake(fsdp)
    core = lax.axis_index("fsdp") % 2
    line = jnp.array(order, jnp.int32)
    blocks = jnp.concatenate([line * 2 + core, line * 2 + 1 - core])
    direct = rows % 128 == 0
    per = max(rows // 128, 1)
    if direct:
        lanes = (blocks[:, None] * per + jnp.arange(per)[None]).reshape(-1)
    else:
        lanes = jnp.arange(width // 128)
    lanes = lanes.astype(jnp.int32)

    def to_cores(v):
        zero = jnp.stack([v[2 * chip] for chip in order])
        one = jnp.stack([v[2 * chip + 1] for chip in order])
        return jnp.where(core == 0, zero, one), jnp.where(core == 0, one, zero)

    def to_ring(v):
        return v if direct else v.reshape(-1, fsdp, rows)[:, blocks].reshape(v.shape)

    def from_ring(v):
        if direct:
            return v
        return v.reshape(-1, fsdp, rows)[:, jnp.argsort(blocks)].reshape(v.shape)

    small = jnp.concatenate(
        [input_norm_gain.reshape(-1), x_conv.reshape(-1), bc_conv.reshape(-1), gate_gain.reshape(-1)]
    )
    sizes = [input_norm_gain.size, x_conv.size, bc_conv.size, gate_gain.size]
    cuts = [0]
    for size in sizes:
        cuts.append(cuts[-1] + size)
    small_all = doubling_gather(jnp.pad(small, (0, -small.size % 128))[None], fsdp)
    payload = jnp.concatenate([x_weight, bc_weight, dt_weight, dt_weight, dt_weight], axis=1)
    payload = jnp.pad(payload, ((0, 0), (0, 128 - 3 * heads)))

    if tp == 2:
        mine = lax.axis_index("tp").astype(jnp.int32)
        slots = jnp.stack([mine, 1 - mine])
        hidden_other = other_half(hidden)
        cot_given, hidden_other = tie(cotangent, hidden_other)
        hidden_parts = [hidden, hidden_other]
        cot_parts = [cotangent, other_half(cot_given)]
    else:
        slots = jnp.zeros((2,), jnp.int32)
        hidden_parts = [lax.all_gather(hidden, "tp", axis=0, tiled=True)]
        cot_parts = [lax.all_gather(cotangent, "tp", axis=0, tiled=True)]
    hidden_parts = [to_ring(v) for v in hidden_parts]
    cot_parts = [to_ring(v) for v in cot_parts]

    norm_gain = small_all[:, cuts[0] : cuts[1]].reshape(1, -1).astype(F32)
    x_taps = small_all[:, cuts[1] : cuts[2]].reshape(fsdp, heads, 4, taps_own)
    x_taps = jnp.transpose(x_taps, (2, 1, 0, 3)).reshape(4, channels).astype(F32)
    bc_taps = small_all[:, cuts[2] : cuts[3]].reshape(fsdp, 4, -1)
    bc_taps = jnp.transpose(bc_taps, (1, 0, 2)).reshape(4, 2 * N).astype(F32)
    gain = small_all[:, cuts[3] : cuts[4]].reshape(fsdp, heads, -1)
    gain = jnp.transpose(gain, (1, 0, 2)).reshape(1, channels).astype(F32)
    skip = jnp.repeat(skip_gain, P_SIZE)[None]
    hidden_parts[-1], (norm_gain, x_taps, bc_taps, gain, skip) = tie(
        hidden_parts[-1], (norm_gain, x_taps, bc_taps, gain, skip)
    )

    x_own = gather(payload, fsdp)
    z_own = gather(z_weight, fsdp)
    out_own = gather(out_weight.T, fsdp)
    x_own, hidden_parts[-1] = tie(x_own, hidden_parts[-1])
    x_other = other_core(x_own, fsdp)

    norm_gain = to_ring(norm_gain)
    normed = place_tokens(lanes, slots, hidden_parts, norm_gain, True)
    na, nb = normed[:, :half_width], normed[:, half_width:]
    few = slice(channels, channels + 2 * N + 128)
    rest_pre = dot(na, x_own[:, few]) + dot(nb, x_other[:, few])
    rest = slice(channels, channels + 2 * N + heads)
    rest_own, rest_other = x_own[:, rest], x_other[:, rest]
    act, cols, head_rows = prep(rest_pre, bc_taps, log_decay, dt_bias)
    x_pre = low(dot(na, x_own[:, :channels]) + dot(nb, x_other[:, :channels]))
    ssd_out = None
    for g in range(groups):
        ssd_out = scan_forward(prefix, x_pre, x_taps, skip, cols, head_rows, act, g, ssd_out)
    (z_own, cot_parts[-1]), ssd_out = tie((z_own, cot_parts[-1]), ssd_out)
    z_other = other_core(z_own, fsdp)

    gate_low, scaled_out, square = gate_product(normed, z_own, z_other, ssd_out, gain)
    square_sum = lax.psum(jnp.sum(square, axis=-1), "tp")

    inv_gate = lax.rsqrt(square_sum / all_channels + EPSILON)[:, None]
    cot_rel = place_tokens(lanes, slots, cot_parts, inv_gate, False)
    ca, cb = cot_rel[:, :half_width], cot_rel[:, half_width:]
    gout_other = low(dot(cb, scaled_out, TN))
    gout_came = other_core(gout_other, fsdp)
    gout_sum = low(dot(ca, scaled_out, TN) + gout_came.astype(F32))
    (scaled_out, out_own), gout_sum = tie((scaled_out, out_own), gout_sum)
    grad_out = scatter(gout_sum, fsdp)
    out_other = other_core(out_own, fsdp)

    branch, along = [], 0.0
    for cot_half, out_half in ((ca, out_own), (cb, out_other)):
        v = dot(scaled_out, out_half, NT)
        along = along + jnp.sum(v * cot_half.astype(F32), axis=-1)
        branch.append(low(v * inv_gate))
    along = lax.psum(along, "tp")
    coef = inv_gate * inv_gate * (along / all_channels)[:, None]
    coef, branch = tie(coef, branch)

    def to_own_tokens(v):
        if tp == 2:
            leaving = lax.dynamic_slice_in_dim(v, (1 - mine) * own_tokens, own_tokens, 0)
            return [(v, True), (other_half(leaving), False)]
        return [(lax.psum_scatter(v, "tp", scatter_dimension=0, tiled=True), False)]

    branch_parts = [to_own_tokens(v) for v in branch]
    kinds = [[whole for _, whole in half] for half in branch_parts]
    branch_parts = [[v for v, _ in half] for half in branch_parts]

    ggate, dy = gating_product(cot_rel, out_own, out_other, gate_low, ssd_out, coef, gain)
    gz_came = other_core(low(dot(nb, ggate, TN)), fsdp)
    z_parts = [dot(ggate, z_own, NT), dot(ggate, z_other, NT)]
    normed, z_parts = tie(normed, z_parts)
    na, nb = normed[:, :half_width], normed[:, half_width:]
    gz_sum = low(dot(na, ggate, TN) + gz_came.astype(F32))
    dy, gz_sum = tie(dy, gz_sum)
    grad_z = scatter(gz_sum, fsdp)

    grows, gsums = [], []
    first = groups // 2
    before = None

    def back_through(start, stop, dy, before):
        gx = None
        for g in range(start, stop):
            gx, gact, gcol, grow, gsum = scan_backward(
                prefix, x_pre, dy, x_taps, skip, cols, head_rows, act, g, g - start, stop - start, gx, before
            )
            before = (gact, gcol)
            grows.append(grow)
            gsums.append(gsum)
        return gx, before

    grad_x = []
    if first:
        gx, before = back_through(0, first, dy, before)
        gx, (branch_parts, grad_out, grad_z) = tie(gx, (branch_parts, grad_out, grad_z))
        came = other_core(low(dot(nb, gx, TN)), fsdp)
        z_parts = [
            v + dot(gx, half[:, : first * CG], NT) for v, half in zip(z_parts, (x_own, x_other))
        ]
        normed, z_parts = tie(normed, z_parts)
        na, nb = normed[:, :half_width], normed[:, half_width:]
        total = low(dot(na, gx, TN) + came.astype(F32))
        dy, total = tie(dy, total)
        grad_x.append(scatter(total, fsdp))
    gx, before = back_through(first, groups, dy, before)
    gx, (grad_z, *grad_x) = tie(gx, (grad_z, *grad_x))
    g_gain = jnp.sum(out_weight.T.astype(F32) * grad_out.astype(F32), axis=0) / gain[0]
    g_gain = jnp.transpose(g_gain.reshape(heads, fsdp, -1), (1, 0, 2))
    grad_x = list(grad_x)
    late = slice(first * CG, channels)
    grest, gbc_taps, ghead = post(rest_pre, bc_taps, log_decay, dt_bias, before[0], before[1], grows)

    gsum = jnp.concatenate(gsums, axis=1)
    gx_taps = jnp.transpose(gsum[0:4].reshape(4, heads, fsdp, taps_own), (2, 1, 0, 3))
    g_taps = jnp.transpose(gbc_taps[0:4].reshape(4, fsdp, -1), (1, 0, 2))
    g_skip = jnp.sum(gsum[4].reshape(heads, P_SIZE), axis=-1)
    per_head = jnp.concatenate([ghead[0, :heads], ghead[1, :heads], g_skip])
    slices = jnp.concatenate(
        [
            g_taps.reshape(fsdp, -1),
            gx_taps.reshape(fsdp, -1),
            g_gain.reshape(fsdp, -1),
            jnp.broadcast_to(per_head[None], (fsdp, per_head.size)),
        ],
        axis=1,
    )
    size = slices.shape[1]
    lone = -(-size // rows)
    lines_own, lines_other = [
        jnp.pad(v, ((0, 0), (0, lone * rows - size))).reshape(half_width, lone) for v in to_cores(slices)
    ]
    rest_leaves = jnp.concatenate([dot(nb, grest, TN), lines_other], axis=1)
    rest_came = other_core(rest_leaves, fsdp)
    gx, rest_leaves = tie(gx, rest_leaves)
    gx_other = low(dot(nb, gx, TN))
    came = other_core(gx_other, fsdp)
    (grest, gx), gx_other = tie((grest, gx), gx_other)
    rest_sum = jnp.concatenate([dot(na, grest, TN), lines_own], axis=1) + rest_came
    (grest, gx), rest_sum = tie((grest, gx), rest_sum)
    mine_rest = scatter(rest_sum, fsdp)

    def first_part(v, x_half):
        return v + dot(gx, x_half[:, late], NT)

    part = low(first_part(z_parts[0], x_own) + dot(grest, rest_own, NT))
    part_sums = [to_own_tokens(part)]
    kinds_part = [whole for _, whole in part_sums[0]]
    gx, part = tie(gx, part)
    gx_sum = low(dot(na, gx, TN) + came.astype(F32))
    gx, gx_sum = tie(gx, gx_sum)
    grad_x.append(scatter(gx_sum, fsdp))
    second = first_part(z_parts[1], x_other)
    (branch_parts, grad_out, grad_z), part = tie((branch_parts, grad_out, grad_z), part)
    mixed = from_ring(
        own_rows(
            mixed_kernel, "add_branch", lanes, slots, to_ring(hidden), [], None,
            [list(zip(half, kind)) for half, kind in zip(branch_parts, kinds)],
        )
    )
    grad_z, grad_out = grad_z.astype(F32), grad_out.astype(F32).T
    arrived = [v for v, _ in part_sums[0]]
    second, (arrived, mixed, grad_out, grad_z) = tie(second, (arrived, mixed, grad_out, grad_z))
    part_sums[0] = list(zip(arrived, kinds_part))
    part_sums.append(to_own_tokens(low(second + dot(grest, rest_other, NT))))

    def over_tp(v):
        return v + other_half(v) if tp == 2 else lax.psum(v, "tp")

    grad_bc, grad_dt = mine_rest[:, : 2 * N], mine_rest[:, 2 * N : 2 * N + heads]
    lines = mine_rest[:, 2 * N + heads :].reshape(-1)
    n_taps, bc_size = bc_conv.size, rows * 2 * N
    at = [n_taps]
    for size in (x_conv.size, gate_gain.size, heads, heads, heads):
        at.append(at[-1] + size)
    gx_taps = lines[at[0] : at[1]].reshape(x_conv.shape)
    g_gain = lines[at[1] : at[2]].reshape(gate_gain.shape)
    g_decay, g_bias, g_skip = [lines[at[k] : at[k + 1]] for k in (2, 3, 4)]

    def weighted(w, g):
        return jnp.sum(w.astype(F32) * g.astype(F32), axis=1)

    grad_gain = weighted(z_weight, grad_z) + weighted(bc_weight, grad_bc) + weighted(dt_weight, grad_dt)
    last, whole = part_sums[1][-1]
    last, (mixed, grad_gain, grad_out, grad_z) = tie(last, (mixed, grad_gain, grad_out, grad_z))
    part_sums[1][-1] = (last, whole)
    grad_hidden = from_ring(
        own_rows(finish_kernel, "finish", lanes, slots, to_ring(hidden), [to_ring(cotangent)], norm_gain, part_sums)
    )
    grad_x = jnp.concatenate(grad_x, axis=1).astype(F32)
    grad_gain = (grad_gain + weighted(x_weight, grad_x)) / input_norm_gain.astype(F32)
    together = over_tp(jnp.concatenate([grad_bc.reshape(-1), lines[:n_taps], grad_gain]))
    grad_bc = together[:bc_size].reshape(rows, 2 * N)
    g_taps = together[bc_size : bc_size + n_taps].reshape(bc_conv.shape)
    grad_gain = together[bc_size + n_taps :]
    return (
        mixed, grad_hidden, grad_gain, grad_z, grad_x, grad_bc, grad_dt, gx_taps, g_taps, g_decay, g_bias,
        g_skip, g_gain, grad_out,
    )


def solution(mesh):
    both = P(("fsdp", "tp"), None)
    split = P("fsdp", "tp")
    ins = (
        both, both, P("fsdp"), P("fsdp"), split, split, P("fsdp", None), split, P("tp", None, "fsdp"),
        P(None, "fsdp"), P("tp"), P("tp"), P("tp"), P("tp", "fsdp"), P("tp", "fsdp"),
    )
    outs = (
        both, both, P("fsdp"), split, split, P("fsdp", None), split, P("tp", None, "fsdp"),
        P(None, "fsdp"), P("tp"), P("tp"), P("tp"), P("tp", "fsdp"), P("tp", "fsdp"),
    )
    return jax.shard_map(on_device, mesh=mesh, in_specs=ins, out_specs=outs, check_vma=False)
```

```python
import functools

import jax
import jax.numpy as jnp
from jax import lax
from jax.experimental import pallas as pl
from jax.experimental.pallas import tpu as pltpu
from jax.sharding import PartitionSpec as P

P_SIZE = 64
N = 128
Q = 128
HG = 8
CG = HG * P_SIZE
MAX_PREFIX = 512
EPSILON = 1e-05
F32 = jnp.float32
BF16 = jnp.bfloat16
NEG = -1e30
NN = ((1,), (0,))
NT = ((1,), (1,))
TN = ((0,), (0,))
MIB = 1024 * 1024
NO_COST = pl.CostEstimate(flops=0, bytes_accessed=0, transcendentals=0)


def dot(a, b, dims=NN):
    return lax.dot_general(a, b, (dims, ((), ())), preferred_element_type=F32)


def low(v):
    return v.astype(BF16)


def split_dot(v, e):
    hi = low(v)
    rest = low(v - hi.astype(F32))
    return dot(jnp.concatenate([hi, rest], axis=1), e)


def low_pair_dot(v, e):
    hi = low(v)
    return dot(hi, e) + dot(low(v - hi.astype(F32)), e)


def three_dot(e, v):
    hi = low(v)
    rest = v - hi.astype(F32)
    mid = low(rest)
    return dot(e, hi) + (dot(e, mid) + dot(e, low(rest - mid.astype(F32))))


def iota(shape, dim):
    return lax.broadcasted_iota(jnp.int32, shape, dim)


def sig(v):
    return 0.5 + 0.5 * jnp.tanh(0.5 * v)


def rows_of(c):
    return pl.ds(pl.multiple_of(c * Q, Q), Q)


def shifted_rows(x_ref, c, width=None):
    lanes = slice(0, width)
    cur = x_ref[rows_of(c), lanes].astype(F32)
    start = pl.multiple_of(jnp.maximum(c * Q - 16, 0), 16)
    before = x_ref[pl.ds(start, 16), lanes].astype(F32)[8:]
    before = jnp.where(c > 0, before, 0.0)
    both = jnp.concatenate([before, cur], axis=0)
    return [cur] + [pltpu.roll(both, j, 0)[8:] for j in (1, 2, 3)]


def conv_of(shifted, taps):
    total = taps[3:4] * shifted[0]
    for j in (1, 2, 3):
        total = total + taps[3 - j : 4 - j] * shifted[j]
    return total


def spread_matrix(start, width):
    return jnp.where(
        iota((256, width), 1) // P_SIZE + start == iota((256, width), 0) % 128, 1.0, 0.0
    ).astype(BF16)


def gather_matrix(start, width):
    return jnp.where(
        iota((width, 128), 0) // P_SIZE + start == iota((width, 128), 1), 1.0, 0.0
    ).astype(BF16)


def prep_kernel(rest_ref, taps_ref, decay_ref, bias_ref, act_ref, cols_ref, rows_ref):
    heads = decay_ref.shape[1]
    length = rest_ref.shape[0]
    taps = taps_ref[...]
    tri = jnp.where(iota((Q, Q), 0) >= iota((Q, Q), 1), 1.0, 0.0).astype(BF16)
    lane = iota((1, 128), 1)
    filler = jnp.zeros((1, 128 - 3 * heads), F32)
    decay = jnp.concatenate([decay_ref[...]] * 3 + [filler], axis=1)
    bias = jnp.concatenate([bias_ref[...]] * 3 + [filler], axis=1)
    growth = -jnp.exp(decay)

    def body(c, _):
        conv = conv_of(shifted_rows(rest_ref, c, 2 * N), taps)
        act_ref[rows_of(c), :] = low(conv * sig(conv))
        raw = rest_ref[rows_of(c), 2 * N :] + bias
        raw = jnp.where(lane < 3 * heads, raw, 0.0)
        step = jnp.maximum(raw, 0.0) + jnp.log(1.0 + jnp.exp(-jnp.abs(raw)))
        rate = growth * step
        cum = three_dot(tri, rate)
        packed = jnp.where(lane < heads, cum, jnp.where(lane < 2 * heads, cum - rate, step))
        packed = jnp.where(lane < 3 * heads, packed, 0.0)
        cols_ref[rows_of(c), :] = packed
        rows_ref[:, rows_of(c)] = packed.T
        return 0

    lax.fori_loop(0, length // Q, body, 0, unroll=4)


def prep(rest_pre, bc_taps, log_decay, dt_bias):
    length = rest_pre.shape[0]
    return pl.pallas_call(
        prep_kernel,
        out_shape=(
            jax.ShapeDtypeStruct((length, 2 * N), BF16),
            jax.ShapeDtypeStruct((length, 128), F32),
            jax.ShapeDtypeStruct((128, length), F32),
        ),
        compiler_params=pltpu.CompilerParams(vmem_limit_bytes=32 * MIB),
        cost_estimate=NO_COST,
        name="prep",
    )(rest_pre, bc_taps, log_decay[None], dt_bias[None])


def prefix_column(prefix, c):
    return jnp.where(iota((Q, 1), 0) + c * Q < prefix, 1.0, 0.0).astype(F32)


def growths(part, heads):
    lane = iota((1, 128), 1)
    used = lane < 2 * heads
    tail = part[Q - 8 :]
    last = jnp.where(lane < heads, tail, pltpu.roll(tail, heads, 1))[7:8]
    within = jnp.where(used, jnp.exp(jnp.where(used, part, 0.0)), 0.0)
    beyond = jnp.where(used, jnp.exp(jnp.where(used, last - part, 0.0)), 0.0)
    return within, beyond


def forward_kernel(
    heads, first, prefix_ref, x_ref, taps_ref, skip_ref, cols_ref, rows_ref, act_ref, *refs
):
    out_ref, states_ref, xd_ref, kept_ref, back_ref, state_ref = refs[-6:]
    length, width = x_ref.shape
    chunks = length // Q
    anti = min(MAX_PREFIX // Q, chunks)
    prefix = prefix_ref[0]
    taps = taps_ref[...].astype(F32)
    skip = skip_ref[...]
    by_cum = spread_matrix(first, width)
    by_ecum = spread_matrix(heads + first, width)
    by_step = spread_matrix(2 * heads + first, width)
    lane_low = iota((1, 128), 1) < P_SIZE

    def stage_a(c, _):
        conv = conv_of(shifted_rows(x_ref, c), taps)
        x = conv * sig(conv)
        xd_ref[rows_of(c), :] = low(x * split_dot(cols_ref[rows_of(c), :], by_step))
        kept_ref[rows_of(c), :] = x * skip
        return 0

    lax.fori_loop(0, chunks, stage_a, 0, unroll=4)

    state_ref[...] = jnp.zeros_like(state_ref)
    back_ref[anti - 1] = jnp.zeros_like(back_ref[anti - 1])
    for c in range(anti - 1, 0, -1):
        within, _ = growths(cols_ref[rows_of(c), :], heads)
        weight = split_dot(within * prefix_column(prefix, c), by_ecum)
        grow = split_dot(within[Q - 8 :], by_cum)[7:8]
        b_mat = act_ref[rows_of(c), 0:N]
        xw = low(xd_ref[rows_of(c), :].astype(F32) * weight)
        state_ref[...] = state_ref[...] * grow + dot(b_mat, xw, TN)
        back_ref[c - 1] = low(state_ref[...])

    state_ref[...] = jnp.zeros_like(state_ref)
    causal_bias = jnp.where(iota((Q, Q), 1) <= iota((Q, Q), 0), 0.0, NEG).astype(F32)

    def chunk_body(c, two_way):
        b_mat = act_ref[rows_of(c), 0:N]
        c_mat = act_ref[rows_of(c), N : 2 * N]
        products = dot(c_mat, b_mat, NT)
        part = cols_ref[rows_of(c), :]
        within, beyond = growths(part, heads)
        entering = split_dot(within, by_cum)
        state_low = low(state_ref[...])
        states_ref[c] = state_low
        total = kept_ref[rows_of(c), :] + dot(c_mat, state_low) * entering
        if two_way:
            leaving = split_dot(beyond, by_ecum)
            total = total + dot(c_mat, back_ref[c]) * leaving
            anti_bias = jnp.where(
                (iota((Q, Q), 1) > iota((Q, Q), 0)) & (iota((Q, Q), 1) + c * Q < prefix), 0.0, NEG
            ).astype(F32)
        xd = xd_ref[rows_of(c), :]
        rows = rows_ref[first : first + HG, rows_of(c)]
        erows = rows_ref[heads + first : heads + first + HG, rows_of(c)]
        parts = []
        for pair in range(HG // 2):
            mixes = []
            for h in (2 * pair, 2 * pair + 1):
                e = part[:, first + h : first + h + 1] - rows[h : h + 1] + causal_bias
                if two_way:
                    at = heads + first + h
                    back = erows[h : h + 1] - part[:, at : at + 1] + anti_bias
                    e = jnp.maximum(e, back)
                mixes.append(low(jnp.exp(e) * products))
            x_pair = xd[:, pair * 128 : pair * 128 + 128]
            zero = jnp.zeros_like(x_pair)
            blocks = jnp.concatenate(
                [jnp.where(lane_low, x_pair, zero), jnp.where(lane_low, zero, x_pair)], axis=0
            )
            parts.append(dot(jnp.concatenate(mixes, axis=1), blocks))
        out_ref[rows_of(c), :] = (total + jnp.concatenate(parts, axis=1)).astype(out_ref.dtype)
        weight = split_dot(beyond, by_cum)
        xw = low(xd.astype(F32) * weight)
        state_ref[...] = state_ref[...] * entering[Q - 1 : Q] + dot(b_mat, xw, TN)
        return 0

    lax.fori_loop(0, anti, lambda c, _: chunk_body(c, True), 0, unroll=4)
    if chunks > anti:
        lax.fori_loop(anti, chunks, lambda c, _: chunk_body(c, False), 0, unroll=4)


def scan_forward(prefix, x_pre, taps, skip, cols, rows, act, group, out):
    length, channels = x_pre.shape
    anti = min(MAX_PREFIX // Q, length // Q)
    given = [prefix, x_pre, taps, skip, cols, rows, act]
    in_specs = [
        pl.BlockSpec(memory_space=pltpu.SMEM),
        pl.BlockSpec((length, CG), lambda g: (0, group)),
        pl.BlockSpec((4, CG), lambda g: (0, group)),
        pl.BlockSpec((1, CG), lambda g: (0, group)),
        pl.BlockSpec((length, 128), lambda g: (0, 0)),
        pl.BlockSpec((128, length), lambda g: (0, 0)),
        pl.BlockSpec((length, 2 * N), lambda g: (0, 0)),
    ]
    aliases = {}
    if out is not None:
        aliases = {len(given): 0}
        given.append(out)
        in_specs.append(pl.BlockSpec(memory_space=pl.ANY))
    return pl.pallas_call(
        functools.partial(forward_kernel, channels // P_SIZE, group * HG),
        grid=(1,),
        in_specs=in_specs,
        out_specs=[
            pl.BlockSpec((length, CG), lambda g: (0, group)),
            pl.BlockSpec((length // Q, N, CG), lambda g: (0, 0, 0)),
        ],
        out_shape=(
            jax.ShapeDtypeStruct((length, channels), BF16),
            jax.ShapeDtypeStruct((length // Q, N, CG), BF16),
        ),
        input_output_aliases=aliases,
        scratch_shapes=[
            pltpu.VMEM((length, CG), BF16),
            pltpu.VMEM((length, CG), F32),
            pltpu.VMEM((anti, N, CG), BF16),
            pltpu.VMEM((N, CG), F32),
        ],
        compiler_params=pltpu.CompilerParams(vmem_limit_bytes=40 * MIB),
        cost_estimate=NO_COST,
        name="scan_forward",
    )(*given)


def backward_kernel(
    heads,
    first,
    more,
    prefix_ref,
    x_ref,
    dy_scr,
    taps_ref,
    skip_ref,
    cols_ref,
    rows_ref,
    act_ref,
    states_scr,
    *refs,
):
    (
        gx_ref,
        gact_ref,
        gcols_ref,
        grows_ref,
        gsum_ref,
        x_scr,
        slope_scr,
        dback_scr,
        state_ref,
        dstate_ref,
        next_scr,
    ) = refs[-11:]
    length, width = x_ref.shape
    chunks = length // Q
    anti = min(MAX_PREFIX // Q, chunks)
    prefix = prefix_ref[0]
    taps = taps_ref[...].astype(F32)
    skip = skip_ref[...]
    by_cum = spread_matrix(first, width)
    by_ecum = spread_matrix(heads + first, width)
    by_step = spread_matrix(2 * heads + first, width)
    collect = gather_matrix(first, width)
    lane_low = iota((1, 128), 1) < P_SIZE

    gsum_ref[...] = jnp.zeros_like(gsum_ref)
    state_ref[...] = jnp.zeros_like(state_ref)

    def stage_a(c, two_way):
        conv = conv_of(shifted_rows(x_ref, c), taps)
        s = sig(conv)
        x = conv * s
        x_scr[rows_of(c), :] = x
        slope_scr[rows_of(c), :] = s + x * (1.0 - s)
        dy = dy_scr[rows_of(c), :].astype(F32)
        gsum_ref[4:5, :] += jnp.sum(dy * x, axis=0, keepdims=True)
        if two_way:
            within, beyond = growths(cols_ref[rows_of(c), :], heads)
            grow = split_dot(within[Q - 8 :], by_cum)[7:8]
            leaving = split_dot(beyond, by_ecum)
            c_mat = act_ref[rows_of(c), N : 2 * N]
            dback_scr[c + 1] = low(
                dback_scr[c].astype(F32) * grow + dot(c_mat, low(dy * leaving), TN)
            )
        return 0

    dback_scr[0] = jnp.zeros_like(dback_scr[0])
    lax.fori_loop(0, anti, lambda c, _: stage_a(c, True), 0, unroll=4)
    if chunks > anti:
        lax.fori_loop(anti, chunks, lambda c, _: stage_a(c, False), 0, unroll=4)

    state_ref[...] = jnp.zeros_like(state_ref)
    dstate_ref[...] = jnp.zeros_like(dstate_ref)
    next_scr[...] = jnp.zeros_like(next_scr)
    s_idx, t_idx = iota((Q, Q), 0), iota((Q, Q), 1)
    causal_bias = jnp.where(s_idx <= t_idx, 0.0, NEG).astype(F32)
    from_r = jnp.where(s_idx >= t_idx, 1.0, 0.0)
    upto_r = jnp.where(s_idx <= t_idx, 1.0, 0.0)
    zero_q = jnp.zeros((Q, Q), F32)

    def twice(m):
        return low(
            jnp.concatenate(
                [jnp.concatenate([m, zero_q], axis=1), jnp.concatenate([zero_q, m], axis=1)], axis=0
            )
        )

    from_pair, upto_pair = twice(from_r), twice(upto_r)
    pair_s, pair_r = iota((Q, 2 * Q), 0), iota((Q, 2 * Q), 1) % Q
    before_pair = pair_s < pair_r
    after_pair = pair_s > pair_r
    sum_from = jnp.where(t_idx >= s_idx, 1.0, 0.0).astype(BF16)
    sum_before = jnp.where(t_idx < s_idx, 1.0, 0.0).astype(BF16)
    sum_upto = jnp.where(t_idx <= s_idx, 1.0, 0.0).astype(BF16)
    sum_after = jnp.where(t_idx > s_idx, 1.0, 0.0).astype(BF16)
    sum_all = jnp.concatenate([sum_from, sum_before, sum_upto, sum_after], axis=1)

    def chunk_body(c, two_way):
        b_mat = act_ref[rows_of(c), 0:N]
        c_mat = act_ref[rows_of(c), N : 2 * N]
        products = dot(b_mat, c_mat, NT)
        part = cols_ref[rows_of(c), :]
        within, beyond = growths(part, heads)
        rows = rows_ref[first : first + HG, rows_of(c)]
        erows = rows_ref[heads + first : heads + first + HG, rows_of(c)]
        x = x_scr[rows_of(c), :]
        dy_low = dy_scr[rows_of(c), :]
        dy = dy_low.astype(F32)
        step_wide = split_dot(part, by_step)
        xd = x * step_wide
        xd_low = low(xd)
        if two_way:
            anti_bias = jnp.where((s_idx > t_idx) & (s_idx + c * Q < prefix), 0.0, NEG).astype(F32)
        dprod = jnp.zeros((Q, Q), F32)
        parts, inner = [], []
        for pair in range(HG // 2):
            lanes = slice(pair * 128, pair * 128 + 128)
            dy_pair = dy_low[:, lanes]
            zero = jnp.zeros_like(dy_pair)
            blocks = jnp.concatenate(
                [jnp.where(lane_low, dy_pair, zero), jnp.where(lane_low, zero, dy_pair)], axis=0
            )
            dmix = dot(xd_low[:, lanes], blocks, NT)
            mixes, moved = [], []
            for k in (0, 1):
                h = 2 * pair + k
                e = rows[h : h + 1] - part[:, first + h : first + h + 1] + causal_bias
                if two_way:
                    at = heads + first + h
                    back = part[:, at : at + 1] - erows[h : h + 1] + anti_bias
                    e = jnp.maximum(e, back)
                decay = jnp.exp(e)
                slab = dmix[:, k * Q : k * Q + Q] * decay
                dprod = dprod + slab
                mixes.append(low(decay * products))
                moved.append(low(slab * products))
            parts.append(dot(jnp.concatenate(mixes, axis=1), blocks))
            both = jnp.concatenate(moved, axis=1)
            crossing = jnp.where(before_pair, dot(both, from_pair), 0.0)
            if two_way:
                crossing = jnp.where(after_pair, dot(both, upto_pair), crossing)
            inner.append(jnp.sum(crossing, axis=0, keepdims=True))
        for pair in range(HG // 2):
            for k in (0, 1):
                h = 2 * pair + k
                grows_ref[0, h : h + 1, rows_of(c)] = inner[pair][:, k * Q : k * Q + Q]

        entering = split_dot(within, by_cum)
        to_last = split_dot(beyond, by_cum)
        grow = entering[Q - 1 : Q]
        dstate_low = low(dstate_ref[...])
        state_in = states_scr[c]
        du_carry = dot(b_mat, dstate_low) * to_last
        du = jnp.concatenate(parts, axis=1) + du_carry
        y_in = dot(c_mat, state_in) * entering
        dy_in = low(dy * entering)
        x_out = low(xd * to_last)
        d_c = dot(low(dprod), b_mat, TN) + dot(dy_in, state_in, NT)
        d_b = dot(low(dprod), c_mat) + dot(x_out, dstate_low, NT)
        moved_by = [low(dy * y_in), low(xd * du_carry)]
        across = jnp.sum(dstate_ref[...] * state_in.astype(F32), axis=0, keepdims=True) * grow
        if two_way:
            back_state = state_ref[...]
            back_low = low(back_state)
            dback_low = dback_scr[c]
            leaving = split_dot(beyond, by_ecum)
            from_first = split_dot(within * prefix_column(prefix, c), by_ecum)
            du_back = dot(b_mat, dback_low) * from_first
            du = du + du_back
            y_back = dot(c_mat, back_low) * leaving
            x_back = low(xd * from_first)
            d_c = d_c + dot(low(dy * leaving), back_low, NT)
            d_b = d_b + dot(x_back, dback_low, NT)
            moved_by = moved_by + [low(dy * y_back), low(xd * du_back)]
            across = across + grow * jnp.sum(
                dback_low.astype(F32) * back_state, axis=0, keepdims=True
            )
            state_ref[...] = back_state * grow + dot(b_mat, x_back, TN)
        dstate_ref[...] = dstate_ref[...] * grow + dot(c_mat, dy_in, TN)
        d_bc = jnp.concatenate([d_b, d_c], axis=1)
        summed = dot(sum_all if two_way else sum_all[:, : 2 * Q], jnp.concatenate(moved_by, axis=0))
        qk = dot(low(summed), collect)
        direct = dot(low(x * du), collect)
        across8 = low_pair_dot(jnp.broadcast_to(across, (8, width)), collect)
        d_cols = jnp.concatenate([direct, qk + across8[0:1]], axis=1)
        if more:
            d_bc = d_bc + refs[0][rows_of(c), :]
            d_cols = d_cols + refs[1][rows_of(c), :]
        gact_ref[rows_of(c), :] = d_bc
        gcols_ref[rows_of(c), :] = d_cols

        dconv = (du * step_wide + skip * dy) * slope_scr[rows_of(c), :]
        shifted = shifted_rows(x_ref, c)
        both = jnp.concatenate([dconv, next_scr[...]], axis=0)
        gx = taps[3:4] * dconv
        gsum_ref[3:4, :] += jnp.sum(dconv * shifted[0], axis=0, keepdims=True)
        for j in (1, 2, 3):
            gx = gx + taps[3 - j : 4 - j] * pltpu.roll(both, Q + 8 - j, 0)[:Q]
            gsum_ref[3 - j : 4 - j, :] += jnp.sum(dconv * shifted[j], axis=0, keepdims=True)
        gx_ref[rows_of(c), :] = low(gx)
        next_scr[...] = dconv[0:8]
        return 0

    if chunks > anti:
        lax.fori_loop(0, chunks - anti, lambda i, _: chunk_body(chunks - 1 - i, False), 0, unroll=4)
    lax.fori_loop(0, anti, lambda i, _: chunk_body(anti - 1 - i, True), 0, unroll=4)


def scan_backward(prefix, x_pre, grad_ssd, taps, skip, cols, rows, act, states, group, place, places, gx, before):
    length, channels = x_pre.shape
    chunks = length // Q
    anti = min(MAX_PREFIX // Q, chunks)
    wide = pl.BlockSpec((length, CG), lambda i: (0, group))
    given = [prefix, x_pre, grad_ssd, taps, skip, cols, rows, act, states]
    in_specs = [
        pl.BlockSpec(memory_space=pltpu.SMEM),
        wide,
        wide,
        pl.BlockSpec((4, CG), lambda i: (0, group)),
        pl.BlockSpec((1, CG), lambda i: (0, group)),
        pl.BlockSpec((length, 128), lambda i: (0, 0)),
        pl.BlockSpec((128, length), lambda i: (0, 0)),
        pl.BlockSpec((length, 2 * N), lambda i: (0, 0)),
        pl.BlockSpec((chunks, N, CG), lambda i: (0, 0, 0)),
    ]
    aliases = {}
    if before is not None:
        given += list(before)
        in_specs += [
            pl.BlockSpec((length, 2 * N), lambda i: (0, 0)),
            pl.BlockSpec((length, 256), lambda i: (0, 0)),
        ]
        aliases = {len(given) - 2: 1, len(given) - 1: 2}
    if gx is not None:
        aliases[len(given)] = 0
        given.append(gx)
        in_specs.append(pl.BlockSpec(memory_space=pl.ANY))
    return pl.pallas_call(
        functools.partial(backward_kernel, channels // P_SIZE, group * HG, before is not None),
        grid=(1,),
        in_specs=in_specs,
        out_specs=[
            pl.BlockSpec((length, CG), lambda i: (0, place)),
            pl.BlockSpec((length, 2 * N), lambda i: (0, 0)),
            pl.BlockSpec((length, 256), lambda i: (0, 0)),
            pl.BlockSpec((1, HG, length), lambda i: (0, 0, 0)),
            pl.BlockSpec((8, CG), lambda i: (0, 0)),
        ],
        out_shape=(
            jax.ShapeDtypeStruct((length, places * CG), BF16),
            jax.ShapeDtypeStruct((length, 2 * N), F32),
            jax.ShapeDtypeStruct((length, 256), F32),
            jax.ShapeDtypeStruct((1, HG, length), F32),
            jax.ShapeDtypeStruct((8, CG), F32),
        ),
        input_output_aliases=aliases,
        scratch_shapes=[
            pltpu.VMEM((length, CG), F32),
            pltpu.VMEM((length, CG), F32),
            pltpu.VMEM((anti + 1, N, CG), BF16),
            pltpu.VMEM((N, CG), F32),
            pltpu.VMEM((N, CG), F32),
            pltpu.VMEM((8, CG), F32),
        ],
        compiler_params=pltpu.CompilerParams(vmem_limit_bytes=40 * MIB),
        cost_estimate=NO_COST,
        name="scan_backward",
    )(*given)


TILE = 128


def block_of(lanes_ref, j):
    return pl.ds(pl.multiple_of(lanes_ref[j] * 128, 128), 128)


def place_kernel(normalize, count, tiles, lanes_ref, slots_ref, *refs):
    sources, by_ref, out_ref = refs[:count], refs[count], refs[count + 1]
    width = out_ref.shape[1]
    for k in range(count):

        @pl.when(pl.program_id(0) // tiles == k)
        def _(ref=sources[k]):
            if normalize:
                wide = ref[...].astype(F32)
                inv = lax.rsqrt(jnp.sum(wide * wide, axis=-1, keepdims=True) / width + EPSILON)
            else:
                inv = by_ref[...]
            for j in range(width // 128):
                there = block_of(lanes_ref, j)
                v = ref[:, there].astype(F32) * inv
                if normalize:
                    v = v * by_ref[:, there]
                out_ref[:, j * 128 : j * 128 + 128] = low(v)


def place_tokens(lanes, slots, sources, by, normalize):
    tokens, width = sources[0].shape
    count, tiles = len(sources), tokens // TILE

    def source(k):
        return pl.BlockSpec((TILE, width), lambda i, a, s: (jnp.clip(i - k * tiles, 0, tiles - 1), 0))

    def placed(i, a, s):
        return (s[i // tiles] * tiles + i % tiles, 0)

    by_spec = pl.BlockSpec((1, width), lambda i, a, s: (0, 0)) if normalize else pl.BlockSpec((TILE, 1), placed)
    return pl.pallas_call(
        functools.partial(place_kernel, normalize, count, tiles),
        grid_spec=pltpu.PrefetchScalarGridSpec(
            num_scalar_prefetch=2,
            grid=(count * tiles,),
            in_specs=[source(k) for k in range(count)] + [by_spec],
            out_specs=pl.BlockSpec((TILE, width), placed),
        ),
        out_shape=jax.ShapeDtypeStruct((tokens * count, width), BF16),
        compiler_params=pltpu.CompilerParams(vmem_limit_bytes=32 * MIB),
        cost_estimate=NO_COST,
        name="place_tokens",
    )(lanes, slots, *sources, by)


def half_sum(refs, j, per_half):
    here = slice((j % per_half) * 128, (j % per_half) * 128 + 128)
    side = refs[: len(refs) // 2] if j < per_half else refs[len(refs) // 2 :]
    total = side[0][:, here].astype(F32)
    for ref in side[1:]:
        total = total + ref[:, here].astype(F32)
    return total


def mixed_kernel(lanes_ref, slots_ref, hidden_ref, *refs):
    out_ref = refs[-1]
    blocks = hidden_ref.shape[1] // 128
    for j in range(blocks):
        there = block_of(lanes_ref, j)
        out_ref[:, there] = hidden_ref[:, there].astype(F32) + half_sum(refs[:-1], j, blocks // 2)


def finish_kernel(lanes_ref, slots_ref, hidden_ref, cot_ref, gain_ref, *refs):
    out_ref = refs[-1]
    width = hidden_ref.shape[1]
    blocks = width // 128
    wide = hidden_ref[...].astype(F32)
    inv = lax.rsqrt(jnp.sum(wide * wide, axis=-1, keepdims=True) / width + EPSILON)
    total = jnp.zeros((TILE, 128), F32)
    for j in range(blocks):
        there = block_of(lanes_ref, j)
        scaled = half_sum(refs[:-1], j, blocks // 2) * gain_ref[:, there]
        total = total + scaled * hidden_ref[:, there].astype(F32)
        out_ref[:, there] = scaled
    coef = inv * inv * inv * (jnp.sum(total, axis=-1, keepdims=True) / width)
    out_ref[...] = inv * out_ref[...] - wide * coef + cot_ref[...].astype(F32)


def own_rows(kernel, name, lanes, slots, hidden, more, gain, halves):
    tokens, width = hidden.shape
    tiles = tokens // TILE
    tile = pl.BlockSpec((TILE, width), lambda i, a, s: (i, 0))
    given, specs = [hidden, *more], [tile] * (1 + len(more))
    if gain is not None:
        given.append(gain)
        specs.append(pl.BlockSpec((1, width), lambda i, a, s: (0, 0)))
    for half in halves:
        for array, whole in half:
            given.append(array)
            if whole:
                specs.append(pl.BlockSpec((TILE, width // 2), lambda i, a, s: (s[0] * tiles + i, 0)))
            else:
                specs.append(pl.BlockSpec((TILE, width // 2), lambda i, a, s: (i, 0)))
    return pl.pallas_call(
        kernel,
        grid_spec=pltpu.PrefetchScalarGridSpec(
            num_scalar_prefetch=2, grid=(tiles,), in_specs=specs, out_specs=tile
        ),
        out_shape=jax.ShapeDtypeStruct((tokens, width), F32),
        compiler_params=pltpu.CompilerParams(vmem_limit_bytes=60 * MIB),
        cost_estimate=NO_COST,
        name=name,
    )(lanes, slots, *given)


def post_kernel(rest_ref, taps_ref, decay_ref, bias_ref, *refs):
    gbc_ref, gtaps_ref, ghead_ref, next_scr = refs[-4:]
    gact_ref, gcols_ref, grows = refs[0], refs[1], refs[2:-4]
    length, heads = rest_ref.shape[0], decay_ref.shape[1]
    chunks = length // Q
    taps = taps_ref[...]
    gtaps_ref[...] = jnp.zeros_like(gtaps_ref)
    ghead_ref[...] = jnp.zeros_like(ghead_ref)
    next_scr[...] = jnp.zeros_like(next_scr)
    filler = jnp.zeros((1, 128 - heads), F32)
    growth = -jnp.exp(jnp.concatenate([decay_ref[...], filler], axis=1))
    bias = jnp.concatenate([bias_ref[...], filler], axis=1)

    def body(i, _):
        c = chunks - 1 - i
        shifted = shifted_rows(rest_ref, c, 2 * N)
        conv = conv_of(shifted, taps)
        s = sig(conv)
        dconv = gact_ref[rows_of(c), :] * (s + conv * s * (1.0 - s))
        both = jnp.concatenate([dconv, next_scr[...]], axis=0)
        g = taps[3:4] * dconv
        gtaps_ref[3:4, :] += jnp.sum(dconv * shifted[0], axis=0, keepdims=True)
        for j in (1, 2, 3):
            g = g + taps[3 - j : 4 - j] * pltpu.roll(both, Q + 8 - j, 0)[:Q]
            gtaps_ref[3 - j : 4 - j, :] += jnp.sum(dconv * shifted[j], axis=0, keepdims=True)
        gbc_ref[rows_of(c), 0 : 2 * N] = low(g)
        next_scr[...] = dconv[0:8]

        direct, moved = gcols_ref[rows_of(c), 0:128], gcols_ref[rows_of(c), 128:256]
        inner = [ref[0, :, rows_of(c)] for ref in grows]
        inner.append(jnp.zeros((128 - heads, Q), F32))
        moved = moved + jnp.concatenate(inner, axis=0).T
        raw = rest_ref[rows_of(c), 2 * N :] + bias
        step = jnp.maximum(raw, 0.0) + jnp.log(1.0 + jnp.exp(-jnp.abs(raw)))
        gdt = (direct + moved * growth) * sig(raw)
        gbc_ref[rows_of(c), 2 * N :] = low(gdt[:, 0:heads])
        ghead_ref[0:1, :] += jnp.sum(moved * growth * step, axis=0, keepdims=True)
        ghead_ref[1:2, :] += jnp.sum(gdt, axis=0, keepdims=True)
        return 0

    lax.fori_loop(0, chunks, body, 0, unroll=4)


def post(rest_pre, bc_taps, log_decay, dt_bias, grad_act, gcols, grows):
    length, heads = rest_pre.shape[0], log_decay.shape[0]
    return pl.pallas_call(
        post_kernel,
        out_shape=(
            jax.ShapeDtypeStruct((length, 2 * N + heads), BF16),
            jax.ShapeDtypeStruct((8, 2 * N), F32),
            jax.ShapeDtypeStruct((8, 128), F32),
        ),
        scratch_shapes=[pltpu.VMEM((8, 2 * N), F32)],
        compiler_params=pltpu.CompilerParams(vmem_limit_bytes=40 * MIB),
        cost_estimate=NO_COST,
        name="post",
    )(rest_pre, bc_taps, log_decay[None], dt_bias[None], grad_act, gcols, *grows)


def gate_kernel(a_ref, other_ref, part_ref, ssd_ref, gain_ref, gate_ref, out_ref, square_ref):
    gain = gain_ref[...]

    @pl.when(pl.program_id(0) == 0)
    def _():
        square_ref[...] = jnp.zeros_like(square_ref)

    for m in range(0, a_ref.shape[0], 256):
        here = slice(m, m + 256)
        z = part_ref[here, :] + dot(a_ref[here, :], other_ref[...])
        gated = ssd_ref[here, :].astype(F32) * (z * sig(z))
        gate_ref[here, :] = low(z)
        out_ref[here, :] = low(gated * gain)
        square = gated * gated
        square_ref[here, :] += sum(square[:, k : k + 128] for k in range(0, CG, 128))


def gate_product(normed, other, part, ssd_out, gain):
    tokens, width = normed.shape
    channels = ssd_out.shape[1]
    tall = pl.BlockSpec((tokens, CG), lambda j: (0, j))
    deep = pl.BlockSpec((width // 2, CG), lambda j: (0, j))
    return pl.pallas_call(
        gate_kernel,
        grid=(channels // CG,),
        in_specs=[
            pl.BlockSpec((tokens, width // 2), lambda j: (0, 1)), deep, tall, tall, pl.BlockSpec((1, CG), lambda j: (0, j)),
        ],
        out_specs=[tall, tall, pl.BlockSpec((tokens, 128), lambda j: (0, 0))],
        out_shape=(
            jax.ShapeDtypeStruct((tokens, channels), BF16),
            jax.ShapeDtypeStruct((tokens, channels), BF16),
            jax.ShapeDtypeStruct((tokens, 128), F32),
        ),
        compiler_params=pltpu.CompilerParams(vmem_limit_bytes=40 * MIB),
        cost_estimate=NO_COST,
        name="gate_product",
    )(normed, other, part, ssd_out, gain)


def gating_kernel(a_ref, own_ref, other_ref, gate_ref, ssd_ref, coef_ref, gain_ref, ggate_ref, dy_ref):
    depth = own_ref.shape[0]
    gain = gain_ref[...]
    for m in range(0, a_ref.shape[0], 256):
        here = slice(m, m + 256)
        scaled = dot(a_ref[here, :depth], own_ref[...]) + dot(a_ref[here, depth:], other_ref[...])
        z = gate_ref[here, :].astype(F32)
        y = ssd_ref[here, :].astype(F32)
        s = sig(z)
        act = z * s
        grad = gain * scaled - y * act * coef_ref[here, :]
        ggate_ref[here, :] = low(grad * y * (s + act * (1.0 - s)))
        dy_ref[here, :] = low(grad * act)


def gating_product(cot, own, other, gate, ssd_out, coef, gain):
    tokens, width = cot.shape
    channels = ssd_out.shape[1]
    tall = pl.BlockSpec((tokens, CG), lambda j: (0, j))
    deep = pl.BlockSpec((width // 2, CG), lambda j: (0, j))
    return pl.pallas_call(
        gating_kernel,
        grid=(channels // CG,),
        in_specs=[
            pl.BlockSpec((tokens, width), lambda j: (0, 0)), deep, deep, tall, tall,
            pl.BlockSpec((tokens, 1), lambda j: (0, 0)), pl.BlockSpec((1, CG), lambda j: (0, j)),
        ],
        out_specs=[tall, tall],
        out_shape=(
            jax.ShapeDtypeStruct((tokens, channels), BF16),
            jax.ShapeDtypeStruct((tokens, channels), BF16),
        ),
        compiler_params=pltpu.CompilerParams(vmem_limit_bytes=40 * MIB),
        cost_estimate=NO_COST,
        name="gating_product",
    )(cot, own, other, gate, ssd_out, coef, gain)


def snake(devices):
    half = devices // 4
    return [z * 2 for z in range(half)] + [z * 2 + 1 for z in reversed(range(half))]


def chip_groups(devices):
    return [[chip * 2 + core for chip in snake(devices)] for core in (0, 1)]


def other_core(v, devices):
    return lax.ppermute(v, "fsdp", [(i, i ^ 1) for i in range(devices)])


def other_half(v):
    return lax.ppermute(v, "tp", [(0, 1), (1, 0)])


def tie(first, second):
    return lax.optimization_barrier((first, second))


def gather(v, devices):
    return lax.all_gather(v, "fsdp", axis=0, tiled=True, axis_index_groups=chip_groups(devices))


def doubling_gather(v, devices):
    me = lax.axis_index("fsdp")
    bit = 1
    while bit < devices:
        came = lax.ppermute(v, "fsdp", [(i, i ^ bit) for i in range(devices)])
        mine_first = me & bit == 0
        v = jnp.concatenate([jnp.where(mine_first, v, came), jnp.where(mine_first, came, v)], axis=0)
        bit *= 2
    return v


def scatter(v, devices):
    return lax.psum_scatter(
        v, "fsdp", scatter_dimension=0, tiled=True, axis_index_groups=chip_groups(devices)
    )


def on_device(
    hidden,
    cotangent,
    prefix,
    input_norm_gain,
    z_weight,
    x_weight,
    bc_weight,
    dt_weight,
    x_conv,
    bc_conv,
    log_decay,
    dt_bias,
    skip_gain,
    gate_gain,
    out_weight,
):
    fsdp = lax.axis_size("fsdp")
    tp = lax.axis_size("tp")
    own_tokens, width = hidden.shape
    heads = log_decay.shape[0]
    channels = heads * P_SIZE
    all_channels = channels * tp
    groups = channels // CG
    taps_own = x_conv.shape[2]
    rows = width // fsdp
    ring = fsdp // 2
    half_width = width // 2

    order = snake(fsdp)
    core = lax.axis_index("fsdp") % 2
    line = jnp.array(order, jnp.int32)
    blocks = jnp.concatenate([line * 2 + core, line * 2 + 1 - core])
    direct = rows % 128 == 0
    per = max(rows // 128, 1)
    if direct:
        lanes = (blocks[:, None] * per + jnp.arange(per)[None]).reshape(-1)
    else:
        lanes = jnp.arange(width // 128)
    lanes = lanes.astype(jnp.int32)

    def to_cores(v):
        zero = jnp.stack([v[2 * chip] for chip in order])
        one = jnp.stack([v[2 * chip + 1] for chip in order])
        return jnp.where(core == 0, zero, one), jnp.where(core == 0, one, zero)

    def to_ring(v):
        return v if direct else v.reshape(-1, fsdp, rows)[:, blocks].reshape(v.shape)

    def from_ring(v):
        if direct:
            return v
        return v.reshape(-1, fsdp, rows)[:, jnp.argsort(blocks)].reshape(v.shape)

    small = jnp.concatenate(
        [input_norm_gain.reshape(-1), x_conv.reshape(-1), bc_conv.reshape(-1), gate_gain.reshape(-1)]
    )
    sizes = [input_norm_gain.size, x_conv.size, bc_conv.size, gate_gain.size]
    cuts = [0]
    for size in sizes:
        cuts.append(cuts[-1] + size)
    small_all = doubling_gather(jnp.pad(small, (0, -small.size % 128))[None], fsdp)
    payload = jnp.concatenate([x_weight, bc_weight, dt_weight, dt_weight, dt_weight], axis=1)
    payload = jnp.pad(payload, ((0, 0), (0, 128 - 3 * heads)))

    if tp == 2:
        mine = lax.axis_index("tp").astype(jnp.int32)
        slots = jnp.stack([mine, 1 - mine])
        hidden_other = other_half(hidden)
        cot_given, hidden_other = tie(cotangent, hidden_other)
        hidden_parts = [hidden, hidden_other]
        cot_parts = [cotangent, other_half(cot_given)]
    else:
        slots = jnp.zeros((2,), jnp.int32)
        hidden_parts = [lax.all_gather(hidden, "tp", axis=0, tiled=True)]
        cot_parts = [lax.all_gather(cotangent, "tp", axis=0, tiled=True)]
    hidden_parts = [to_ring(v) for v in hidden_parts]
    cot_parts = [to_ring(v) for v in cot_parts]

    norm_gain = small_all[:, cuts[0] : cuts[1]].reshape(1, -1).astype(F32)
    x_taps = small_all[:, cuts[1] : cuts[2]].reshape(fsdp, heads, 4, taps_own)
    x_taps = jnp.transpose(x_taps, (2, 1, 0, 3)).reshape(4, channels).astype(F32)
    bc_taps = small_all[:, cuts[2] : cuts[3]].reshape(fsdp, 4, -1)
    bc_taps = jnp.transpose(bc_taps, (1, 0, 2)).reshape(4, 2 * N).astype(F32)
    gain = small_all[:, cuts[3] : cuts[4]].reshape(fsdp, heads, -1)
    gain = jnp.transpose(gain, (1, 0, 2)).reshape(1, channels).astype(F32)
    skip = jnp.repeat(skip_gain, P_SIZE)[None]
    hidden_parts[-1], (norm_gain, x_taps, bc_taps, gain, skip) = tie(
        hidden_parts[-1], (norm_gain, x_taps, bc_taps, gain, skip)
    )

    def over_tp(v):
        return v + other_half(v) if tp == 2 else lax.psum(v, "tp")

    x_own = gather(payload, fsdp)
    z_own = gather(z_weight, fsdp)
    out_own = gather(out_weight.T, fsdp)
    x_own, hidden_parts[-1] = tie(x_own, hidden_parts[-1])
    x_other = other_core(x_own, fsdp)

    norm_gain = to_ring(norm_gain)
    normed = place_tokens(lanes, slots, hidden_parts, norm_gain, True)
    na, nb = normed[:, :half_width], normed[:, half_width:]
    few = slice(channels, channels + 2 * N + 128)
    rest_pre = dot(na, x_own[:, few]) + dot(nb, x_other[:, few])
    rest = slice(channels, channels + 2 * N + heads)
    rest_own, rest_other = x_own[:, rest], x_other[:, rest]
    act, cols, head_rows = prep(rest_pre, bc_taps, log_decay, dt_bias)
    x_pre = low(dot(na, x_own[:, :channels]) + dot(nb, x_other[:, :channels]))
    ssd_out, states = None, []
    for g in range(groups):
        ssd_out, kept = scan_forward(prefix, x_pre, x_taps, skip, cols, head_rows, act, g, ssd_out)
        states.append(kept)
    (z_own, cot_parts[-1]), ssd_out = tie((z_own, cot_parts[-1]), ssd_out)
    z_other = other_core(z_own, fsdp)

    part = lax.optimization_barrier(dot(na, z_own))
    gate_low, scaled_out, square = gate_product(normed, z_other, part, ssd_out, gain)
    square_sum = over_tp(jnp.sum(square, axis=-1))

    inv_gate = lax.rsqrt(square_sum / all_channels + EPSILON)[:, None]
    cot_rel = place_tokens(lanes, slots, cot_parts, inv_gate, False)
    ca, cb = cot_rel[:, :half_width], cot_rel[:, half_width:]
    gout_other = low(dot(cb, scaled_out, TN))
    gout_came = other_core(gout_other, fsdp)
    gout_sum = low(dot(ca, scaled_out, TN) + gout_came.astype(F32))
    (scaled_out, out_own), gout_sum = tie((scaled_out, out_own), gout_sum)
    grad_out = scatter(gout_sum, fsdp)
    out_other = other_core(out_own, fsdp)

    branch, along = [], 0.0
    for cot_half, out_half in ((ca, out_own), (cb, out_other)):
        v = dot(scaled_out, out_half, NT)
        along = along + jnp.sum(v * cot_half.astype(F32), axis=-1)
        branch.append(low(v * inv_gate))
    along = over_tp(along)
    coef = inv_gate * inv_gate * (along / all_channels)[:, None]
    coef, branch = tie(coef, branch)

    def to_own_tokens(v):
        if tp == 2:
            leaving = lax.dynamic_slice_in_dim(v, (1 - mine) * own_tokens, own_tokens, 0)
            return [(v, True), (other_half(leaving), False)]
        return [(lax.psum_scatter(v, "tp", scatter_dimension=0, tiled=True), False)]

    branch_parts = [to_own_tokens(v) for v in branch]
    kinds = [[whole for _, whole in half] for half in branch_parts]
    branch_parts = [[v for v, _ in half] for half in branch_parts]

    ggate, dy = gating_product(cot_rel, out_own, out_other, gate_low, ssd_out, coef, gain)
    gz_came = other_core(low(dot(nb, ggate, TN)), fsdp)
    z_parts = [dot(ggate, z_own, NT), dot(ggate, z_other, NT)]
    normed, z_parts = tie(normed, z_parts)
    na, nb = normed[:, :half_width], normed[:, half_width:]
    gz_sum = low(dot(na, ggate, TN) + gz_came.astype(F32))
    dy, gz_sum = tie(dy, gz_sum)
    grad_z = scatter(gz_sum, fsdp)

    grows, gsums = [], []
    first = groups * 3 // 4
    before = None

    def back_through(start, stop, dy, before):
        gx = None
        for g in range(start, stop):
            gx, gact, gcol, grow, gsum = scan_backward(
                prefix, x_pre, dy, x_taps, skip, cols, head_rows, act, states[g], g, g - start, stop - start, gx, before
            )
            before = (gact, gcol)
            grows.append(grow)
            gsums.append(gsum)
        return gx, before

    grad_x = []
    if first:
        gx, before = back_through(0, first, dy, before)
        gx, (branch_parts, grad_out, grad_z) = tie(gx, (branch_parts, grad_out, grad_z))
        came = other_core(low(dot(nb, gx, TN)), fsdp)
        z_parts = [
            v + dot(gx, half[:, : first * CG], NT) for v, half in zip(z_parts, (x_own, x_other))
        ]
        normed, z_parts = tie(normed, z_parts)
        na, nb = normed[:, :half_width], normed[:, half_width:]
        total = low(dot(na, gx, TN) + came.astype(F32))
        dy, total = tie(dy, total)
        grad_x.append(scatter(total, fsdp))
    gx, before = back_through(first, groups, dy, before)
    if not first:
        gx, grad_z = tie(gx, grad_z)
    g_gain = jnp.sum(out_weight.T.astype(F32) * grad_out.astype(F32), axis=0) / gain[0]
    g_gain = jnp.transpose(g_gain.reshape(heads, fsdp, -1), (1, 0, 2))
    late = slice(first * CG, channels)
    grest, gbc_taps, ghead = post(rest_pre, bc_taps, log_decay, dt_bias, before[0], before[1], grows)

    gsum = jnp.concatenate(gsums, axis=1)
    gx_taps = jnp.transpose(gsum[0:4].reshape(4, heads, fsdp, taps_own), (2, 1, 0, 3))
    g_taps = jnp.transpose(gbc_taps[0:4].reshape(4, fsdp, -1), (1, 0, 2))
    g_skip = jnp.sum(gsum[4].reshape(heads, P_SIZE), axis=-1)
    per_head = jnp.concatenate([ghead[0, :heads], ghead[1, :heads], g_skip])
    slices = jnp.concatenate(
        [
            g_taps.reshape(fsdp, -1),
            gx_taps.reshape(fsdp, -1),
            g_gain.reshape(fsdp, -1),
            jnp.broadcast_to(per_head[None], (fsdp, per_head.size)),
        ],
        axis=1,
    )
    size = slices.shape[1]
    lone = -(-size // rows)
    lines_own, lines_other = [
        jnp.pad(v, ((0, 0), (0, lone * rows - size))).reshape(half_width, lone) for v in to_cores(slices)
    ]
    rest_leaves = jnp.concatenate([dot(nb, grest, TN), lines_other], axis=1)
    rest_came = other_core(rest_leaves, fsdp)
    gx, rest_leaves = tie(gx, rest_leaves)
    gx_other = low(dot(nb, gx, TN))
    came = other_core(gx_other, fsdp)
    (grest, gx), gx_other = tie((grest, gx), gx_other)
    rest_sum = jnp.concatenate([dot(na, grest, TN), lines_own], axis=1) + rest_came
    (grest, gx), (rest_sum, grad_x) = tie((grest, gx), (rest_sum, grad_x))
    mine_rest = scatter(rest_sum, fsdp)

    def first_part(v, x_half):
        return v + dot(gx, x_half[:, late], NT)

    part = low(first_part(z_parts[0], x_own) + dot(grest, rest_own, NT))
    part_sums = [to_own_tokens(part)]
    kinds_part = [whole for _, whole in part_sums[0]]
    gx, part = tie(gx, part)
    gx_sum = low(dot(na, gx, TN) + came.astype(F32))
    gx, gx_sum = tie(gx, gx_sum)
    grad_x.append(scatter(gx_sum, fsdp))
    second = first_part(z_parts[1], x_other)
    (branch_parts, grad_out, grad_z), part = tie((branch_parts, grad_out, grad_z), part)
    mixed = from_ring(
        own_rows(
            mixed_kernel, "add_branch", lanes, slots, to_ring(hidden), [], None,
            [list(zip(half, kind)) for half, kind in zip(branch_parts, kinds)],
        )
    )
    grad_z, grad_out = grad_z.astype(F32), grad_out.astype(F32).T
    arrived = [v for v, _ in part_sums[0]]
    second, (arrived, mixed, grad_out, grad_z, mine_rest) = tie(
        second, (arrived, mixed, grad_out, grad_z, mine_rest)
    )
    part_sums[0] = list(zip(arrived, kinds_part))
    part_sums.append(to_own_tokens(low(second + dot(grest, rest_other, NT))))

    grad_bc, grad_dt = mine_rest[:, : 2 * N], mine_rest[:, 2 * N : 2 * N + heads]
    lines = mine_rest[:, 2 * N + heads :].reshape(-1)
    n_taps, bc_size = bc_conv.size, rows * 2 * N
    at = [n_taps]
    for size in (x_conv.size, gate_gain.size, heads, heads, heads):
        at.append(at[-1] + size)
    gx_taps = lines[at[0] : at[1]].reshape(x_conv.shape)
    g_gain = lines[at[1] : at[2]].reshape(gate_gain.shape)
    g_decay, g_bias, g_skip = [lines[at[k] : at[k + 1]] for k in (2, 3, 4)]

    def weighted(w, g):
        return jnp.sum(w.astype(F32) * g.astype(F32), axis=1)

    grad_gain = weighted(z_weight, grad_z) + weighted(bc_weight, grad_bc) + weighted(dt_weight, grad_dt)
    last, whole = part_sums[1][-1]
    last, (mixed, grad_gain, grad_out, grad_z) = tie(last, (mixed, grad_gain, grad_out, grad_z))
    part_sums[1][-1] = (last, whole)
    grad_hidden = from_ring(
        own_rows(finish_kernel, "finish", lanes, slots, to_ring(hidden), [to_ring(cotangent)], norm_gain, part_sums)
    )
    grad_x = jnp.concatenate(grad_x, axis=1).astype(F32)
    grad_gain = (grad_gain + weighted(x_weight, grad_x)) / input_norm_gain.astype(F32)
    together = over_tp(jnp.concatenate([grad_bc.reshape(-1), lines[:n_taps], grad_gain]))
    grad_bc = together[:bc_size].reshape(rows, 2 * N)
    g_taps = together[bc_size : bc_size + n_taps].reshape(bc_conv.shape)
    grad_gain = together[bc_size + n_taps :]
    return (
        mixed, grad_hidden, grad_gain, grad_z, grad_x, grad_bc, grad_dt, gx_taps, g_taps, g_decay, g_bias,
        g_skip, g_gain, grad_out,
    )


def solution(mesh):
    both = P(("fsdp", "tp"), None)
    split = P("fsdp", "tp")
    ins = (
        both, both, P("fsdp"), P("fsdp"), split, split, P("fsdp", None), split, P("tp", None, "fsdp"),
        P(None, "fsdp"), P("tp"), P("tp"), P("tp"), P("tp", "fsdp"), P("tp", "fsdp"),
    )
    outs = (
        both, both, P("fsdp"), split, split, P("fsdp", None), split, P("tp", None, "fsdp"),
        P(None, "fsdp"), P("tp"), P("tp"), P("tp"), P("tp", "fsdp"), P("tp", "fsdp"),
    )
    return jax.shard_map(on_device, mesh=mesh, in_specs=ins, out_specs=outs, check_vma=False)
```

```python
import functools

import jax
import jax.numpy as jnp
from jax import lax
from jax.experimental import pallas as pl
from jax.experimental.pallas import tpu as pltpu
from jax.sharding import PartitionSpec as P

P_SIZE = 64
N = 128
Q = 128
HG = 8
CG = HG * P_SIZE
MAX_PREFIX = 512
EPSILON = 1e-05
F32 = jnp.float32
BF16 = jnp.bfloat16
NEG = -1e30
NN = ((1,), (0,))
NT = ((1,), (1,))
TN = ((0,), (0,))
MIB = 1024 * 1024
NO_COST = pl.CostEstimate(flops=0, bytes_accessed=0, transcendentals=0)


def dot(a, b, dims=NN):
    return lax.dot_general(a, b, (dims, ((), ())), preferred_element_type=F32)


def low(v):
    return v.astype(BF16)


def split_dot(v, e):
    hi = low(v)
    rest = low(v - hi.astype(F32))
    return dot(jnp.concatenate([hi, rest], axis=1), e)


def low_pair_dot(v, e):
    hi = low(v)
    return dot(hi, e) + dot(low(v - hi.astype(F32)), e)


def three_dot(e, v):
    hi = low(v)
    rest = v - hi.astype(F32)
    mid = low(rest)
    return dot(e, hi) + (dot(e, mid) + dot(e, low(rest - mid.astype(F32))))


def iota(shape, dim):
    return lax.broadcasted_iota(jnp.int32, shape, dim)


def sig(v):
    return 0.5 + 0.5 * jnp.tanh(0.5 * v)


def rows_of(c):
    return pl.ds(pl.multiple_of(c * Q, Q), Q)


def shifted_rows(x_ref, c, width=None):
    lanes = slice(0, width)
    cur = x_ref[rows_of(c), lanes].astype(F32)
    start = pl.multiple_of(jnp.maximum(c * Q - 16, 0), 16)
    before = x_ref[pl.ds(start, 16), lanes].astype(F32)[8:]
    before = jnp.where(c > 0, before, 0.0)
    both = jnp.concatenate([before, cur], axis=0)
    return [cur] + [pltpu.roll(both, j, 0)[8:] for j in (1, 2, 3)]


def conv_of(shifted, taps):
    total = taps[3:4] * shifted[0]
    for j in (1, 2, 3):
        total = total + taps[3 - j : 4 - j] * shifted[j]
    return total


def spread_matrix(start, width):
    return jnp.where(
        iota((256, width), 1) // P_SIZE + start == iota((256, width), 0) % 128, 1.0, 0.0
    ).astype(BF16)


def gather_matrix(start, width):
    return jnp.where(
        iota((width, 128), 0) // P_SIZE + start == iota((width, 128), 1), 1.0, 0.0
    ).astype(BF16)


def prep_kernel(rest_ref, taps_ref, decay_ref, bias_ref, act_ref, cols_ref, rows_ref):
    heads = decay_ref.shape[1]
    length = rest_ref.shape[0]
    taps = taps_ref[...]
    tri = jnp.where(iota((Q, Q), 0) >= iota((Q, Q), 1), 1.0, 0.0).astype(BF16)
    lane = iota((1, 128), 1)
    filler = jnp.zeros((1, 128 - 3 * heads), F32)
    decay = jnp.concatenate([decay_ref[...]] * 3 + [filler], axis=1)
    bias = jnp.concatenate([bias_ref[...]] * 3 + [filler], axis=1)
    growth = -jnp.exp(decay)

    def body(c, _):
        conv = conv_of(shifted_rows(rest_ref, c, 2 * N), taps)
        act_ref[rows_of(c), :] = low(conv * sig(conv))
        raw = rest_ref[rows_of(c), 2 * N :] + bias
        raw = jnp.where(lane < 3 * heads, raw, 0.0)
        step = jnp.maximum(raw, 0.0) + jnp.log(1.0 + jnp.exp(-jnp.abs(raw)))
        rate = growth * step
        cum = three_dot(tri, rate)
        packed = jnp.where(lane < heads, cum, jnp.where(lane < 2 * heads, cum - rate, step))
        packed = jnp.where(lane < 3 * heads, packed, 0.0)
        cols_ref[rows_of(c), :] = packed
        rows_ref[:, rows_of(c)] = packed.T
        return 0

    lax.fori_loop(0, length // Q, body, 0, unroll=4)


def prep(rest_pre, bc_taps, log_decay, dt_bias):
    length = rest_pre.shape[0]
    return pl.pallas_call(
        prep_kernel,
        out_shape=(
            jax.ShapeDtypeStruct((length, 2 * N), BF16),
            jax.ShapeDtypeStruct((length, 128), F32),
            jax.ShapeDtypeStruct((128, length), F32),
        ),
        compiler_params=pltpu.CompilerParams(vmem_limit_bytes=32 * MIB),
        cost_estimate=NO_COST,
        name="prep",
    )(rest_pre, bc_taps, log_decay[None], dt_bias[None])


def prefix_column(prefix, c):
    return jnp.where(iota((Q, 1), 0) + c * Q < prefix, 1.0, 0.0).astype(F32)


def growths(part, heads):
    lane = iota((1, 128), 1)
    used = lane < 2 * heads
    tail = part[Q - 8 :]
    last = jnp.where(lane < heads, tail, pltpu.roll(tail, heads, 1))[7:8]
    within = jnp.where(used, jnp.exp(jnp.where(used, part, 0.0)), 0.0)
    beyond = jnp.where(used, jnp.exp(jnp.where(used, last - part, 0.0)), 0.0)
    return within, beyond


def forward_kernel(
    heads, first, prefix_ref, x_ref, taps_ref, skip_ref, cols_ref, rows_ref, act_ref, *refs
):
    out_ref, states_ref, xd_ref, kept_ref, back_ref, state_ref = refs[-6:]
    length, width = x_ref.shape
    chunks = length // Q
    anti = min(MAX_PREFIX // Q, chunks)
    prefix = prefix_ref[0]
    taps = taps_ref[...].astype(F32)
    skip = skip_ref[...]
    by_cum = spread_matrix(first, width)
    by_ecum = spread_matrix(heads + first, width)
    by_step = spread_matrix(2 * heads + first, width)
    lane_low = iota((1, 128), 1) < P_SIZE

    def stage_a(c, _):
        conv = conv_of(shifted_rows(x_ref, c), taps)
        x = conv * sig(conv)
        xd_ref[rows_of(c), :] = low(x * split_dot(cols_ref[rows_of(c), :], by_step))
        kept_ref[rows_of(c), :] = x * skip
        return 0

    lax.fori_loop(0, chunks, stage_a, 0, unroll=4)

    state_ref[...] = jnp.zeros_like(state_ref)
    back_ref[anti - 1] = jnp.zeros_like(back_ref[anti - 1])
    for c in range(anti - 1, 0, -1):
        within, _ = growths(cols_ref[rows_of(c), :], heads)
        weight = split_dot(within * prefix_column(prefix, c), by_ecum)
        grow = split_dot(within[Q - 8 :], by_cum)[7:8]
        b_mat = act_ref[rows_of(c), 0:N]
        xw = low(xd_ref[rows_of(c), :].astype(F32) * weight)
        state_ref[...] = state_ref[...] * grow + dot(b_mat, xw, TN)
        back_ref[c - 1] = low(state_ref[...])

    state_ref[...] = jnp.zeros_like(state_ref)
    causal_bias = jnp.where(iota((Q, Q), 1) <= iota((Q, Q), 0), 0.0, NEG).astype(F32)

    def chunk_body(c, two_way):
        b_mat = act_ref[rows_of(c), 0:N]
        c_mat = act_ref[rows_of(c), N : 2 * N]
        products = dot(c_mat, b_mat, NT)
        part = cols_ref[rows_of(c), :]
        within, beyond = growths(part, heads)
        entering = split_dot(within, by_cum)
        state_low = low(state_ref[...])
        states_ref[c] = state_low
        total = kept_ref[rows_of(c), :] + dot(c_mat, state_low) * entering
        if two_way:
            leaving = split_dot(beyond, by_ecum)
            total = total + dot(c_mat, back_ref[c]) * leaving
            anti_bias = jnp.where(
                (iota((Q, Q), 1) > iota((Q, Q), 0)) & (iota((Q, Q), 1) + c * Q < prefix), 0.0, NEG
            ).astype(F32)
        xd = xd_ref[rows_of(c), :]
        rows = rows_ref[first : first + HG, rows_of(c)]
        erows = rows_ref[heads + first : heads + first + HG, rows_of(c)]
        parts = []
        for pair in range(HG // 2):
            mixes = []
            for h in (2 * pair, 2 * pair + 1):
                e = part[:, first + h : first + h + 1] - rows[h : h + 1] + causal_bias
                if two_way:
                    at = heads + first + h
                    back = erows[h : h + 1] - part[:, at : at + 1] + anti_bias
                    e = jnp.maximum(e, back)
                mixes.append(low(jnp.exp(e) * products))
            x_pair = xd[:, pair * 128 : pair * 128 + 128]
            zero = jnp.zeros_like(x_pair)
            blocks = jnp.concatenate(
                [jnp.where(lane_low, x_pair, zero), jnp.where(lane_low, zero, x_pair)], axis=0
            )
            parts.append(dot(jnp.concatenate(mixes, axis=1), blocks))
        out_ref[rows_of(c), :] = (total + jnp.concatenate(parts, axis=1)).astype(out_ref.dtype)
        weight = split_dot(beyond, by_cum)
        xw = low(xd.astype(F32) * weight)
        state_ref[...] = state_ref[...] * entering[Q - 1 : Q] + dot(b_mat, xw, TN)
        return 0

    lax.fori_loop(0, anti, lambda c, _: chunk_body(c, True), 0, unroll=4)
    if chunks > anti:
        lax.fori_loop(anti, chunks, lambda c, _: chunk_body(c, False), 0, unroll=4)


def scan_forward(prefix, x_pre, taps, skip, cols, rows, act, group, out):
    length, channels = x_pre.shape
    anti = min(MAX_PREFIX // Q, length // Q)
    given = [prefix, x_pre, taps, skip, cols, rows, act]
    in_specs = [
        pl.BlockSpec(memory_space=pltpu.SMEM),
        pl.BlockSpec((length, CG), lambda g: (0, group)),
        pl.BlockSpec((4, CG), lambda g: (0, group)),
        pl.BlockSpec((1, CG), lambda g: (0, group)),
        pl.BlockSpec((length, 128), lambda g: (0, 0)),
        pl.BlockSpec((128, length), lambda g: (0, 0)),
        pl.BlockSpec((length, 2 * N), lambda g: (0, 0)),
    ]
    aliases = {}
    if out is not None:
        aliases = {len(given): 0}
        given.append(out)
        in_specs.append(pl.BlockSpec(memory_space=pl.ANY))
    return pl.pallas_call(
        functools.partial(forward_kernel, channels // P_SIZE, group * HG),
        grid=(1,),
        in_specs=in_specs,
        out_specs=[
            pl.BlockSpec((length, CG), lambda g: (0, group)),
            pl.BlockSpec((length // Q, N, CG), lambda g: (0, 0, 0)),
        ],
        out_shape=(
            jax.ShapeDtypeStruct((length, channels), BF16),
            jax.ShapeDtypeStruct((length // Q, N, CG), BF16),
        ),
        input_output_aliases=aliases,
        scratch_shapes=[
            pltpu.VMEM((length, CG), BF16),
            pltpu.VMEM((length, CG), F32),
            pltpu.VMEM((anti, N, CG), BF16),
            pltpu.VMEM((N, CG), F32),
        ],
        compiler_params=pltpu.CompilerParams(vmem_limit_bytes=40 * MIB),
        cost_estimate=NO_COST,
        name="scan_forward",
    )(*given)


def backward_kernel(
    heads,
    first,
    more,
    prefix_ref,
    x_ref,
    dy_scr,
    taps_ref,
    skip_ref,
    cols_ref,
    rows_ref,
    act_ref,
    states_scr,
    *refs,
):
    (
        gx_ref,
        gact_ref,
        gcols_ref,
        grows_ref,
        gsum_ref,
        x_scr,
        slope_scr,
        dback_scr,
        state_ref,
        dstate_ref,
        next_scr,
    ) = refs[-11:]
    length, width = x_ref.shape
    chunks = length // Q
    anti = min(MAX_PREFIX // Q, chunks)
    prefix = prefix_ref[0]
    taps = taps_ref[...].astype(F32)
    skip = skip_ref[...]
    by_cum = spread_matrix(first, width)
    by_ecum = spread_matrix(heads + first, width)
    by_step = spread_matrix(2 * heads + first, width)
    collect = gather_matrix(first, width)
    lane_low = iota((1, 128), 1) < P_SIZE

    gsum_ref[...] = jnp.zeros_like(gsum_ref)
    state_ref[...] = jnp.zeros_like(state_ref)

    def stage_a(c, two_way):
        conv = conv_of(shifted_rows(x_ref, c), taps)
        s = sig(conv)
        x = conv * s
        x_scr[rows_of(c), :] = x
        slope_scr[rows_of(c), :] = s + x * (1.0 - s)
        dy = dy_scr[rows_of(c), :].astype(F32)
        gsum_ref[4:5, :] += jnp.sum(dy * x, axis=0, keepdims=True)
        if two_way:
            within, beyond = growths(cols_ref[rows_of(c), :], heads)
            grow = split_dot(within[Q - 8 :], by_cum)[7:8]
            leaving = split_dot(beyond, by_ecum)
            c_mat = act_ref[rows_of(c), N : 2 * N]
            dback_scr[c + 1] = low(
                dback_scr[c].astype(F32) * grow + dot(c_mat, low(dy * leaving), TN)
            )
        return 0

    dback_scr[0] = jnp.zeros_like(dback_scr[0])
    lax.fori_loop(0, anti, lambda c, _: stage_a(c, True), 0, unroll=4)
    if chunks > anti:
        lax.fori_loop(anti, chunks, lambda c, _: stage_a(c, False), 0, unroll=4)

    state_ref[...] = jnp.zeros_like(state_ref)
    dstate_ref[...] = jnp.zeros_like(dstate_ref)
    next_scr[...] = jnp.zeros_like(next_scr)
    s_idx, t_idx = iota((Q, Q), 0), iota((Q, Q), 1)
    causal_bias = jnp.where(s_idx <= t_idx, 0.0, NEG).astype(F32)
    from_r = jnp.where(s_idx >= t_idx, 1.0, 0.0)
    upto_r = jnp.where(s_idx <= t_idx, 1.0, 0.0)
    zero_q = jnp.zeros((Q, Q), F32)

    def twice(m):
        return low(
            jnp.concatenate(
                [jnp.concatenate([m, zero_q], axis=1), jnp.concatenate([zero_q, m], axis=1)], axis=0
            )
        )

    from_pair, upto_pair = twice(from_r), twice(upto_r)
    pair_s, pair_r = iota((Q, 2 * Q), 0), iota((Q, 2 * Q), 1) % Q
    before_pair = pair_s < pair_r
    after_pair = pair_s > pair_r
    sum_from = jnp.where(t_idx >= s_idx, 1.0, 0.0).astype(BF16)
    sum_before = jnp.where(t_idx < s_idx, 1.0, 0.0).astype(BF16)
    sum_upto = jnp.where(t_idx <= s_idx, 1.0, 0.0).astype(BF16)
    sum_after = jnp.where(t_idx > s_idx, 1.0, 0.0).astype(BF16)
    sum_all = jnp.concatenate([sum_from, sum_before, sum_upto, sum_after], axis=1)

    def chunk_body(c, two_way):
        b_mat = act_ref[rows_of(c), 0:N]
        c_mat = act_ref[rows_of(c), N : 2 * N]
        products = dot(b_mat, c_mat, NT)
        part = cols_ref[rows_of(c), :]
        within, beyond = growths(part, heads)
        rows = rows_ref[first : first + HG, rows_of(c)]
        erows = rows_ref[heads + first : heads + first + HG, rows_of(c)]
        x = x_scr[rows_of(c), :]
        dy_low = dy_scr[rows_of(c), :]
        dy = dy_low.astype(F32)
        step_wide = split_dot(part, by_step)
        xd = x * step_wide
        xd_low = low(xd)
        if two_way:
            anti_bias = jnp.where((s_idx > t_idx) & (s_idx + c * Q < prefix), 0.0, NEG).astype(F32)
        dprod = jnp.zeros((Q, Q), F32)
        parts, inner = [], []
        for pair in range(HG // 2):
            lanes = slice(pair * 128, pair * 128 + 128)
            dy_pair = dy_low[:, lanes]
            zero = jnp.zeros_like(dy_pair)
            blocks = jnp.concatenate(
                [jnp.where(lane_low, dy_pair, zero), jnp.where(lane_low, zero, dy_pair)], axis=0
            )
            dmix = dot(xd_low[:, lanes], blocks, NT)
            mixes, moved = [], []
            for k in (0, 1):
                h = 2 * pair + k
                e = rows[h : h + 1] - part[:, first + h : first + h + 1] + causal_bias
                if two_way:
                    at = heads + first + h
                    back = part[:, at : at + 1] - erows[h : h + 1] + anti_bias
                    e = jnp.maximum(e, back)
                decay = jnp.exp(e)
                slab = dmix[:, k * Q : k * Q + Q] * decay
                dprod = dprod + slab
                mixes.append(low(decay * products))
                moved.append(low(slab * products))
            parts.append(dot(jnp.concatenate(mixes, axis=1), blocks))
            both = jnp.concatenate(moved, axis=1)
            crossing = jnp.where(before_pair, dot(both, from_pair), 0.0)
            if two_way:
                crossing = jnp.where(after_pair, dot(both, upto_pair), crossing)
            inner.append(jnp.sum(crossing, axis=0, keepdims=True))
        for pair in range(HG // 2):
            for k in (0, 1):
                h = 2 * pair + k
                grows_ref[0, h : h + 1, rows_of(c)] = inner[pair][:, k * Q : k * Q + Q]

        entering = split_dot(within, by_cum)
        to_last = split_dot(beyond, by_cum)
        grow = entering[Q - 1 : Q]
        dstate_low = low(dstate_ref[...])
        state_in = states_scr[c]
        du_carry = dot(b_mat, dstate_low) * to_last
        du = jnp.concatenate(parts, axis=1) + du_carry
        y_in = dot(c_mat, state_in) * entering
        dy_in = low(dy * entering)
        x_out = low(xd * to_last)
        d_c = dot(low(dprod), b_mat, TN) + dot(dy_in, state_in, NT)
        d_b = dot(low(dprod), c_mat) + dot(x_out, dstate_low, NT)
        moved_by = [low(dy * y_in), low(xd * du_carry)]
        across = jnp.sum(dstate_ref[...] * state_in.astype(F32), axis=0, keepdims=True) * grow
        if two_way:
            back_state = state_ref[...]
            back_low = low(back_state)
            dback_low = dback_scr[c]
            leaving = split_dot(beyond, by_ecum)
            from_first = split_dot(within * prefix_column(prefix, c), by_ecum)
            du_back = dot(b_mat, dback_low) * from_first
            du = du + du_back
            y_back = dot(c_mat, back_low) * leaving
            x_back = low(xd * from_first)
            d_c = d_c + dot(low(dy * leaving), back_low, NT)
            d_b = d_b + dot(x_back, dback_low, NT)
            moved_by = moved_by + [low(dy * y_back), low(xd * du_back)]
            across = across + grow * jnp.sum(
                dback_low.astype(F32) * back_state, axis=0, keepdims=True
            )
            state_ref[...] = back_state * grow + dot(b_mat, x_back, TN)
        dstate_ref[...] = dstate_ref[...] * grow + dot(c_mat, dy_in, TN)
        d_bc = jnp.concatenate([d_b, d_c], axis=1)
        summed = dot(sum_all if two_way else sum_all[:, : 2 * Q], jnp.concatenate(moved_by, axis=0))
        qk = dot(low(summed), collect)
        direct = dot(low(x * du), collect)
        across8 = low_pair_dot(jnp.broadcast_to(across, (8, width)), collect)
        d_cols = jnp.concatenate([direct, qk + across8[0:1]], axis=1)
        if more:
            d_bc = d_bc + refs[0][rows_of(c), :]
            d_cols = d_cols + refs[1][rows_of(c), :]
        gact_ref[rows_of(c), :] = d_bc
        gcols_ref[rows_of(c), :] = d_cols

        dconv = (du * step_wide + skip * dy) * slope_scr[rows_of(c), :]
        shifted = shifted_rows(x_ref, c)
        both = jnp.concatenate([dconv, next_scr[...]], axis=0)
        gx = taps[3:4] * dconv
        gsum_ref[3:4, :] += jnp.sum(dconv * shifted[0], axis=0, keepdims=True)
        for j in (1, 2, 3):
            gx = gx + taps[3 - j : 4 - j] * pltpu.roll(both, Q + 8 - j, 0)[:Q]
            gsum_ref[3 - j : 4 - j, :] += jnp.sum(dconv * shifted[j], axis=0, keepdims=True)
        gx_ref[rows_of(c), :] = low(gx)
        next_scr[...] = dconv[0:8]
        return 0

    if chunks > anti:
        lax.fori_loop(0, chunks - anti, lambda i, _: chunk_body(chunks - 1 - i, False), 0, unroll=4)
    lax.fori_loop(0, anti, lambda i, _: chunk_body(anti - 1 - i, True), 0, unroll=4)
    by_head = low_pair_dot(jnp.broadcast_to(gsum_ref[4:5, :], (8, width)), collect)
    gsum_ref[5:6, 0:128] = by_head[0:1]


def scan_backward(prefix, x_pre, grad_ssd, taps, skip, cols, rows, act, states, group, column, place, places, gx, before):
    length, heads = x_pre.shape[0], taps.shape[1] // P_SIZE
    chunks = length // Q
    anti = min(MAX_PREFIX // Q, chunks)
    wide = pl.BlockSpec((length, CG), lambda i: (0, column))
    given = [prefix, x_pre, grad_ssd, taps, skip, cols, rows, act, states]
    in_specs = [
        pl.BlockSpec(memory_space=pltpu.SMEM),
        wide,
        wide,
        pl.BlockSpec((4, CG), lambda i: (0, group)),
        pl.BlockSpec((1, CG), lambda i: (0, group)),
        pl.BlockSpec((length, 128), lambda i: (0, 0)),
        pl.BlockSpec((128, length), lambda i: (0, 0)),
        pl.BlockSpec((length, 2 * N), lambda i: (0, 0)),
        pl.BlockSpec((chunks, N, CG), lambda i: (0, 0, 0)),
    ]
    aliases = {}
    if before is not None:
        given += list(before)
        in_specs += [
            pl.BlockSpec((length, 2 * N), lambda i: (0, 0)),
            pl.BlockSpec((length, 256), lambda i: (0, 0)),
        ]
        aliases = {len(given) - 2: 1, len(given) - 1: 2}
    if gx is not None:
        aliases[len(given)] = 0
        given.append(gx)
        in_specs.append(pl.BlockSpec(memory_space=pl.ANY))
    return pl.pallas_call(
        functools.partial(backward_kernel, heads, group * HG, before is not None),
        grid=(1,),
        in_specs=in_specs,
        out_specs=[
            pl.BlockSpec((length, CG), lambda i: (0, place)),
            pl.BlockSpec((length, 2 * N), lambda i: (0, 0)),
            pl.BlockSpec((length, 256), lambda i: (0, 0)),
            pl.BlockSpec((1, HG, length), lambda i: (0, 0, 0)),
            pl.BlockSpec((8, CG), lambda i: (0, 0)),
        ],
        out_shape=(
            jax.ShapeDtypeStruct((length, places * CG), BF16),
            jax.ShapeDtypeStruct((length, 2 * N), F32),
            jax.ShapeDtypeStruct((length, 256), F32),
            jax.ShapeDtypeStruct((1, HG, length), F32),
            jax.ShapeDtypeStruct((8, CG), F32),
        ),
        input_output_aliases=aliases,
        scratch_shapes=[
            pltpu.VMEM((length, CG), F32),
            pltpu.VMEM((length, CG), F32),
            pltpu.VMEM((anti + 1, N, CG), BF16),
            pltpu.VMEM((N, CG), F32),
            pltpu.VMEM((N, CG), F32),
            pltpu.VMEM((8, CG), F32),
        ],
        compiler_params=pltpu.CompilerParams(vmem_limit_bytes=40 * MIB),
        cost_estimate=NO_COST,
        name="scan_backward",
    )(*given)


TILE = 256


def block_of(lanes_ref, j):
    return pl.ds(pl.multiple_of(lanes_ref[j] * 128, 128), 128)


def place_kernel(normalize, count, tiles, lanes_ref, slots_ref, *refs):
    sources, by_ref, out_ref = refs[:count], refs[count], refs[count + 1]
    width = out_ref.shape[1]
    for k in range(count):

        @pl.when(pl.program_id(0) // tiles == k)
        def _(ref=sources[k]):
            if normalize:
                wide = ref[...].astype(F32)
                inv = lax.rsqrt(jnp.sum(wide * wide, axis=-1, keepdims=True) / width + EPSILON)
            else:
                inv = by_ref[...]
            for j in range(width // 128):
                there = block_of(lanes_ref, j)
                v = ref[:, there].astype(F32) * inv
                if normalize:
                    v = v * by_ref[:, there]
                out_ref[:, j * 128 : j * 128 + 128] = low(v)


def place_tokens(lanes, slots, sources, by, normalize):
    tokens, width = sources[0].shape
    size = min(TILE, tokens)
    count, tiles = len(sources), tokens // size

    def source(k):
        return pl.BlockSpec((size, width), lambda i, a, s: (jnp.clip(i - k * tiles, 0, tiles - 1), 0))

    def placed(i, a, s):
        return (s[i // tiles] * tiles + i % tiles, 0)

    by_spec = pl.BlockSpec((1, width), lambda i, a, s: (0, 0)) if normalize else pl.BlockSpec((size, 1), placed)
    return pl.pallas_call(
        functools.partial(place_kernel, normalize, count, tiles),
        grid_spec=pltpu.PrefetchScalarGridSpec(
            num_scalar_prefetch=2,
            grid=(count * tiles,),
            in_specs=[source(k) for k in range(count)] + [by_spec],
            out_specs=pl.BlockSpec((size, width), placed),
        ),
        out_shape=jax.ShapeDtypeStruct((tokens * count, width), BF16),
        compiler_params=pltpu.CompilerParams(vmem_limit_bytes=32 * MIB),
        cost_estimate=NO_COST,
        name="place_tokens",
    )(lanes, slots, *sources, by)


def half_sum(refs, j, per_half):
    here = slice((j % per_half) * 128, (j % per_half) * 128 + 128)
    side = refs[: len(refs) // 2] if j < per_half else refs[len(refs) // 2 :]
    total = side[0][:, here].astype(F32)
    for ref in side[1:]:
        total = total + ref[:, here].astype(F32)
    return total


def mixed_kernel(lanes_ref, slots_ref, hidden_ref, *refs):
    out_ref = refs[-1]
    blocks = hidden_ref.shape[1] // 128
    for j in range(blocks):
        there = block_of(lanes_ref, j)
        out_ref[:, there] = hidden_ref[:, there].astype(F32) + half_sum(refs[:-1], j, blocks // 2)


def finish_kernel(lanes_ref, slots_ref, hidden_ref, cot_ref, gain_ref, *refs):
    out_ref = refs[-1]
    width = hidden_ref.shape[1]
    blocks = width // 128
    wide = hidden_ref[...].astype(F32)
    inv = lax.rsqrt(jnp.sum(wide * wide, axis=-1, keepdims=True) / width + EPSILON)
    total = jnp.zeros((hidden_ref.shape[0], 128), F32)
    for j in range(blocks):
        there = block_of(lanes_ref, j)
        scaled = half_sum(refs[:-1], j, blocks // 2) * gain_ref[:, there]
        total = total + scaled * hidden_ref[:, there].astype(F32)
        out_ref[:, there] = scaled
    coef = inv * inv * inv * (jnp.sum(total, axis=-1, keepdims=True) / width)
    out_ref[...] = inv * out_ref[...] - wide * coef + cot_ref[...].astype(F32)


def own_rows(kernel, name, lanes, slots, hidden, more, gain, halves):
    tokens, width = hidden.shape
    size = min(TILE, tokens)
    tiles = tokens // size
    tile = pl.BlockSpec((size, width), lambda i, a, s: (i, 0))
    given, specs = [hidden, *more], [tile] * (1 + len(more))
    if gain is not None:
        given.append(gain)
        specs.append(pl.BlockSpec((1, width), lambda i, a, s: (0, 0)))
    for half in halves:
        for array, whole in half:
            given.append(array)
            if whole:
                specs.append(pl.BlockSpec((size, width // 2), lambda i, a, s: (s[0] * tiles + i, 0)))
            else:
                specs.append(pl.BlockSpec((size, width // 2), lambda i, a, s: (i, 0)))
    return pl.pallas_call(
        kernel,
        grid_spec=pltpu.PrefetchScalarGridSpec(
            num_scalar_prefetch=2, grid=(tiles,), in_specs=specs, out_specs=tile
        ),
        out_shape=jax.ShapeDtypeStruct((tokens, width), F32),
        compiler_params=pltpu.CompilerParams(vmem_limit_bytes=60 * MIB),
        cost_estimate=NO_COST,
        name=name,
    )(lanes, slots, *given)


def turn_kernel(v_ref, out_ref):
    for j in range(out_ref.shape[0] // 128):
        here = slice(j * 128, j * 128 + 128)
        out_ref[here, :] = v_ref[:, here].astype(F32).T


def turned(v):
    rows, columns = v.shape
    if rows % 128:
        return v.astype(F32).T
    return pl.pallas_call(
        turn_kernel,
        out_shape=jax.ShapeDtypeStruct((columns, rows), F32),
        compiler_params=pltpu.CompilerParams(vmem_limit_bytes=32 * MIB),
        cost_estimate=NO_COST,
        name="turned",
    )(v)


def post_kernel(rest_ref, taps_ref, decay_ref, bias_ref, *refs):
    gbc_ref, gtaps_ref, ghead_ref, next_scr = refs[-4:]
    gact_ref, gcols_ref, grows = refs[0], refs[1], refs[2:-4]
    length, heads = rest_ref.shape[0], decay_ref.shape[1]
    chunks = length // Q
    taps = taps_ref[...]
    gtaps_ref[...] = jnp.zeros_like(gtaps_ref)
    ghead_ref[...] = jnp.zeros_like(ghead_ref)
    next_scr[...] = jnp.zeros_like(next_scr)
    filler = jnp.zeros((1, 128 - heads), F32)
    growth = -jnp.exp(jnp.concatenate([decay_ref[...], filler], axis=1))
    bias = jnp.concatenate([bias_ref[...], filler], axis=1)

    def body(i, _):
        c = chunks - 1 - i
        shifted = shifted_rows(rest_ref, c, 2 * N)
        conv = conv_of(shifted, taps)
        s = sig(conv)
        dconv = gact_ref[rows_of(c), :] * (s + conv * s * (1.0 - s))
        both = jnp.concatenate([dconv, next_scr[...]], axis=0)
        g = taps[3:4] * dconv
        gtaps_ref[3:4, :] += jnp.sum(dconv * shifted[0], axis=0, keepdims=True)
        for j in (1, 2, 3):
            g = g + taps[3 - j : 4 - j] * pltpu.roll(both, Q + 8 - j, 0)[:Q]
            gtaps_ref[3 - j : 4 - j, :] += jnp.sum(dconv * shifted[j], axis=0, keepdims=True)
        gbc_ref[rows_of(c), 0 : 2 * N] = low(g)
        next_scr[...] = dconv[0:8]

        direct, moved = gcols_ref[rows_of(c), 0:128], gcols_ref[rows_of(c), 128:256]
        inner = [ref[0, :, rows_of(c)] for ref in grows]
        inner.append(jnp.zeros((128 - heads, Q), F32))
        moved = moved + jnp.concatenate(inner, axis=0).T
        raw = rest_ref[rows_of(c), 2 * N :] + bias
        step = jnp.maximum(raw, 0.0) + jnp.log(1.0 + jnp.exp(-jnp.abs(raw)))
        gdt = (direct + moved * growth) * sig(raw)
        gbc_ref[rows_of(c), 2 * N :] = low(gdt[:, 0:heads])
        ghead_ref[0:1, :] += jnp.sum(moved * growth * step, axis=0, keepdims=True)
        ghead_ref[1:2, :] += jnp.sum(gdt, axis=0, keepdims=True)
        return 0

    lax.fori_loop(0, chunks, body, 0, unroll=4)


def post(rest_pre, bc_taps, log_decay, dt_bias, grad_act, gcols, grows):
    length, heads = rest_pre.shape[0], log_decay.shape[0]
    return pl.pallas_call(
        post_kernel,
        out_shape=(
            jax.ShapeDtypeStruct((length, 2 * N + heads), BF16),
            jax.ShapeDtypeStruct((8, 2 * N), F32),
            jax.ShapeDtypeStruct((8, 128), F32),
        ),
        scratch_shapes=[pltpu.VMEM((8, 2 * N), F32)],
        compiler_params=pltpu.CompilerParams(vmem_limit_bytes=40 * MIB),
        cost_estimate=NO_COST,
        name="post",
    )(rest_pre, bc_taps, log_decay[None], dt_bias[None], grad_act, gcols, *grows)


def gate_kernel(a_ref, other_ref, part_ref, ssd_ref, gain_ref, gate_ref, out_ref, square_ref):
    gain = gain_ref[...]

    @pl.when(pl.program_id(0) == 0)
    def _():
        square_ref[...] = jnp.zeros_like(square_ref)

    for m in range(0, a_ref.shape[0], 256):
        here = slice(m, m + 256)
        z = part_ref[here, :] + dot(a_ref[here, :], other_ref[...])
        gated = ssd_ref[here, :].astype(F32) * (z * sig(z))
        gate_ref[here, :] = low(z)
        out_ref[here, :] = low(gated * gain)
        square = gated * gated
        square_ref[here, :] += sum(square[:, k : k + 128] for k in range(0, CG, 128))


def gate_product(normed, other, part, ssd_out, gain):
    tokens, width = normed.shape
    channels = ssd_out.shape[1]
    tall = pl.BlockSpec((tokens, CG), lambda j: (0, j))
    deep = pl.BlockSpec((width // 2, CG), lambda j: (0, j))
    return pl.pallas_call(
        gate_kernel,
        grid=(channels // CG,),
        in_specs=[
            pl.BlockSpec((tokens, width // 2), lambda j: (0, 1)), deep, tall, tall, pl.BlockSpec((1, CG), lambda j: (0, j)),
        ],
        out_specs=[tall, tall, pl.BlockSpec((tokens, 128), lambda j: (0, 0))],
        out_shape=(
            jax.ShapeDtypeStruct((tokens, channels), BF16),
            jax.ShapeDtypeStruct((tokens, channels), BF16),
            jax.ShapeDtypeStruct((tokens, 128), F32),
        ),
        compiler_params=pltpu.CompilerParams(vmem_limit_bytes=40 * MIB),
        cost_estimate=NO_COST,
        name="gate_product",
    )(normed, other, part, ssd_out, gain)


def gating_kernel(a_ref, own_ref, other_ref, gate_ref, ssd_ref, coef_ref, gain_ref, ggate_ref, dy_ref):
    depth = own_ref.shape[0]
    gain = gain_ref[...]
    for m in range(0, a_ref.shape[0], 256):
        here = slice(m, m + 256)
        scaled = dot(a_ref[here, :depth], own_ref[...]) + dot(a_ref[here, depth:], other_ref[...])
        z = gate_ref[here, :].astype(F32)
        y = ssd_ref[here, :].astype(F32)
        s = sig(z)
        act = z * s
        grad = gain * scaled - y * act * coef_ref[here, :]
        ggate_ref[here, :] = low(grad * y * (s + act * (1.0 - s)))
        dy_ref[here, :] = low(grad * act)


def gating_product(cot, own, other, gate, ssd_out, coef, gain):
    tokens, width = cot.shape
    channels = ssd_out.shape[1]
    tall = pl.BlockSpec((tokens, CG), lambda j: (0, j))
    deep = pl.BlockSpec((width // 2, CG), lambda j: (0, j))
    return pl.pallas_call(
        gating_kernel,
        grid=(channels // CG,),
        in_specs=[
            pl.BlockSpec((tokens, width), lambda j: (0, 0)), deep, deep, tall, tall,
            pl.BlockSpec((tokens, 1), lambda j: (0, 0)), pl.BlockSpec((1, CG), lambda j: (0, j)),
        ],
        out_specs=[tall, tall],
        out_shape=(
            jax.ShapeDtypeStruct((tokens, channels), BF16),
            jax.ShapeDtypeStruct((tokens, channels), BF16),
        ),
        compiler_params=pltpu.CompilerParams(vmem_limit_bytes=40 * MIB),
        cost_estimate=NO_COST,
        name="gating_product",
    )(cot, own, other, gate, ssd_out, coef, gain)


def snake(devices):
    half = devices // 4
    return [z * 2 for z in range(half)] + [z * 2 + 1 for z in reversed(range(half))]


def chip_groups(devices):
    return [[chip * 2 + core for chip in snake(devices)] for core in (0, 1)]


def other_core(v, devices):
    return lax.ppermute(v, "fsdp", [(i, i ^ 1) for i in range(devices)])


def other_half(v):
    return lax.ppermute(v, "tp", [(0, 1), (1, 0)])


def tie(first, second):
    return lax.optimization_barrier((first, second))


def gather(v, devices):
    return lax.all_gather(v, "fsdp", axis=0, tiled=True, axis_index_groups=chip_groups(devices))


def doubling_gather(v, devices):
    me = lax.axis_index("fsdp")
    bit = 1
    while bit < devices:
        came = lax.ppermute(v, "fsdp", [(i, i ^ bit) for i in range(devices)])
        mine_first = me & bit == 0
        v = jnp.concatenate([jnp.where(mine_first, v, came), jnp.where(mine_first, came, v)], axis=0)
        bit *= 2
    return v


def scatter(v, devices):
    return lax.psum_scatter(
        v, "fsdp", scatter_dimension=0, tiled=True, axis_index_groups=chip_groups(devices)
    )


def on_device(
    hidden,
    cotangent,
    prefix,
    input_norm_gain,
    z_weight,
    x_weight,
    bc_weight,
    dt_weight,
    x_conv,
    bc_conv,
    log_decay,
    dt_bias,
    skip_gain,
    gate_gain,
    out_weight,
):
    fsdp = lax.axis_size("fsdp")
    tp = lax.axis_size("tp")
    own_tokens, width = hidden.shape
    heads = log_decay.shape[0]
    channels = heads * P_SIZE
    all_channels = channels * tp
    groups = channels // CG
    taps_own = x_conv.shape[2]
    rows = width // fsdp
    ring = fsdp // 2
    half_width = width // 2

    order = snake(fsdp)
    core = lax.axis_index("fsdp") % 2
    line = jnp.array(order, jnp.int32)
    blocks = jnp.concatenate([line * 2 + core, line * 2 + 1 - core])
    direct = rows % 128 == 0
    per = max(rows // 128, 1)
    if direct:
        lanes = (blocks[:, None] * per + jnp.arange(per)[None]).reshape(-1)
    else:
        lanes = jnp.arange(width // 128)
    lanes = lanes.astype(jnp.int32)

    def to_cores(v):
        zero = jnp.stack([v[2 * chip] for chip in order])
        one = jnp.stack([v[2 * chip + 1] for chip in order])
        return jnp.where(core == 0, zero, one), jnp.where(core == 0, one, zero)

    def to_ring(v):
        return v if direct else v.reshape(-1, fsdp, rows)[:, blocks].reshape(v.shape)

    def from_ring(v):
        if direct:
            return v
        return v.reshape(-1, fsdp, rows)[:, jnp.argsort(blocks)].reshape(v.shape)

    small = jnp.concatenate(
        [input_norm_gain.reshape(-1), x_conv.reshape(-1), bc_conv.reshape(-1), gate_gain.reshape(-1)]
    )
    sizes = [input_norm_gain.size, x_conv.size, bc_conv.size, gate_gain.size]
    cuts = [0]
    for size in sizes:
        cuts.append(cuts[-1] + size)
    small_all = doubling_gather(jnp.pad(small, (0, -small.size % 128))[None], fsdp)
    payload = jnp.concatenate([x_weight, bc_weight, dt_weight, dt_weight, dt_weight], axis=1)
    payload = jnp.pad(payload, ((0, 0), (0, 128 - 3 * heads)))

    if tp == 2:
        mine = lax.axis_index("tp").astype(jnp.int32)
        slots = jnp.stack([mine, 1 - mine])
        hidden_other = other_half(hidden)
        cot_given, hidden_other = tie(cotangent, hidden_other)
        hidden_parts = [hidden, hidden_other]
        cot_parts = [cotangent, other_half(cot_given)]
    else:
        slots = jnp.zeros((2,), jnp.int32)
        hidden_parts = [lax.all_gather(hidden, "tp", axis=0, tiled=True)]
        cot_parts = [lax.all_gather(cotangent, "tp", axis=0, tiled=True)]
    hidden_parts = [to_ring(v) for v in hidden_parts]
    cot_parts = [to_ring(v) for v in cot_parts]

    norm_gain = small_all[:, cuts[0] : cuts[1]].reshape(1, -1).astype(F32)
    x_taps = small_all[:, cuts[1] : cuts[2]].reshape(fsdp, heads, 4, taps_own)
    x_taps = jnp.transpose(x_taps, (2, 1, 0, 3)).reshape(4, channels).astype(F32)
    bc_taps = small_all[:, cuts[2] : cuts[3]].reshape(fsdp, 4, -1)
    bc_taps = jnp.transpose(bc_taps, (1, 0, 2)).reshape(4, 2 * N).astype(F32)
    gain = small_all[:, cuts[3] : cuts[4]].reshape(fsdp, heads, -1)
    gain = jnp.transpose(gain, (1, 0, 2)).reshape(1, channels).astype(F32)
    skip = jnp.repeat(skip_gain, P_SIZE)[None]
    hidden_parts[-1], (norm_gain, x_taps, bc_taps, gain, skip) = tie(
        hidden_parts[-1], (norm_gain, x_taps, bc_taps, gain, skip)
    )

    def over_tp(v):
        return v + other_half(v) if tp == 2 else lax.psum(v, "tp")

    x_own = gather(payload, fsdp)
    z_own = gather(z_weight, fsdp)
    out_own = gather(out_weight.T, fsdp)
    x_own, hidden_parts[-1] = tie(x_own, hidden_parts[-1])
    x_other = other_core(x_own, fsdp)

    norm_gain = to_ring(norm_gain)
    normed = place_tokens(lanes, slots, hidden_parts, norm_gain, True)
    na, nb = normed[:, :half_width], normed[:, half_width:]
    few = slice(channels, channels + 2 * N + 128)
    rest_pre = dot(na, x_own[:, few]) + dot(nb, x_other[:, few])
    rest = slice(channels, channels + 2 * N + heads)
    rest_own, rest_other = x_own[:, rest], x_other[:, rest]
    act, cols, head_rows = prep(rest_pre, bc_taps, log_decay, dt_bias)
    x_pre = low(dot(na, x_own[:, :channels]) + dot(nb, x_other[:, :channels]))
    ssd_out, states = None, []
    for g in range(groups):
        ssd_out, kept = scan_forward(prefix, x_pre, x_taps, skip, cols, head_rows, act, g, ssd_out)
        states.append(kept)
    (z_own, cot_parts[-1]), ssd_out = tie((z_own, cot_parts[-1]), ssd_out)
    z_other = other_core(z_own, fsdp)

    part = lax.optimization_barrier(dot(na, z_own))
    gate_low, scaled_out, square = gate_product(normed, z_other, part, ssd_out, gain)
    square_sum = over_tp(jnp.sum(square, axis=-1))

    inv_gate = lax.rsqrt(square_sum / all_channels + EPSILON)[:, None]
    cot_rel = place_tokens(lanes, slots, cot_parts, inv_gate, False)
    ca, cb = cot_rel[:, :half_width], cot_rel[:, half_width:]
    gout_other = low(dot(cb, scaled_out, TN))
    gout_came = other_core(gout_other, fsdp)
    gout_sum = low(dot(ca, scaled_out, TN) + gout_came.astype(F32))
    (scaled_out, out_own), gout_sum = tie((scaled_out, out_own), gout_sum)
    grad_out = scatter(gout_sum, fsdp)
    out_other = other_core(out_own, fsdp)

    branch, along = [], 0.0
    for cot_half, out_half in ((ca, out_own), (cb, out_other)):
        v = dot(scaled_out, out_half, NT)
        along = along + jnp.sum(v * cot_half.astype(F32), axis=-1)
        branch.append(low(v * inv_gate))
    along = over_tp(along)
    coef = inv_gate * inv_gate * (along / all_channels)[:, None]
    coef, branch = tie(coef, branch)

    def to_own_tokens(v):
        if tp == 2:
            leaving = lax.dynamic_slice_in_dim(v, (1 - mine) * own_tokens, own_tokens, 0)
            return [(v, True), (other_half(leaving), False)]
        return [(lax.psum_scatter(v, "tp", scatter_dimension=0, tiled=True), False)]

    branch_parts = [to_own_tokens(v) for v in branch]
    kinds = [[whole for _, whole in half] for half in branch_parts]
    branch_parts = [[v for v, _ in half] for half in branch_parts]

    ggate, dy = gating_product(cot_rel, out_own, out_other, gate_low, ssd_out, coef, gain)
    gz_came = other_core(low(dot(nb, ggate, TN)), fsdp)
    z_parts = [dot(ggate, z_own, NT), dot(ggate, z_other, NT)]
    normed, z_parts = tie(normed, z_parts)
    na, nb = normed[:, :half_width], normed[:, half_width:]
    gz_sum = low(dot(na, ggate, TN) + gz_came.astype(F32))
    dy, gz_sum = tie(dy, gz_sum)
    grad_z = scatter(gz_sum, fsdp)

    grows, gsums = [], []
    first = groups * 3 // 4
    before = None

    def back_through(start, stop, dy, before):
        gx = None
        dy = dy[:, start * CG : stop * CG] if start else dy
        for g in range(start, stop):
            gx, gact, gcol, grow, gsum = scan_backward(
                prefix, x_pre[:, start * CG : stop * CG] if start else x_pre, dy, x_taps, skip, cols, head_rows, act, states[g],
                g, g - start, g - start, stop - start, gx, before
            )
            before = (gact, gcol)
            grows.append(grow)
            gsums.append(gsum)
        return gx, before

    grad_x = []
    if first:
        gx, before = back_through(0, first, dy, before)
        gx, (branch_parts, grad_out, grad_z) = tie(gx, (branch_parts, grad_out, grad_z))
        came = other_core(low(dot(nb, gx, TN)), fsdp)
        z_parts = [
            v + dot(gx, half[:, : first * CG], NT) for v, half in zip(z_parts, (x_own, x_other))
        ]
        normed, z_parts = tie(normed, z_parts)
        na, nb = normed[:, :half_width], normed[:, half_width:]
        total = low(dot(na, gx, TN) + came.astype(F32))
        dy, total = tie(dy, total)
        grad_x.append(scatter(total, fsdp))
    gx, before = back_through(first, groups, dy, before)
    if not first:
        gx, grad_z = tie(gx, grad_z)
    g_gain = jnp.sum(out_weight.T.astype(F32) * grad_out.astype(F32), axis=0) / gain[0]
    g_gain = jnp.transpose(g_gain.reshape(heads, fsdp, -1), (1, 0, 2))
    late = slice(first * CG, channels)
    grest, gbc_taps, ghead = post(rest_pre, bc_taps, log_decay, dt_bias, before[0], before[1], grows)

    gsum = jnp.concatenate(gsums, axis=1)
    gx_taps = jnp.transpose(gsum[0:4].reshape(4, heads, fsdp, taps_own), (2, 1, 0, 3))
    g_taps = jnp.transpose(gbc_taps[0:4].reshape(4, fsdp, -1), (1, 0, 2))
    g_skip = sum(v[5, :heads] for v in gsums)
    per_head = jnp.concatenate([ghead[0, :heads], ghead[1, :heads], g_skip])
    slices = jnp.concatenate(
        [
            g_taps.reshape(fsdp, -1),
            gx_taps.reshape(fsdp, -1),
            g_gain.reshape(fsdp, -1),
            jnp.broadcast_to(per_head[None], (fsdp, per_head.size)),
        ],
        axis=1,
    )
    size = slices.shape[1]
    lone = -(-size // rows)
    lines_own, lines_other = [
        jnp.pad(v, ((0, 0), (0, lone * rows - size))).reshape(half_width, lone) for v in to_cores(slices)
    ]
    rest_leaves = jnp.concatenate([dot(nb, grest, TN), lines_other], axis=1)
    rest_came = other_core(rest_leaves, fsdp)
    gx, rest_leaves = tie(gx, rest_leaves)
    gx_other = low(dot(nb, gx, TN))
    came = other_core(gx_other, fsdp)
    (grest, gx), gx_other = tie((grest, gx), gx_other)
    rest_sum = jnp.concatenate([dot(na, grest, TN), lines_own], axis=1) + rest_came
    (grest, gx), (rest_sum, grad_x) = tie((grest, gx), (rest_sum, grad_x))
    mine_rest = scatter(rest_sum, fsdp)

    def first_part(v, x_half):
        return v + dot(gx, x_half[:, late], NT)

    part = low(first_part(z_parts[0], x_own) + dot(grest, rest_own, NT))
    part_sums = [to_own_tokens(part)]
    kinds_part = [whole for _, whole in part_sums[0]]
    gx, part = tie(gx, part)
    gx_sum = low(dot(na, gx, TN) + came.astype(F32))
    gx, gx_sum = tie(gx, gx_sum)
    grad_x.append(scatter(gx_sum, fsdp))
    second = first_part(z_parts[1], x_other)
    (branch_parts, grad_out, grad_z), part = tie((branch_parts, grad_out, grad_z), part)
    mixed = from_ring(
        own_rows(
            mixed_kernel, "add_branch", lanes, slots, to_ring(hidden), [], None,
            [list(zip(half, kind)) for half, kind in zip(branch_parts, kinds)],
        )
    )
    grad_z, grad_out = grad_z.astype(F32), turned(grad_out)
    arrived = [v for v, _ in part_sums[0]]
    second, (arrived, mixed, grad_out, grad_z, mine_rest) = tie(
        second, (arrived, mixed, grad_out, grad_z, mine_rest)
    )
    part_sums[0] = list(zip(arrived, kinds_part))
    part_sums.append(to_own_tokens(low(second + dot(grest, rest_other, NT))))

    grad_bc, grad_dt = mine_rest[:, : 2 * N], mine_rest[:, 2 * N : 2 * N + heads]
    lines = mine_rest[:, 2 * N + heads :].reshape(-1)
    n_taps, bc_size = bc_conv.size, rows * 2 * N
    at = [n_taps]
    for size in (x_conv.size, gate_gain.size, heads, heads, heads):
        at.append(at[-1] + size)
    gx_taps = lines[at[0] : at[1]].reshape(x_conv.shape)
    g_gain = lines[at[1] : at[2]].reshape(gate_gain.shape)
    g_decay, g_bias, g_skip = [lines[at[k] : at[k + 1]] for k in (2, 3, 4)]

    def weighted(w, g):
        return jnp.sum(w.astype(F32) * g.astype(F32), axis=1)

    grad_gain = weighted(z_weight, grad_z) + weighted(bc_weight, grad_bc) + weighted(dt_weight, grad_dt)
    last, whole = part_sums[1][-1]
    last, (mixed, grad_gain, grad_out, grad_z) = tie(last, (mixed, grad_gain, grad_out, grad_z))
    part_sums[1][-1] = (last, whole)
    grad_hidden = from_ring(
        own_rows(finish_kernel, "finish", lanes, slots, to_ring(hidden), [to_ring(cotangent)], norm_gain, part_sums)
    )
    grad_x = jnp.concatenate(grad_x, axis=1).astype(F32)
    grad_gain = (grad_gain + weighted(x_weight, grad_x)) / input_norm_gain.astype(F32)
    together = over_tp(jnp.concatenate([grad_bc.reshape(-1), lines[:n_taps], grad_gain]))
    grad_bc = together[:bc_size].reshape(rows, 2 * N)
    g_taps = together[bc_size : bc_size + n_taps].reshape(bc_conv.shape)
    grad_gain = together[bc_size + n_taps :]
    return (
        mixed, grad_hidden, grad_gain, grad_z, grad_x, grad_bc, grad_dt, gx_taps, g_taps, g_decay, g_bias,
        g_skip, g_gain, grad_out,
    )


def solution(mesh):
    both = P(("fsdp", "tp"), None)
    split = P("fsdp", "tp")
    ins = (
        both, both, P("fsdp"), P("fsdp"), split, split, P("fsdp", None), split, P("tp", None, "fsdp"),
        P(None, "fsdp"), P("tp"), P("tp"), P("tp"), P("tp", "fsdp"), P("tp", "fsdp"),
    )
    outs = (
        both, both, P("fsdp"), split, split, P("fsdp", None), split, P("tp", None, "fsdp"),
        P(None, "fsdp"), P("tp"), P("tp"), P("tp"), P("tp", "fsdp"), P("tp", "fsdp"),
    )
    return jax.shard_map(on_device, mesh=mesh, in_specs=ins, out_specs=outs, check_vma=False)
```
